32 devices in a mesh: expert: 8 (over y, x, core), wshard: 4 (over z).
Axes of the slice: x: 2, y: 2, z: 4, core: 2. Of those that a mesh axis runs over, the one named last changes fastest.
Arguments:
- tokens: bfloat16 [32768, 1024], P(('expert', 'wshard')), may hold values from -6 to 6
- gain_attn: bfloat16 [1024], P('wshard'), may hold values from 0.099609375 to 1.8984375
- w_query: bfloat16 [1024, 1024], P('wshard'), may hold values from -0.1875 to 0.1875
- key_weight: bfloat16 [1024, 512], P('wshard'), may hold values from -0.1875 to 0.1875
- value_weight: bfloat16 [1024, 512], P('wshard'), may hold values from -0.1875 to 0.1875
- w_out: bfloat16 [1024, 1024], P('wshard'), may hold values from -1.5 to 1.5
- gain_ffn: bfloat16 [1024], P('wshard'), may hold values from 0.099609375 to 1.8984375
- w_router: bfloat16 [1024, 8], P('wshard'), may hold values from -0.09375 to 0.09375
- w_gate: bfloat16 [8, 1024, 512], P('expert'), may hold values from -0.1875 to 0.1875
- w_up: bfloat16 [8, 1024, 512], P('expert'), may hold values from -0.1875 to 0.1875
- w_down: bfloat16 [8, 512, 1024], P('expert'), may hold values from -0.75 to 0.75
- routes: int32 [32768, 4], P(('expert', 'wshard')), may hold values from 0 to 7, all different within a row; in each aligned block of 512 rows (0 to 511, 512 to 1023, ...) at most 512 rows name the same one
- cotangent: bfloat16 [32768, 1024], P(('expert', 'wshard')), may hold values from -6 to 6
Outputs:
- mixed: bfloat16 [32768, 1024], P(('expert', 'wshard'))
- d_tokens: float32 [32768, 1024], P(('expert', 'wshard'))
- d_gain_attn: float32 [1024], P('wshard')
- d_w_query: float32 [1024, 1024], P('wshard')
- d_w_key: float32 [1024, 512], P('wshard')
- d_w_value: float32 [1024, 512], P('wshard')
- d_w_out: float32 [1024, 1024], P('wshard')
- d_gain_ffn: float32 [1024], P('wshard')
- d_w_router: float32 [1024, 8], P('wshard')
- d_w_gate: float32 [8, 1024, 512], P('expert')
- d_w_up: float32 [8, 1024, 512], P('expert')
- d_w_down: float32 [8, 512, 1024], P('expert')
The draws below stay inside these ranges and needn't reach their ends.
Inputs may be any that keep to these rules, and one draw needn't show every extreme that they name: `routes`: each row names 4 different experts; in each aligned block of 512 rows (one micro-batch of one device) no expert is named more than 512 times, and one is named exactly 512 times in some block.
All inputs are finite; a program needn't handle non-finite values.
Results may differ from the reference program's by a relative error of at most 0.018.
Values may be sent and summed in bfloat16 or wider, within the bound.
A program may use at most 512 MiB of HBM per device.

```python
import math
import jax
import jax.numpy as jnp
import numpy as np
from jax import lax

MODEL_WIDTH = 1024
QUERY_HEADS = 16
KEY_VALUE_HEADS = 8
HEAD_WIDTH = 64
FF = 512
SEQUENCE_LENGTH = 1024
BLOCK = 256
EXPERTS = 8
TOPK = 4
MB_ROWS = 512
CAP = 512
TOKENS = 32768


def level_of(rng, extent, shards, low, largest):
    factor_of, own = 1.0, jax.random.fold_in(rng, 6)
    for axis_at, shards_of in shards:
        heights = jnp.exp(jax.random.uniform(jax.random.fold_in(own, axis_at), (shards_of,), jnp.float32, low / len(shards), largest / len(shards)))
        factor_of = factor_of * jnp.repeat(heights, extent[axis_at] // shards_of).reshape([-1 if axis == axis_at else 1 for axis in range(len(extent))])
    return factor_of


def routed_block(rng, own, number, rows, amount, top, most, skew):
    sequence = jax.random.permutation(rng, amount)
    packed, ordinary = load_shares(amount, rows * top, most, skew, True), load_shares(amount, rows * top, most, skew, False)
    places = jnp.arange(amount)

    def named(sizes, offset_by):
        used = int((sizes > 0).sum())
        fixed = max(1, used // 4)
        shifted = fixed + (places - fixed + offset_by * (used - fixed)) % max(1, amount - fixed)
        return jnp.zeros((amount,), jnp.int32).at[sequence[jnp.where(places < fixed, places, shifted)]].set(jnp.asarray(sizes, jnp.int32))

    sizes = jnp.where(number % 4 == 0, named(packed, number // 4), named(ordinary, number - number // 4 - 1))
    mixed = jax.random.permutation(jax.random.fold_in(own, 3), amount)
    donor, sink = mixed[0:amount // 2 * 2:2], mixed[1:amount // 2 * 2:2]
    room = jnp.minimum(sizes[donor] - 1, most - sizes[sink]) // 2
    room = jnp.where((donor == sequence[0]) | (sink == sequence[0]) | (sizes[sink] == 0), 0, jnp.maximum(room, 0))
    shifted = jax.random.randint(jax.random.fold_in(own, 4), (amount // 2,), 0, 1 << 20) % (room + 1)
    sizes = sizes.at[donor].add(-shifted).at[sink].add(shifted)
    members = jnp.searchsorted(jnp.cumsum(sizes), jnp.arange(rows * top), side="right").astype(jnp.int32)
    table = members.reshape(top, rows).T
    table = table[jax.random.permutation(jax.random.fold_in(own, 1), rows)]
    offset_by = jax.random.randint(jax.random.fold_in(own, 2), (rows, 1), 0, top)
    return jnp.take_along_axis(table, (jnp.arange(top)[None, :] + offset_by) % top, axis=1)


def load_shares(count, total, bound, skew, full):
    weights = [(1 << 20) // math.isqrt(grade ** skew) + 1 for grade in range(1, count + 1)]
    largest = bound if full else min(bound, max(-(-total // count), total * weights[0] // sum(weights)))
    least = 1 if total - largest >= count - 1 else 0
    counts, spare = [largest] + [least] * (count - 1), total - largest - least * (count - 1)
    while spare > 0:
        candidates = [i for i in range(1, count) if counts[i] < largest] or [i for i in range(1, count) if counts[i] < bound]
        mass, left = sum([weights[i] for i in candidates]), spare
        for i in candidates:
            more = min(bound - counts[i], max(1, left * weights[i] // mass), spare)
            counts[i] = counts[i] + more
            spare = spare - more
    return np.array(counts)


def normal_values(rng, extent, scale, reach, split=(), kind=jnp.bfloat16):
    drawn = jax.random.normal(rng, extent, jnp.float32) * scale
    if len(split) > 0:
        drawn = level_of(rng, extent, split, -0.22, 0.18) * drawn
    return jnp.clip(drawn, min=-reach, max=reach).astype(kind)


def setup_inputs(seed: int = 0) -> dict:
    seeds = jax.random.split(jax.random.key(seed), 14)
    tokens = normal_values(seeds[0], (TOKENS, MODEL_WIDTH), 1.0, 6.0, ((0, 32),))
    gain_attn = jnp.clip(1.0 + 0.18 * jax.random.normal(seeds[1], (MODEL_WIDTH,), jnp.float32), 0.099609375, 1.8984375).astype(jnp.bfloat16)
    w_query = normal_values(seeds[2], (MODEL_WIDTH, QUERY_HEADS * HEAD_WIDTH), MODEL_WIDTH ** -0.5, 0.1875, ((0, 4),))
    key_weight = normal_values(seeds[3], (MODEL_WIDTH, KEY_VALUE_HEADS * HEAD_WIDTH), MODEL_WIDTH ** -0.5, 0.1875, ((0, 4),))
    value_weight = normal_values(seeds[4], (MODEL_WIDTH, KEY_VALUE_HEADS * HEAD_WIDTH), MODEL_WIDTH ** -0.5, 0.1875, ((0, 4),))
    w_out = normal_values(seeds[5], (QUERY_HEADS * HEAD_WIDTH, MODEL_WIDTH), (QUERY_HEADS * HEAD_WIDTH // 64) ** -0.5, 1.5, ((0, 4),))
    gain_ffn = jnp.clip(1.0 + 0.18 * jax.random.normal(seeds[6], (MODEL_WIDTH,), jnp.float32), 0.099609375, 1.8984375).astype(jnp.bfloat16)
    w_router = normal_values(seeds[7], (MODEL_WIDTH, EXPERTS), (4 * MODEL_WIDTH) ** -0.5, 0.09375, ((0, 4),))
    w_gate = normal_values(seeds[8], (EXPERTS, MODEL_WIDTH, FF), MODEL_WIDTH ** -0.5, 0.1875, ((0, 8),))
    w_up = normal_values(seeds[9], (EXPERTS, MODEL_WIDTH, FF), MODEL_WIDTH ** -0.5, 0.1875, ((0, 8),))
    w_down = normal_values(seeds[10], (EXPERTS, FF, MODEL_WIDTH), (FF // 8) ** -0.5, 0.75, ((0, 8),))
    routes_keys = jax.random.split(jax.random.fold_in(seeds[11], 1), TOKENS // MB_ROWS)
    routes_turns = jax.random.permutation(jax.random.fold_in(seeds[11], 3), TOKENS // MB_ROWS)
    routes = jax.vmap(lambda own, number: routed_block(jax.random.fold_in(seeds[11], 2), own, number, MB_ROWS, EXPERTS, TOPK, CAP, 2))(routes_keys, routes_turns).reshape((TOKENS, TOPK))
    cotangent = normal_values(seeds[12], (TOKENS, MODEL_WIDTH), 1.0, 6.0, ((0, 32),))
    return {"tokens": tokens, "gain_attn": gain_attn, "w_query": w_query, "key_weight": key_weight, "value_weight": value_weight, "w_out": w_out, "gain_ffn": gain_ffn, "w_router": w_router, "w_gate": w_gate, "w_up": w_up, "w_down": w_down, "routes": routes, "cotangent": cotangent}


@jax.custom_vjp
def reduced_precision(v):
    return lax.optimization_barrier(v.astype(jnp.bfloat16)).astype(jnp.float32)

@jax.custom_vjp
def reduced_precision_backward(v):
    return v

def low_keep(v):
    return (reduced_precision(v), None)

def low_pass(kept, grad):
    return (grad,)

def back_keep(v):
    return (v, None)

def back_low(kept, grad):
    return (reduced_precision(grad),)
reduced_precision.defvjp(low_keep, low_pass)
reduced_precision_backward.defvjp(back_keep, back_low)

def matrix_product(left, right):
    return jnp.dot(left, right, precision=lax.Precision.HIGHEST, preferred_element_type=jnp.float32)

def rms_scale(values, gain):
    return values * lax.rsqrt(lax.optimization_barrier(jnp.mean(values * values, axis=-1, keepdims=True)) + 1e-06) * gain

def rotary_embed(values, token_positions):
    half_size = HEAD_WIDTH // 2
    frequency = jnp.exp(-jnp.log(10000.0) * jnp.arange(half_size).astype(jnp.float32) * 2.0 / HEAD_WIDTH)
    angles = token_positions.astype(jnp.float32)[:, None] * frequency[None, :]
    cosine = jnp.cos(angles)[:, None, :].astype(values.dtype)
    sines = jnp.sin(angles)[:, None, :].astype(values.dtype)
    leading = values[..., :half_size]
    trailing = values[..., half_size:]
    return jnp.concatenate([leading * cosine - trailing * sines, trailing * cosine + leading * sines], axis=-1)

def attention_block(query_rows, keys_seq, vals_seq):
    head_groups = QUERY_HEADS // KEY_VALUE_HEADS
    grouped_heads = query_rows.reshape(SEQUENCE_LENGTH, KEY_VALUE_HEADS, head_groups, HEAD_WIDTH)
    scores = jnp.einsum('sagd,tad->agst', grouped_heads, keys_seq, precision=lax.Precision.HIGHEST) * HEAD_WIDTH ** (-0.5)
    scores = reduced_precision_backward(scores)
    blocks = jnp.arange(SEQUENCE_LENGTH) // BLOCK
    allowed = blocks[None, :] <= blocks[:, None]
    scores = jnp.where(allowed, scores, -1e+30)
    probs = jax.nn.softmax(scores, axis=-1)
    result = jnp.einsum('agst,tad->sagd', reduced_precision(probs), vals_seq, precision=lax.Precision.HIGHEST)
    return result.reshape(SEQUENCE_LENGTH, QUERY_HEADS * HEAD_WIDTH)

def forward(route_part, inputs, gain_one, query_w, key_matrix, value_matrix, out_w, gain_two, router_w, gate_w, up_w, down_w):
    total_row_count = inputs.shape[0]
    token_positions = jnp.arange(total_row_count) % SEQUENCE_LENGTH
    normalized_input = reduced_precision(rms_scale(inputs, gain_one))
    qpre = reduced_precision_backward(matrix_product(normalized_input, query_w)).reshape(total_row_count, QUERY_HEADS, HEAD_WIDTH)
    prerotation_keys = reduced_precision_backward(matrix_product(normalized_input, key_matrix)).reshape(total_row_count, KEY_VALUE_HEADS, HEAD_WIDTH)
    value_rows = reduced_precision(reduced_precision_backward(matrix_product(normalized_input, value_matrix))).reshape(total_row_count, KEY_VALUE_HEADS, HEAD_WIDTH)
    query_rows = reduced_precision(rotary_embed(qpre, token_positions))
    complete_keys = reduced_precision(rotary_embed(prerotation_keys, token_positions))
    sequence_count = total_row_count // SEQUENCE_LENGTH
    verified_result = jax.checkpoint(attention_block)
    attended_rows = lax.map(lambda single_entry: verified_result(single_entry[0], single_entry[1], single_entry[2]), (query_rows.reshape(sequence_count, SEQUENCE_LENGTH, QUERY_HEADS, HEAD_WIDTH), complete_keys.reshape(sequence_count, SEQUENCE_LENGTH, KEY_VALUE_HEADS, HEAD_WIDTH), value_rows.reshape(sequence_count, SEQUENCE_LENGTH, KEY_VALUE_HEADS, HEAD_WIDTH)))
    attended_rows = reduced_precision(reduced_precision_backward(attended_rows.reshape(total_row_count, QUERY_HEADS * HEAD_WIDTH)))
    resid = inputs + reduced_precision_backward(matrix_product(attended_rows, out_w))
    moe_in = reduced_precision(rms_scale(resid, gain_two))
    logits = reduced_precision_backward(matrix_product(moe_in, router_w))
    picked = (route_part[:, :, None] == jnp.arange(EXPERTS)[None, None, :]).astype(inputs.dtype)
    top = jnp.einsum('tke,te->tk', picked, logits, precision=lax.Precision.HIGHEST)
    gates = jax.nn.softmax(top, axis=-1)
    shares = jnp.einsum('tk,tke->te', gates, picked, precision=lax.Precision.HIGHEST)

    def expert_step(running, single_entry):
        gate_one, up_one, down_one, column = single_entry
        expert_in = reduced_precision_backward(moe_in)
        gate = reduced_precision_backward(matrix_product(expert_in, gate_one))
        upval = reduced_precision_backward(matrix_product(expert_in, up_one))
        hidden = reduced_precision(reduced_precision_backward(jax.nn.silu(gate) * upval))
        produced = reduced_precision(reduced_precision_backward(matrix_product(hidden, down_one)))
        return (running + column[:, None] * produced, None)
    combined, unused = lax.scan(jax.checkpoint(expert_step), jnp.zeros_like(inputs), (gate_w, up_w, down_w, shares.T))
    return resid + combined

def reference(tokens, gain_attn, w_query, key_weight, value_weight, w_out, gain_ffn, w_router, w_gate, w_up, w_down, routes, cotangent):
    params = tuple((p.astype(jnp.float32) for p in (gain_attn, w_query, key_weight, value_weight, w_out, gain_ffn, w_router, w_gate, w_up, w_down)))
    seq_total = TOKENS // SEQUENCE_LENGTH
    per_group = math.gcd(seq_total, max(1, 4096 // SEQUENCE_LENGTH))
    group_rows = per_group * SEQUENCE_LENGTH
    group_count = TOKENS // group_rows
    inputs = tokens.astype(jnp.float32).reshape(group_count, group_rows, MODEL_WIDTH)
    grads_in = cotangent.astype(jnp.float32).reshape(group_count, group_rows, MODEL_WIDTH)
    route_groups = routes.reshape(group_count, group_rows, TOPK)

    def one_group(totals, single_entry):
        input_part, route_part, grad_part = single_entry
        output, pullback = jax.vjp(lambda *values: forward(route_part, *values), input_part, *params)
        grads = pullback(grad_part)
        return (tuple((a + b for a, b in zip(totals, grads[1:]))), (output, grads[0]))
    zeros = tuple((jnp.zeros_like(p) for p in params))
    totals, stacked = lax.scan(one_group, zeros, (inputs, route_groups, grads_in))
    outputs, input_grads = stacked
    mixed = outputs.reshape(TOKENS, MODEL_WIDTH).astype(jnp.bfloat16)
    d_tokens = input_grads.reshape(TOKENS, MODEL_WIDTH)
    return (mixed, d_tokens, totals[0], totals[1], totals[2], totals[3], totals[4], totals[5], totals[6], totals[7], totals[8], totals[9])
```

```python
import functools
import jax
import jax.numpy as jnp
import numpy as np
from jax import lax
from jax.experimental import pallas as pl
from jax.experimental.pallas import tpu as pltpu
from jax.sharding import PartitionSpec as P

QUERY_HEADS = 16
KEY_VALUE_HEADS = 8
HEAD_WIDTH = 64
SEQUENCE_LENGTH = 1024
BLOCK = 256
TILE = 256
LANES = 128
F32 = jnp.float32
BF16 = jnp.bfloat16
ANY = pl.BlockSpec(memory_space=pl.ANY)
VMEM = pl.BlockSpec(memory_space=pltpu.VMEM)
VMEM_BYTES = 60 * 1024 * 1024


def dot(a, b):
    return jnp.dot(a, b, preferred_element_type=F32)


def dot_nt(a, b):
    return lax.dot_general(a, b, (((1,), (1,)), ((), ())), preferred_element_type=F32)


def dot_tn(a, b):
    return lax.dot_general(a, b, (((0,), (0,)), ((), ())), preferred_element_type=F32)


def params(**kw):
    return pltpu.CompilerParams(vmem_limit_bytes=VMEM_BYTES, **kw)


def cost(flops, nbytes, transcendentals=0):
    return pl.CostEstimate(flops=int(flops), bytes_accessed=int(nbytes), transcendentals=int(transcendentals))


def rope_tables(rows):
    half = HEAD_WIDTH // 2
    freq = np.exp(-np.log(10000.0) * np.arange(half, dtype=np.float32) * 2.0 / HEAD_WIDTH).astype(np.float32)
    pos = (np.arange(rows) % SEQUENCE_LENGTH).astype(np.float32)
    angles = (pos[:, None] * freq[None, :]).astype(np.float32)
    cos, sin = np.cos(angles), np.sin(angles)
    return (
        np.concatenate([cos, cos, cos, cos], 1).astype(np.float32),
        np.concatenate([-sin, sin, -sin, sin], 1).astype(np.float32),
    )


def rope(u, cos, sin):
    half = HEAD_WIDTH // 2
    lane = lax.broadcasted_iota(jnp.int32, u.shape, 1)
    swapped = jnp.where(
        lane % HEAD_WIDTH < half, pltpu.roll(u, LANES - half, 1), pltpu.roll(u, half, 1)
    )
    return u * cos + swapped * sin


def row_block(width):
    return pl.BlockSpec((TILE, width), lambda i: (i, 0))


def whole_block(shape):
    return pl.BlockSpec(shape, lambda i: (0,) * len(shape))


def project_kernel(x_ref, gain_ref, w_ref, cos_ref, sin_ref, n_ref, q_ref, k_ref, v_ref):
    x = x_ref[...].astype(F32)
    inverse = lax.rsqrt(jnp.mean(x * x, axis=-1, keepdims=True) + 1e-06)
    normed = (x * inverse * gain_ref[...].astype(F32)).astype(BF16)
    n_ref[...] = normed
    cos, sin = cos_ref[...], sin_ref[...]
    step = 512
    for at in range(0, w_ref.shape[1], step):
        made = dot(normed, w_ref[:, at : at + step])
        for lo in range(0, step, LANES):
            u = made[:, lo : lo + LANES]
            c = at + lo
            if c < q_ref.shape[1]:
                q_ref[:, c : c + LANES] = (rope(u, cos, sin).astype(BF16) * jnp.asarray(HEAD_WIDTH**-0.5, BF16))
            elif c < q_ref.shape[1] + k_ref.shape[1]:
                c -= q_ref.shape[1]
                k_ref[:, c : c + LANES] = rope(u, cos, sin).astype(BF16)
            else:
                c -= q_ref.shape[1] + k_ref.shape[1]
                v_ref[:, c : c + LANES] = u.astype(BF16)


def project(tokens, gain, weights, cos, sin):
    rows, width = tokens.shape
    qw, kw = QUERY_HEADS * HEAD_WIDTH, KEY_VALUE_HEADS * HEAD_WIDTH
    return pl.pallas_call(
        project_kernel,
        grid=(rows // TILE,),
        in_specs=[row_block(width), whole_block((1, width)), whole_block(weights.shape), row_block(LANES), row_block(LANES)],
        out_specs=[row_block(width), row_block(qw), row_block(kw), row_block(kw)],
        out_shape=[jax.ShapeDtypeStruct((rows, w), BF16) for w in (width, qw, kw, kw)],
        compiler_params=params(),
        cost_estimate=cost(2 * rows * width * (qw + 2 * kw), 12 * rows * width),
        name="project",
    )(tokens, gain, weights, cos, sin)


def attend_kernel(q_ref, k_ref, v_ref, o_ref):
    for c in range(2):
        k = k_ref[:, c * HEAD_WIDTH : (c + 1) * HEAD_WIDTH]
        v = v_ref[:, c * HEAD_WIDTH : (c + 1) * HEAD_WIDTH]
        for h in range(2):
            at = (2 * c + h) * HEAD_WIDTH
            for b in range(SEQUENCE_LENGTH // BLOCK):
                n = (b + 1) * BLOCK
                rows = slice(b * BLOCK, (b + 1) * BLOCK)
                s = dot_nt(q_ref[rows, at : at + HEAD_WIDTH], k[:n])
                p = jnp.exp(s - jnp.max(s, axis=-1, keepdims=True))
                total = jnp.sum(p, axis=-1, keepdims=True)
                o = dot((p * (1.0 / total)).astype(BF16), v[:n])
                o_ref[rows, at : at + HEAD_WIDTH] = o.astype(BF16)


def head_block(width, sequence=SEQUENCE_LENGTH):
    return pl.BlockSpec((sequence, width), lambda s, i: (s, i))


def attend(queries, keys, vals):
    rows = queries.shape[0]
    steps = KEY_VALUE_HEADS // 2
    flops = 2 * QUERY_HEADS * rows * SEQUENCE_LENGTH * HEAD_WIDTH * 2
    return pl.pallas_call(
        attend_kernel,
        grid=(rows // SEQUENCE_LENGTH, steps),
        in_specs=[head_block(4 * HEAD_WIDTH), head_block(2 * HEAD_WIDTH), head_block(2 * HEAD_WIDTH)],
        out_specs=head_block(4 * HEAD_WIDTH),
        out_shape=jax.ShapeDtypeStruct(queries.shape, BF16),
        compiler_params=params(),
        cost_estimate=cost(flops * 8, 6 * rows * 1024, QUERY_HEADS * rows * 640),
        name="attend",
    )(queries, keys, vals)


def attend_back_kernel(q_ref, k_ref, v_ref, g_ref, cos_ref, sin_ref, dq_ref, dk_ref, dv_ref, dk_acc, dv_acc, dq_acc):
    dk_acc[...] = jnp.zeros_like(dk_acc)
    dv_acc[...] = jnp.zeros_like(dv_acc)
    for c in range(2):
        lanes = slice(c * HEAD_WIDTH, (c + 1) * HEAD_WIDTH)
        k, v = k_ref[:, lanes], v_ref[:, lanes]
        for h in range(2):
            at = slice((2 * c + h) * HEAD_WIDTH, (2 * c + h + 1) * HEAD_WIDTH)
            for b in range(SEQUENCE_LENGTH // BLOCK):
                n = (b + 1) * BLOCK
                rows = slice(b * BLOCK, (b + 1) * BLOCK)
                q, g = q_ref[rows, at], g_ref[rows, at]
                s = dot_nt(k[:n], q)
                dp = dot_nt(v[:n], g)
                p = jnp.exp(s - jnp.max(s, axis=0, keepdims=True))
                p = p * (1.0 / jnp.sum(p, axis=0, keepdims=True))
                ds = (p * (dp - jnp.sum(p * dp, axis=0, keepdims=True))).astype(BF16)
                dv_acc[:n, lanes] += dot(p.astype(BF16), g)
                dk_acc[:n, lanes] += dot(ds, q)
                dq_acc[rows, at] = dot_tn(ds, k[:n])
    cos, sin = cos_ref[...], -sin_ref[...]
    scale = HEAD_WIDTH**-0.5
    dq_ref[:, :LANES] = rope(dq_acc[:, :LANES] * scale, cos, sin).astype(BF16)
    dq_ref[:, LANES:] = rope(dq_acc[:, LANES:] * scale, cos, sin).astype(BF16)
    dk_ref[...] = rope(dk_acc[...], cos, sin).astype(BF16)
    dv_ref[...] = dv_acc[...].astype(BF16)


def attend_back(queries, keys, vals, grad, cos, sin):
    rows = queries.shape[0]
    steps = KEY_VALUE_HEADS // 2
    flops = 5 * QUERY_HEADS * rows * SEQUENCE_LENGTH * HEAD_WIDTH * 2
    table = pl.BlockSpec((SEQUENCE_LENGTH, LANES), lambda s, i: (s, 0))
    two, four = head_block(2 * HEAD_WIDTH), head_block(4 * HEAD_WIDTH)
    return pl.pallas_call(
        attend_back_kernel,
        grid=(rows // SEQUENCE_LENGTH, steps),
        in_specs=[four, two, two, four, table, table],
        out_specs=[four, two, two],
        out_shape=[jax.ShapeDtypeStruct(a.shape, BF16) for a in (queries, keys, vals)],
        scratch_shapes=[
            pltpu.VMEM((SEQUENCE_LENGTH, LANES), F32),
            pltpu.VMEM((SEQUENCE_LENGTH, LANES), F32),
            pltpu.VMEM((SEQUENCE_LENGTH, 2 * LANES), F32),
        ],
        compiler_params=params(),
        cost_estimate=cost(flops * 8, 12 * rows * 1024, QUERY_HEADS * rows * 640),
        name="attend_back",
    )(queries, keys, vals, grad, cos, sin)


def middle_kernel(a_ref, w_ref, x_ref, gain_ref, router_ref, routes_ref, r_ref, m_ref, mt_ref, gates_ref):
    resid = x_ref[...].astype(F32) + dot(a_ref[...], w_ref[...])
    r_ref[...] = resid
    inverse = lax.rsqrt(jnp.mean(resid * resid, axis=-1, keepdims=True) + 1e-06)
    moe_in = (resid * inverse * gain_ref[...].astype(F32)).astype(BF16)
    m_ref[...] = moe_in
    mt_ref[...] = moe_in.T
    logits = dot(moe_in, router_ref[...])
    lane = lax.broadcasted_iota(jnp.int32, logits.shape, 1)
    routes = routes_ref[...]
    picked = lane == routes[:, 0:1]
    for k in range(1, routes.shape[1]):
        picked = jnp.logical_or(picked, lane == routes[:, k : k + 1])
    logits = jnp.where(picked, logits, -1e30)
    weights = jnp.where(picked, jnp.exp(logits - jnp.max(logits, axis=-1, keepdims=True)), 0.0)
    gates_ref[...] = weights / jnp.sum(weights, axis=-1, keepdims=True)


def middle(attended, out_w, tokens, gain, router_w, routes):
    rows, width = tokens.shape
    return pl.pallas_call(
        middle_kernel,
        grid=(rows // TILE,),
        in_specs=[
            row_block(width),
            whole_block(out_w.shape),
            row_block(width),
            whole_block((1, width)),
            whole_block(router_w.shape),
            row_block(routes.shape[1]),
        ],
        out_specs=[row_block(width), row_block(width), pl.BlockSpec((width, TILE), lambda i: (0, i)), row_block(LANES)],
        out_shape=[
            jax.ShapeDtypeStruct((rows, width), F32),
            jax.ShapeDtypeStruct((rows, width), BF16),
            jax.ShapeDtypeStruct((width, rows), BF16),
            jax.ShapeDtypeStruct((rows, LANES), F32),
        ],
        compiler_params=params(),
        cost_estimate=cost(2 * rows * width * (width + LANES), 14 * rows * width),
        name="middle",
    )(attended, out_w, tokens, gain, router_w, routes)


def moe_kernel(slots, chunks, first, last, me_ref, *refs):
    refs = list(refs)
    take = lambda count: [refs.pop(0) for _ in range(count)]
    x_hbm, xt_hbm, dy_hbm, dyt_hbm, gates_ref = take(5)
    if not first:
        made_in, dmoe_in, gg_in = take(3)
    weights = [[take(count) for count in per_slot] for per_slot in chunks]
    made_out, dmoe_out, gg_ref = take(3)
    grads = [take(3) for _ in slots]
    x, xt, dy, dyt, made, dmoe, wg, wu, wd, hg, dg, du, stage, sem_in, sem_w, sem_out, sem_acc = take(17)
    rows = x.shape[0]
    tiles = rows // TILE

    def load(source, target, sem):
        copy = pltpu.make_async_copy(source, target, sem)
        copy.start()
        return copy

    def load_weights(index):
        buffer = index % 2
        out = []
        for which, target in enumerate((wg, wu, wd)):
            at, copies = 0, []
            for piece, ref in enumerate(weights[index][which]):
                count = ref.shape[0]
                copies.append(load(ref, target.at[buffer, at : at + count], sem_w.at[buffer, which, piece]))
                at += count
            out.append(copies)
        return out

    pending = {0: load_weights(0)}
    inputs = [load(a, b, sem_in.at[i]) for i, (a, b) in enumerate(((x_hbm, x), (dy_hbm, dy)))]
    if not first:
        acc = [load(made_in, made, sem_acc.at[0]), load(dmoe_in, dmoe, sem_acc.at[1])]
        gg_ref[...] = gg_in[...]
    else:
        acc = []
        made[...] = jnp.zeros_like(made)
        dmoe[...] = jnp.zeros_like(dmoe)
        gg_ref[...] = jnp.zeros_like(gg_ref)
    late = [load(a, b, sem_in.at[i]) for i, (a, b) in enumerate(((xt_hbm, xt), (dyt_hbm, dyt)), 2)]
    for copy in inputs:
        copy.wait()
    stores = []
    lane = lax.broadcasted_iota(jnp.int32, (TILE, LANES), 1)
    for index, slot in enumerate(slots):
        buffer = index % 2
        for copies in pending.pop(index):
            for copy in copies:
                copy.wait()
        if index + 1 < len(slots):
            pending[index + 1] = load_weights(index + 1)
        for copy in acc:
            copy.wait()
        acc = []
        me = me_ref[0] ^ slot
        g_w, u_w, d_w = wg.at[buffer], wu.at[buffer], wd.at[buffer]

        def rows_step(i, carry):
            at = pl.ds(pl.multiple_of(i * TILE, TILE), TILE)
            xi, yi = x[at], dy[at]
            gate, upval, pre = dot(xi, g_w[...]), dot(xi, u_w[...]), dot_nt(yi, d_w[...])
            column = jnp.sum(jnp.where(lane == me, gates_ref[at], 0.0), axis=1, keepdims=True)
            sigma = 1.0 / (1.0 + jnp.exp(-gate))
            silu = gate * sigma
            hidden = silu * upval
            gained = jnp.sum(hidden * pre, axis=1, keepdims=True)
            gg_ref[at] = gg_ref[at] + jnp.where(lane == me, gained, 0.0)
            weighted = (hidden * column).astype(BF16)
            dhidden = pre * column
            dgate = (dhidden * upval * (sigma + silu * (1.0 - sigma))).astype(BF16)
            dup = (dhidden * silu).astype(BF16)
            hg[at], dg[at], du[at] = weighted, dgate, dup
            made[at] += dot(weighted, d_w[...])
            dmoe[at] += dot_nt(dgate, g_w[...]) + dot_nt(dup, u_w[...])
            return carry

        lax.fori_loop(0, tiles, rows_step, 0)
        for copy in late:
            copy.wait()
        late = []
        for copy in stores:
            copy.wait()
        stores = []

        def grads_step(i, carry):
            at = pl.ds(pl.multiple_of(i * TILE, TILE), TILE)
            a = xt[at]
            stage[0, at] = dot(a, dg[...]).astype(BF16)
            stage[1, at] = dot(a, du[...]).astype(BF16)
            stage[2, at] = dot(dyt[at], hg[...]).astype(BF16)
            return carry

        lax.fori_loop(0, x.shape[1] // TILE, grads_step, 0)
        for which in range(3):
            stores.append(load(stage.at[which], grads[index][which], sem_out.at[which]))
    done = [load(made, made_out, sem_acc.at[0]), load(dmoe, dmoe_out, sem_acc.at[1])]
    for copy in stores + done:
        copy.wait()


def moe(slots, me, moe_in, moe_in_t, dy, dy_t, gates, acc, weights):
    rows, width = moe_in.shape
    hidden = weights[0][0][0].shape[1]
    first = acc is None
    flat = [piece for per_slot in weights for pieces in per_slot for piece in pieces]
    chunks = tuple(tuple(len(pieces) for pieces in per_slot) for per_slot in weights)
    accs = [] if first else list(acc)
    grad = jax.ShapeDtypeStruct((width, hidden), BF16)
    outs = pl.pallas_call(
        functools.partial(moe_kernel, tuple(slots), chunks, first, False),
        in_specs=[pl.BlockSpec(memory_space=pltpu.SMEM), ANY, ANY, ANY, ANY, VMEM]
        + ([] if first else [ANY, ANY, VMEM])
        + [ANY] * len(flat),
        out_specs=[ANY, ANY, VMEM] + [ANY] * (3 * len(slots)),
        out_shape=[
            jax.ShapeDtypeStruct((rows, width), F32),
            jax.ShapeDtypeStruct((rows, width), F32),
            jax.ShapeDtypeStruct((rows, LANES), F32),
        ]
        + [grad] * (3 * len(slots)),
        scratch_shapes=[
            pltpu.VMEM((rows, width), BF16),
            pltpu.VMEM((width, rows), BF16),
            pltpu.VMEM((rows, width), BF16),
            pltpu.VMEM((width, rows), BF16),
            pltpu.VMEM((rows, width), F32),
            pltpu.VMEM((rows, width), F32),
            pltpu.VMEM((2, width, hidden), BF16),
            pltpu.VMEM((2, width, hidden), BF16),
            pltpu.VMEM((2, hidden, width), BF16),
            pltpu.VMEM((rows, hidden), BF16),
            pltpu.VMEM((rows, hidden), BF16),
            pltpu.VMEM((rows, hidden), BF16),
            pltpu.VMEM((3, width, hidden), BF16),
            pltpu.SemaphoreType.DMA((4,)),
            pltpu.SemaphoreType.DMA((2, 3, 2)),
            pltpu.SemaphoreType.DMA((3,)),
            pltpu.SemaphoreType.DMA((2,)),
        ],
        compiler_params=params(),
        cost_estimate=cost(18 * rows * width * hidden * len(slots), 20 * rows * width),
        name="experts",
    )(me, moe_in, moe_in_t, dy, dy_t, gates, *accs, *flat)
    return outs[:3], [tuple(outs[3 + 3 * i : 6 + 3 * i]) for i in range(len(slots))]


def turn_kernel(
    resid_ref, made_ref, dmoe_ref, gates_ref, gg_ref, dy_ref, gain_ref, router_ref, mt_ref, w_ref,
    mixed_ref, dresid_ref, dz_ref, da_ref, gain_grad_ref, router_grad_ref,
):
    @pl.when(pl.program_id(0) == 0)
    def _():
        gain_grad_ref[...] = jnp.zeros_like(gain_grad_ref)
        router_grad_ref[...] = jnp.zeros_like(router_grad_ref)

    resid = resid_ref[...]
    mixed_ref[...] = (resid + made_ref[...]).astype(BF16)
    gates, gg = gates_ref[...], gg_ref[...]
    dlogits = (gates * (gg - jnp.sum(gates * gg, axis=1, keepdims=True))).astype(BF16)
    router_grad_ref[...] += dot(mt_ref[...], dlogits)
    dmoe = dmoe_ref[...] + dot_nt(dlogits, router_ref[...])
    inverse = lax.rsqrt(jnp.mean(resid * resid, axis=-1, keepdims=True) + 1e-06)
    gain_grad_ref[...] += jnp.sum(dmoe * resid * inverse, axis=0, keepdims=True)
    scaled = dmoe * gain_ref[...].astype(F32)
    inner = jnp.mean(scaled * resid, axis=-1, keepdims=True)
    dresid = dy_ref[...].astype(F32) + inverse * scaled - resid * (inverse * inverse * inverse * inner)
    dresid_ref[...] = dresid
    dz = dresid.astype(BF16)
    dz_ref[...] = dz
    da_ref[...] = dot_nt(dz, w_ref[...]).astype(BF16)


def turn(resid, made, dmoe, gates, gg, dy, gain, router_w, moe_in_t, out_w):
    rows, width = resid.shape
    return pl.pallas_call(
        turn_kernel,
        grid=(rows // TILE,),
        in_specs=[
            row_block(width), row_block(width), row_block(width), row_block(LANES), row_block(LANES), row_block(width),
            whole_block((1, width)), whole_block(router_w.shape), pl.BlockSpec((width, TILE), lambda i: (0, i)),
            whole_block(out_w.shape),
        ],
        out_specs=[row_block(width)] * 4 + [whole_block((1, width)), whole_block((width, LANES))],
        out_shape=[
            jax.ShapeDtypeStruct((rows, width), BF16),
            jax.ShapeDtypeStruct((rows, width), F32),
            jax.ShapeDtypeStruct((rows, width), BF16),
            jax.ShapeDtypeStruct((rows, width), BF16),
            jax.ShapeDtypeStruct((1, width), F32),
            jax.ShapeDtypeStruct((width, LANES), F32),
        ],
        compiler_params=params(),
        cost_estimate=cost(2 * rows * width * (width + 2 * LANES), 28 * rows * width),
        name="turn",
    )(resid, made, dmoe, gates, gg, dy, gain, router_w, moe_in_t, out_w)


def finish_kernel(dq_ref, dk_ref, dv_ref, w_ref, x_ref, dresid_ref, gain_ref, out_ref, gain_grad_ref):
    @pl.when(pl.program_id(0) == 0)
    def _():
        gain_grad_ref[...] = jnp.zeros_like(gain_grad_ref)

    qw, kw = dq_ref.shape[1], dk_ref.shape[1]
    dn = dot_nt(dq_ref[...], w_ref[:, :qw])
    dn += dot_nt(dk_ref[...], w_ref[:, qw : qw + kw])
    dn += dot_nt(dv_ref[...], w_ref[:, qw + kw :])
    x = x_ref[...].astype(F32)
    inverse = lax.rsqrt(jnp.mean(x * x, axis=-1, keepdims=True) + 1e-06)
    gain_grad_ref[...] += jnp.sum(dn * x * inverse, axis=0, keepdims=True)
    scaled = dn * gain_ref[...].astype(F32)
    inner = jnp.mean(scaled * x, axis=-1, keepdims=True)
    out_ref[...] = dresid_ref[...] + inverse * scaled - x * (inverse * inverse * inverse * inner)


def finish(dq, dk, dv, weights, tokens, dresid, gain):
    rows, width = tokens.shape
    return pl.pallas_call(
        finish_kernel,
        grid=(rows // TILE,),
        in_specs=[
            row_block(dq.shape[1]), row_block(dk.shape[1]), row_block(dv.shape[1]), whole_block(weights.shape),
            row_block(width), row_block(width), whole_block((1, width)),
        ],
        out_specs=[row_block(width), whole_block((1, width))],
        out_shape=[jax.ShapeDtypeStruct((rows, width), F32), jax.ShapeDtypeStruct((1, width), F32)],
        compiler_params=params(),
        cost_estimate=cost(2 * rows * width * weights.shape[1], 20 * rows * width),
        name="finish",
    )(dq, dk, dv, weights, tokens, dresid, gain)


def flip(value, axis, bit):
    size = lax.axis_size(axis)
    return lax.ppermute(value, axis, [(i, i ^ bit) for i in range(size)])


def gather_experts(mats, owners):
    slots = {0: tuple([m] for m in mats)}
    if owners == 8:
        slots[2] = tuple([flip(m, "expert", 2)] for m in mats)
        slots[4] = tuple([flip(m, "expert", 4)] for m in mats)
        third = []
        for (a,), (b,) in zip(slots[2], slots[4]):
            cut = a.shape[0] // 2
            third.append([flip(a[:cut], "expert", 4), flip(b[cut:], "expert", 2)])
        slots[6] = tuple(third)
    else:
        bit = 2
        while bit < owners:
            for j in sorted(slots):
                slots[j | bit] = tuple([flip(p, "expert", bit) for p in m] for m in slots[j])
            bit *= 2
    for j in sorted(slots):
        slots[j | 1] = tuple([flip(p, "expert", 1) for p in m] for m in slots[j])
    return slots


def add(a, b):
    return (a.astype(F32) + b.astype(F32)).astype(BF16)


def reduce_experts(parts, owners):
    pairs = {}
    for j in parts:
        if j & 1:
            pairs[j ^ 1] = tuple(add(m, flip(s, "expert", 1)) for m, s in zip(parts[j ^ 1], parts[j]))
    if owners == 8:
        own = []
        for m0, m2, m4, m6 in zip(pairs[0], pairs[2], pairs[4], pairs[6]):
            cut = m0.shape[0] // 2
            left, right = flip(m6[:cut], "expert", 2), flip(m6[cut:], "expert", 4)
            top = add(m0[:cut], flip(m2[:cut], "expert", 2))
            bottom = add(m0[cut:], flip(m4[cut:], "expert", 4))
            top = add(top, flip(add(m4[:cut], left), "expert", 4))
            bottom = add(bottom, flip(add(m2[cut:], right), "expert", 2))
            own.append(jnp.concatenate([top, bottom], axis=0))
        return tuple(own)
    bit = 2
    while bit < owners:
        for j in sorted(pairs, reverse=True):
            if j & bit:
                gone = pairs.pop(j)
                pairs[j ^ bit] = tuple(add(m, flip(s, "expert", bit)) for m, s in zip(pairs[j ^ bit], gone))
        bit *= 2
    return pairs[0]


def on_device(
    tokens, gain_attn, w_query, key_weight, value_weight, w_out, gain_ffn, w_router, w_gate, w_up, w_down, routes, cotangent
):
    owners = lax.axis_size("expert")
    me = lax.axis_index("expert").astype(jnp.int32)[None]
    rows, width = tokens.shape
    experts = w_router.shape[1] * 1
    slots = gather_experts((w_gate[0], w_up[0], w_down[0]), owners)

    small = jnp.concatenate([gain_attn[:, None], gain_ffn[:, None], w_router], axis=1)
    packed = lax.all_gather(
        jnp.concatenate([w_query, key_weight, value_weight], axis=1), "wshard", axis=0, tiled=True
    )
    small = lax.all_gather(small, "wshard", axis=0, tiled=True)
    out_w = lax.all_gather(w_out, "wshard", axis=0, tiled=True)
    gain_one, gain_two = small[:, 0][None], small[:, 1][None]
    router_w = jnp.pad(small[:, 2:], ((0, 0), (0, LANES - experts)))
    cos, sin = (jnp.asarray(a) for a in rope_tables(rows))

    normed, queries, keys, vals = project(tokens, gain_one, packed, cos, sin)
    attended = attend(queries, keys, vals)
    resid, moe_in, moe_in_t, gates = middle(attended, out_w, tokens, gain_two, router_w, routes)

    order = [2, 3, 4, 5, 6, 7, 0, 1] if owners == 8 else list(range(owners))
    dy_t = cotangent.T
    acc, parts = None, {}
    for at in range(0, len(order), 2):
        pair = order[at : at + 2]
        acc, grads = moe(
            pair, me, moe_in, moe_in_t, cotangent, dy_t, gates, acc, [slots[j] for j in pair]
        )
        parts.update(zip(pair, grads))
    made, dmoe, gate_grads = acc
    mixed, dresid, dz, dattended, gain_two_grad, router_grad = turn(
        resid, made, dmoe, gates, gate_grads, cotangent, gain_two, router_w, moe_in_t, out_w
    )
    own = reduce_experts(parts, owners)
    out_grad = dot_tn(attended, dz)
    dq, dk, dv = attend_back(queries, keys, vals, dattended, cos, sin)
    qkv_grad = dot_tn(normed, jnp.concatenate([dq, dk, dv], axis=1))
    d_tokens, gain_one_grad = finish(dq, dk, dv, packed, tokens, dresid, gain_one)

    small_grad = jnp.concatenate([gain_one_grad.T, gain_two_grad.T, router_grad[:, :experts]], axis=1)

    def total(grad):
        return lax.psum(lax.psum_scatter(grad, "wshard", scatter_dimension=0, tiled=True), "expert")

    small_grad = total(small_grad)
    out_grad = total(out_grad.astype(BF16)).astype(F32)
    qkv_grad = total(qkv_grad.astype(BF16)).astype(F32)
    own = tuple(lax.psum(m, "wshard").astype(F32) for m in own)
    qw, kw = w_query.shape[1], key_weight.shape[1]
    return (
        mixed,
        d_tokens,
        small_grad[:, 0],
        qkv_grad[:, :qw],
        qkv_grad[:, qw : qw + kw],
        qkv_grad[:, qw + kw :],
        out_grad,
        small_grad[:, 1],
        small_grad[:, 2:],
        own[0][None],
        own[1][None],
        own[2].T[None],
    )


def solution(mesh):
    whole, shard, matrix, owned = P(("expert", "wshard"), None), P("wshard"), P("wshard", None), P("expert", None, None)
    return jax.shard_map(
        on_device,
        mesh=mesh,
        in_specs=(whole, shard, matrix, matrix, matrix, matrix, shard, matrix, owned, owned, owned, whole, whole),
        out_specs=(whole, whole, shard, matrix, matrix, matrix, matrix, shard, matrix, owned, owned, owned),
        check_vma=False,
    )
```

```python
import functools
import jax
import jax.numpy as jnp
import numpy as np
from jax import lax
from jax.experimental import pallas as pl
from jax.experimental.pallas import tpu as pltpu
from jax.sharding import PartitionSpec as P

QUERY_HEADS = 16
KEY_VALUE_HEADS = 8
HEAD_WIDTH = 64
SEQUENCE_LENGTH = 1024
BLOCK = 256
TILE = 256
LANES = 128
F32 = jnp.float32
BF16 = jnp.bfloat16
ANY = pl.BlockSpec(memory_space=pl.ANY)
VMEM = pl.BlockSpec(memory_space=pltpu.VMEM)
VMEM_BYTES = 60 * 1024 * 1024


def dot(a, b):
    return jnp.dot(a, b, preferred_element_type=F32)


def dot_nt(a, b):
    return lax.dot_general(a, b, (((1,), (1,)), ((), ())), preferred_element_type=F32)


def dot_tn(a, b):
    return lax.dot_general(a, b, (((0,), (0,)), ((), ())), preferred_element_type=F32)


def params(**kw):
    return pltpu.CompilerParams(vmem_limit_bytes=VMEM_BYTES, **kw)


def cost(flops, nbytes, transcendentals=0):
    return pl.CostEstimate(flops=int(flops), bytes_accessed=int(nbytes), transcendentals=int(transcendentals))


def rope_tables(rows):
    half = HEAD_WIDTH // 2
    freq = np.exp(-np.log(10000.0) * np.arange(half, dtype=np.float32) * 2.0 / HEAD_WIDTH).astype(np.float32)
    pos = (np.arange(rows) % SEQUENCE_LENGTH).astype(np.float32)
    angles = (pos[:, None] * freq[None, :]).astype(np.float32)
    cos, sin = np.cos(angles), np.sin(angles)
    return (
        np.concatenate([cos, cos, cos, cos], 1).astype(np.float32),
        np.concatenate([-sin, sin, -sin, sin], 1).astype(np.float32),
    )


def rope(u, cos, sin):
    half = HEAD_WIDTH // 2
    lane = lax.broadcasted_iota(jnp.int32, u.shape, 1)
    swapped = jnp.where(
        lane % HEAD_WIDTH < half, pltpu.roll(u, LANES - half, 1), pltpu.roll(u, half, 1)
    )
    return u * cos + swapped * sin


def row_block(width):
    return pl.BlockSpec((TILE, width), lambda i: (i, 0))


def whole_block(shape):
    return pl.BlockSpec(shape, lambda i: (0,) * len(shape))


def tied(kernel, inputs, ties):
    return lambda *refs: kernel(*refs[:inputs], *refs[inputs + len(ties) :])


def project_kernel(x_ref, gain_ref, w_ref, cos_ref, sin_ref, n_ref, q_ref, k_ref, v_ref):
    x = x_ref[...].astype(F32)
    inverse = lax.rsqrt(jnp.mean(x * x, axis=-1, keepdims=True) + 1e-06)
    normed = (x * inverse * gain_ref[...].astype(F32)).astype(BF16)
    n_ref[...] = normed
    cos, sin = cos_ref[...], sin_ref[...]
    step = 512
    for at in range(0, w_ref.shape[1], step):
        made = dot(normed, w_ref[:, at : at + step])
        for lo in range(0, step, LANES):
            u = made[:, lo : lo + LANES]
            c = at + lo
            if c < q_ref.shape[1]:
                q_ref[:, c : c + LANES] = (rope(u, cos, sin).astype(BF16) * jnp.asarray(HEAD_WIDTH**-0.5, BF16))
            elif c < q_ref.shape[1] + k_ref.shape[1]:
                c -= q_ref.shape[1]
                k_ref[:, c : c + LANES] = rope(u, cos, sin).astype(BF16)
            else:
                c -= q_ref.shape[1] + k_ref.shape[1]
                v_ref[:, c : c + LANES] = u.astype(BF16)


def project(tokens, gain, weights, cos, sin):
    rows, width = tokens.shape
    qw, kw = QUERY_HEADS * HEAD_WIDTH, KEY_VALUE_HEADS * HEAD_WIDTH
    return pl.pallas_call(
        project_kernel,
        grid=(rows // TILE,),
        in_specs=[row_block(width), whole_block((1, width)), whole_block(weights.shape), row_block(LANES), row_block(LANES)],
        out_specs=[row_block(width), row_block(qw), row_block(kw), row_block(kw)],
        out_shape=[jax.ShapeDtypeStruct((rows, w), BF16) for w in (width, qw, kw, kw)],
        compiler_params=params(),
        cost_estimate=cost(2 * rows * width * (qw + 2 * kw), 12 * rows * width),
        name="project",
    )(tokens, gain, weights, cos, sin)


def attend_kernel(q_ref, k_ref, v_ref, o_ref):
    for c in range(2):
        k = k_ref[:, c * HEAD_WIDTH : (c + 1) * HEAD_WIDTH]
        v = v_ref[:, c * HEAD_WIDTH : (c + 1) * HEAD_WIDTH]
        for h in range(2):
            at = (2 * c + h) * HEAD_WIDTH
            for b in range(SEQUENCE_LENGTH // BLOCK):
                n = (b + 1) * BLOCK
                rows = slice(b * BLOCK, (b + 1) * BLOCK)
                s = dot_nt(q_ref[rows, at : at + HEAD_WIDTH], k[:n])
                p = jnp.exp(s - jnp.max(s, axis=-1, keepdims=True))
                total = jnp.sum(p, axis=-1, keepdims=True)
                o = dot((p * (1.0 / total)).astype(BF16), v[:n])
                o_ref[rows, at : at + HEAD_WIDTH] = o.astype(BF16)


def head_block(width, sequence=SEQUENCE_LENGTH):
    return pl.BlockSpec((sequence, width), lambda s, i: (s, i))


def attend(queries, keys, vals):
    rows = queries.shape[0]
    steps = KEY_VALUE_HEADS // 2
    flops = 2 * QUERY_HEADS * rows * SEQUENCE_LENGTH * HEAD_WIDTH * 2
    return pl.pallas_call(
        attend_kernel,
        grid=(rows // SEQUENCE_LENGTH, steps),
        in_specs=[head_block(4 * HEAD_WIDTH), head_block(2 * HEAD_WIDTH), head_block(2 * HEAD_WIDTH)],
        out_specs=head_block(4 * HEAD_WIDTH),
        out_shape=jax.ShapeDtypeStruct(queries.shape, BF16),
        compiler_params=params(),
        cost_estimate=cost(flops * 8, 6 * rows * 1024, QUERY_HEADS * rows * 640),
        name="attend",
    )(queries, keys, vals)


def attend_back_kernel(q_ref, k_ref, v_ref, g_ref, cos_ref, sin_ref, dq_ref, dk_ref, dv_ref, dk_acc, dv_acc, dq_acc):
    dk_acc[...] = jnp.zeros_like(dk_acc)
    dv_acc[...] = jnp.zeros_like(dv_acc)
    for c in range(2):
        lanes = slice(c * HEAD_WIDTH, (c + 1) * HEAD_WIDTH)
        k, v = k_ref[:, lanes], v_ref[:, lanes]
        for h in range(2):
            at = slice((2 * c + h) * HEAD_WIDTH, (2 * c + h + 1) * HEAD_WIDTH)
            for b in range(SEQUENCE_LENGTH // BLOCK):
                n = (b + 1) * BLOCK
                rows = slice(b * BLOCK, (b + 1) * BLOCK)
                q, g = q_ref[rows, at], g_ref[rows, at]
                s = dot_nt(k[:n], q)
                dp = dot_nt(v[:n], g)
                p = jnp.exp(s - jnp.max(s, axis=0, keepdims=True))
                p = p * (1.0 / jnp.sum(p, axis=0, keepdims=True))
                ds = (p * (dp - jnp.sum(p * dp, axis=0, keepdims=True))).astype(BF16)
                dv_acc[:n, lanes] += dot(p.astype(BF16), g)
                dk_acc[:n, lanes] += dot(ds, q)
                dq_acc[rows, at] = dot_tn(ds, k[:n])
    cos, sin = cos_ref[...], -sin_ref[...]
    scale = HEAD_WIDTH**-0.5
    dq_ref[:, :LANES] = rope(dq_acc[:, :LANES] * scale, cos, sin).astype(BF16)
    dq_ref[:, LANES:] = rope(dq_acc[:, LANES:] * scale, cos, sin).astype(BF16)
    dk_ref[...] = rope(dk_acc[...], cos, sin).astype(BF16)
    dv_ref[...] = dv_acc[...].astype(BF16)


def attend_back(queries, keys, vals, grad, cos, sin, first=0, steps=KEY_VALUE_HEADS // 2, ties=()):
    rows = queries.shape[0]
    flops = 5 * QUERY_HEADS * rows * SEQUENCE_LENGTH * HEAD_WIDTH * 2 * steps // (KEY_VALUE_HEADS // 2)
    table = pl.BlockSpec((SEQUENCE_LENGTH, LANES), lambda s, i: (s, 0))

    def block(width, start):
        return pl.BlockSpec((SEQUENCE_LENGTH, width), lambda s, i: (s, i + start))

    two, four = block(2 * HEAD_WIDTH, first), block(4 * HEAD_WIDTH, first)
    out_two, out_four = block(2 * HEAD_WIDTH, 0), block(4 * HEAD_WIDTH, 0)
    return pl.pallas_call(
        tied(attend_back_kernel, 6, ties),
        grid=(rows // SEQUENCE_LENGTH, steps),
        in_specs=[four, two, two, four, table, table] + [ANY] * len(ties),
        out_specs=[out_four, out_two, out_two],
        out_shape=[jax.ShapeDtypeStruct((rows, steps * w), BF16) for w in (4 * HEAD_WIDTH, 2 * HEAD_WIDTH, 2 * HEAD_WIDTH)],
        scratch_shapes=[
            pltpu.VMEM((SEQUENCE_LENGTH, LANES), F32),
            pltpu.VMEM((SEQUENCE_LENGTH, LANES), F32),
            pltpu.VMEM((SEQUENCE_LENGTH, 2 * LANES), F32),
        ],
        compiler_params=params(),
        cost_estimate=cost(flops * 8, 12 * rows * 1024, QUERY_HEADS * rows * 640),
        name="attend_back",
    )(queries, keys, vals, grad, cos, sin, *ties)


def middle_kernel(a_ref, w_ref, x_ref, gain_ref, router_ref, routes_ref, r_ref, m_ref, mt_ref, gates_ref):
    resid = x_ref[...].astype(F32) + dot(a_ref[...], w_ref[...])
    r_ref[...] = resid
    inverse = lax.rsqrt(jnp.mean(resid * resid, axis=-1, keepdims=True) + 1e-06)
    moe_in = (resid * inverse * gain_ref[...].astype(F32)).astype(BF16)
    m_ref[...] = moe_in
    mt_ref[...] = moe_in.T
    logits = dot(moe_in, router_ref[...])
    lane = lax.broadcasted_iota(jnp.int32, logits.shape, 1)
    routes = routes_ref[...]
    picked = lane == routes[:, 0:1]
    for k in range(1, routes.shape[1]):
        picked = jnp.logical_or(picked, lane == routes[:, k : k + 1])
    logits = jnp.where(picked, logits, -1e30)
    weights = jnp.where(picked, jnp.exp(logits - jnp.max(logits, axis=-1, keepdims=True)), 0.0)
    gates_ref[...] = weights / jnp.sum(weights, axis=-1, keepdims=True)


def middle(attended, out_w, tokens, gain, router_w, routes):
    rows, width = tokens.shape
    return pl.pallas_call(
        middle_kernel,
        grid=(rows // TILE,),
        in_specs=[
            row_block(width),
            whole_block(out_w.shape),
            row_block(width),
            whole_block((1, width)),
            whole_block(router_w.shape),
            row_block(routes.shape[1]),
        ],
        out_specs=[row_block(width), row_block(width), pl.BlockSpec((width, TILE), lambda i: (0, i)), row_block(LANES)],
        out_shape=[
            jax.ShapeDtypeStruct((rows, width), F32),
            jax.ShapeDtypeStruct((rows, width), BF16),
            jax.ShapeDtypeStruct((width, rows), BF16),
            jax.ShapeDtypeStruct((rows, LANES), F32),
        ],
        compiler_params=params(),
        cost_estimate=cost(2 * rows * width * (width + LANES), 14 * rows * width),
        name="middle",
    )(attended, out_w, tokens, gain, router_w, routes)


def moe_kernel(slots, chunks, first, ties, me_ref, *refs):
    refs = list(refs)
    take = lambda count: [refs.pop(0) for _ in range(count)]
    x_hbm, xt_hbm, dy_hbm, dyt_hbm, gates_ref = take(5)
    if not first:
        made_in, dmoe_in, gg_in = take(3)
    weights = [[take(count) for count in per_slot] for per_slot in chunks]
    take(ties)
    made_out, dmoe_out, gg_ref = take(3)
    grads = [take(2) for _ in slots]
    x, xt, dy, dyt, made, dmoe, wg, wu, wd, hg, dg, du, stage, sem_in, sem_w, sem_out, sem_acc = take(17)
    rows = x.shape[0]
    tiles = rows // TILE

    def load(source, target, sem):
        copy = pltpu.make_async_copy(source, target, sem)
        copy.start()
        return copy

    def load_weights(index):
        buffer = index % 2
        out = []
        for which, target in enumerate((wg, wu, wd)):
            at, copies = 0, []
            for piece, ref in enumerate(weights[index][which]):
                count = ref.shape[0]
                copies.append(load(ref, target.at[buffer, at : at + count], sem_w.at[buffer, which, piece]))
                at += count
            out.append(copies)
        return out

    pending = {0: load_weights(0)}
    inputs = [load(a, b, sem_in.at[i]) for i, (a, b) in enumerate(((x_hbm, x), (dy_hbm, dy)))]
    if not first:
        acc = [load(made_in, made, sem_acc.at[0]), load(dmoe_in, dmoe, sem_acc.at[1])]
        gg_ref[...] = gg_in[...]
    else:
        acc = []
        made[...] = jnp.zeros_like(made)
        dmoe[...] = jnp.zeros_like(dmoe)
        gg_ref[...] = jnp.zeros_like(gg_ref)
    late = [load(a, b, sem_in.at[i]) for i, (a, b) in enumerate(((xt_hbm, xt), (dyt_hbm, dyt)), 2)]
    for copy in inputs:
        copy.wait()
    stores = []
    lane = lax.broadcasted_iota(jnp.int32, (TILE, LANES), 1)
    for index, slot in enumerate(slots):
        buffer = index % 2
        for copies in pending.pop(index):
            for copy in copies:
                copy.wait()
        if index + 1 < len(slots):
            pending[index + 1] = load_weights(index + 1)
        for copy in acc:
            copy.wait()
        acc = []
        me = me_ref[0] ^ slot
        g_w, u_w, d_w = wg.at[buffer], wu.at[buffer], wd.at[buffer]

        def rows_step(i, carry):
            at = pl.ds(pl.multiple_of(i * TILE, TILE), TILE)
            xi, yi = x[at], dy[at]
            gate, upval, pre = dot(xi, g_w[...]), dot(xi, u_w[...]), dot_nt(yi, d_w[...])
            column = jnp.sum(jnp.where(lane == me, gates_ref[at], 0.0), axis=1, keepdims=True)
            sigma = 1.0 / (1.0 + jnp.exp(-gate))
            silu = gate * sigma
            hidden = silu * upval
            gained = jnp.sum(hidden * pre, axis=1, keepdims=True)
            gg_ref[at] = gg_ref[at] + jnp.where(lane == me, gained, 0.0)
            weighted = (hidden * column).astype(BF16)
            dhidden = pre * column
            dgate = (dhidden * upval * (sigma + silu * (1.0 - sigma))).astype(BF16)
            dup = (dhidden * silu).astype(BF16)
            hg[at], dg[at], du[at] = weighted, dgate, dup
            made[at] += dot(weighted, d_w[...])
            dmoe[at] += dot_nt(dgate, g_w[...]) + dot_nt(dup, u_w[...])
            return carry

        lax.fori_loop(0, tiles, rows_step, 0)
        for copy in late:
            copy.wait()
        late = []
        for copy in stores:
            copy.wait()
        stores = []

        def grads_step(i, carry):
            at = pl.ds(pl.multiple_of(i * TILE, TILE), TILE)
            a = xt[at]
            stage[0, at] = dot(a, dg[...]).astype(BF16)
            stage[1, at] = dot(a, du[...]).astype(BF16)
            stage[2, at] = dot(dyt[at], hg[...]).astype(BF16)
            return carry

        lax.fori_loop(0, x.shape[1] // TILE, grads_step, 0)
        half = stage.shape[1] // 2
        for part in range(2):
            stores.append(load(stage.at[:, part * half : (part + 1) * half], grads[index][part], sem_out.at[part]))
    done = [load(made, made_out, sem_acc.at[0]), load(dmoe, dmoe_out, sem_acc.at[1])]
    for copy in stores + done:
        copy.wait()


def moe(slots, me, moe_in, moe_in_t, dy, dy_t, gates, acc, weights, ties=()):
    rows, width = moe_in.shape
    hidden = weights[0][0][0].shape[1]
    first = acc is None
    flat = [piece for per_slot in weights for pieces in per_slot for piece in pieces]
    chunks = tuple(tuple(len(pieces) for pieces in per_slot) for per_slot in weights)
    accs = [] if first else list(acc)
    grad = jax.ShapeDtypeStruct((3, width // 2, hidden), BF16)
    outs = pl.pallas_call(
        functools.partial(moe_kernel, tuple(slots), chunks, first, len(ties)),
        in_specs=[pl.BlockSpec(memory_space=pltpu.SMEM), ANY, ANY, ANY, ANY, VMEM]
        + ([] if first else [ANY, ANY, VMEM])
        + [ANY] * (len(flat) + len(ties)),
        out_specs=[ANY, ANY, VMEM] + [ANY] * (2 * len(slots)),
        out_shape=[
            jax.ShapeDtypeStruct((rows, width), F32),
            jax.ShapeDtypeStruct((rows, width), F32),
            jax.ShapeDtypeStruct((rows, LANES), F32),
        ]
        + [grad] * (2 * len(slots)),
        scratch_shapes=[
            pltpu.VMEM((rows, width), BF16),
            pltpu.VMEM((width, rows), BF16),
            pltpu.VMEM((rows, width), BF16),
            pltpu.VMEM((width, rows), BF16),
            pltpu.VMEM((rows, width), F32),
            pltpu.VMEM((rows, width), F32),
            pltpu.VMEM((2, width, hidden), BF16),
            pltpu.VMEM((2, width, hidden), BF16),
            pltpu.VMEM((2, hidden, width), BF16),
            pltpu.VMEM((rows, hidden), BF16),
            pltpu.VMEM((rows, hidden), BF16),
            pltpu.VMEM((rows, hidden), BF16),
            pltpu.VMEM((3, width, hidden), BF16),
            pltpu.SemaphoreType.DMA((4,)),
            pltpu.SemaphoreType.DMA((2, 3, 2)),
            pltpu.SemaphoreType.DMA((2,)),
            pltpu.SemaphoreType.DMA((2,)),
        ],
        compiler_params=params(),
        cost_estimate=cost(18 * rows * width * hidden * len(slots), 20 * rows * width),
        name="experts",
    )(me, moe_in, moe_in_t, dy, dy_t, gates, *accs, *flat, *ties)
    return outs[:3], [tuple(outs[3 + 2 * i : 5 + 2 * i]) for i in range(len(slots))]


def turn_kernel(
    resid_ref, made_ref, dmoe_ref, gates_ref, gg_ref, dy_ref, gain_ref, router_ref, mt_ref, w_ref,
    mixed_ref, dresid_ref, dz_ref, da_ref, gain_grad_ref, router_grad_ref,
):
    @pl.when(pl.program_id(0) == 0)
    def _():
        gain_grad_ref[...] = jnp.zeros_like(gain_grad_ref)
        router_grad_ref[...] = jnp.zeros_like(router_grad_ref)

    resid = resid_ref[...]
    mixed_ref[...] = (resid + made_ref[...]).astype(BF16)
    gates, gg = gates_ref[...], gg_ref[...]
    dlogits = (gates * (gg - jnp.sum(gates * gg, axis=1, keepdims=True))).astype(BF16)
    router_grad_ref[...] += dot(mt_ref[...], dlogits)
    dmoe = dmoe_ref[...] + dot_nt(dlogits, router_ref[...])
    inverse = lax.rsqrt(jnp.mean(resid * resid, axis=-1, keepdims=True) + 1e-06)
    gain_grad_ref[...] += jnp.sum(dmoe * resid * inverse, axis=0, keepdims=True)
    scaled = dmoe * gain_ref[...].astype(F32)
    inner = jnp.mean(scaled * resid, axis=-1, keepdims=True)
    dresid = dy_ref[...].astype(F32) + inverse * scaled - resid * (inverse * inverse * inverse * inner)
    dresid_ref[...] = dresid
    dz = dresid.astype(BF16)
    dz_ref[...] = dz
    da_ref[...] = dot_nt(dz, w_ref[...]).astype(BF16)


def turn(resid, made, dmoe, gates, gg, dy, gain, router_w, moe_in_t, out_w, ties=()):
    rows, width = resid.shape
    return pl.pallas_call(
        tied(turn_kernel, 10, ties),
        grid=(rows // TILE,),
        in_specs=[
            row_block(width), row_block(width), row_block(width), row_block(LANES), row_block(LANES), row_block(width),
            whole_block((1, width)), whole_block(router_w.shape), pl.BlockSpec((width, TILE), lambda i: (0, i)),
            whole_block(out_w.shape),
        ]
        + [ANY] * len(ties),
        out_specs=[row_block(width)] * 4 + [whole_block((1, width)), whole_block((width, LANES))],
        out_shape=[
            jax.ShapeDtypeStruct((rows, width), BF16),
            jax.ShapeDtypeStruct((rows, width), F32),
            jax.ShapeDtypeStruct((rows, width), BF16),
            jax.ShapeDtypeStruct((rows, width), BF16),
            jax.ShapeDtypeStruct((1, width), F32),
            jax.ShapeDtypeStruct((width, LANES), F32),
        ],
        compiler_params=params(),
        cost_estimate=cost(2 * rows * width * (width + 2 * LANES), 28 * rows * width),
        name="turn",
    )(resid, made, dmoe, gates, gg, dy, gain, router_w, moe_in_t, out_w, *ties)


def finish_kernel(count, *refs):
    grads = refs[:count]
    w_ref, x_ref, dresid_ref, gain_ref, out_ref, gain_grad_ref = refs[count:]

    @pl.when(pl.program_id(0) == 0)
    def _():
        gain_grad_ref[...] = jnp.zeros_like(gain_grad_ref)

    at, dn = 0, 0.0
    for ref in grads:
        dn += dot_nt(ref[...], w_ref[:, at : at + ref.shape[1]])
        at += ref.shape[1]
    x = x_ref[...].astype(F32)
    inverse = lax.rsqrt(jnp.mean(x * x, axis=-1, keepdims=True) + 1e-06)
    gain_grad_ref[...] += jnp.sum(dn * x * inverse, axis=0, keepdims=True)
    scaled = dn * gain_ref[...].astype(F32)
    inner = jnp.mean(scaled * x, axis=-1, keepdims=True)
    out_ref[...] = dresid_ref[...] + inverse * scaled - x * (inverse * inverse * inverse * inner)


def finish(grads, weights, tokens, dresid, gain, ties=()):
    rows, width = tokens.shape
    return pl.pallas_call(
        tied(functools.partial(finish_kernel, len(grads)), len(grads) + 4, ties),
        grid=(rows // TILE,),
        in_specs=[row_block(g.shape[1]) for g in grads]
        + [whole_block(weights.shape), row_block(width), row_block(width), whole_block((1, width))]
        + [ANY] * len(ties),
        out_specs=[row_block(width), whole_block((1, width))],
        out_shape=[jax.ShapeDtypeStruct((rows, width), F32), jax.ShapeDtypeStruct((1, width), F32)],
        compiler_params=params(),
        cost_estimate=cost(2 * rows * width * weights.shape[1], 20 * rows * width),
        name="finish",
    )(*grads, weights, tokens, dresid, gain, *ties)


def plus_kernel(*refs):
    total = refs[0][...].astype(F32)
    for ref in refs[1:-1]:
        total += ref[...].astype(F32)
    refs[-1][...] = total.astype(BF16)


def plus(*terms, ties=()):
    shape = terms[0].shape
    block = pl.BlockSpec((1,) + shape[1:], lambda i: (i, 0, 0))
    return pl.pallas_call(
        tied(plus_kernel, len(terms), ties),
        grid=(shape[0],),
        in_specs=[block] * len(terms) + [ANY] * len(ties),
        out_specs=block,
        out_shape=jax.ShapeDtypeStruct(shape, BF16),
        compiler_params=params(),
        cost_estimate=cost(len(terms) * terms[0].size, 2 * (len(terms) + 1) * terms[0].size),
        name="plus",
    )(*terms, *ties)


def gather_kernel(size, q_ref, k_ref, v_ref, s_ref, o_ref, packed_ref, small_ref, out_ref, send_sem, recv_sem, pass_sem, take_sem):
    me, z = lax.axis_index("expert"), lax.axis_index("wshard")
    core = lax.rem(me, 2)
    sibling = me + 1 - 2 * core
    rows = q_ref.shape[0]
    half = rows // 2
    there = lambda step: jnp.logical_and(z + step >= 0, z + step < size)

    barrier = pltpu.get_barrier_semaphore()
    pl.semaphore_signal(barrier, inc=1, device_id=(sibling, z), device_id_type=pl.DeviceIdType.MESH)
    for step in (1, -1):

        @pl.when(there(step))
        def _():
            pl.semaphore_signal(barrier, inc=1, device_id=(me, z + step), device_id_type=pl.DeviceIdType.MESH)

    pl.semaphore_wait(barrier, 1 + jnp.where(z > 0, 1, 0) + jnp.where(z < size - 1, 1, 0))

    own = pl.ds(pl.multiple_of(z * rows, rows), rows)
    at = 0
    for ref in (q_ref, k_ref, v_ref):
        packed_ref[own, at : at + ref.shape[1]] = ref[...]
        at += ref.shape[1]
    small_ref[own] = s_ref[...]

    def moves(way, hop, origin, which, device, send, recv):
        at = pl.ds(pl.multiple_of(origin * rows + which * half, half), half)
        return [
            pltpu.make_async_remote_copy(
                src_ref=ref.at[at], dst_ref=ref.at[at], send_sem=send.at[way, hop, i], recv_sem=recv.at[way, hop, i],
                device_id=device, device_id_type=pl.DeviceIdType.MESH,
            )
            for i, ref in enumerate((packed_ref, small_ref))
        ]

    def onward(way, step, hop):
        return moves(way, hop, z - step * (hop - 1), core, (me, z + step), send_sem, recv_sem)

    def across(way, step, hop, which):
        return moves(way, hop, z - step * hop, which, (sibling, z), pass_sem, take_sem)

    ways = ((0, 1), (1, -1))
    for way, step in ways:

        @pl.when(there(step))
        def _():
            for move in onward(way, step, 1):
                move.start()

    for hop in range(1, size):
        for way, step in ways:

            @pl.when(there(-step * hop))
            def _():
                for move in moves(way, hop, z - step * hop, core, (me, z), send_sem, recv_sem):
                    move.wait_recv()

                @pl.when(there(step))
                def _():
                    for move in onward(way, step, hop + 1):
                        move.start()

                for move in across(way, step, hop, core):
                    move.start()

    for hop in range(1, size):
        for way, step in ways:

            @pl.when(there(-step * hop))
            def _():
                for move in across(way, step, hop, 1 - core):
                    move.wait_recv()
                for move in across(way, step, hop, core):
                    move.wait_send()

            @pl.when(jnp.logical_and(there(step), there(-step * (hop - 1))))
            def _():
                for move in onward(way, step, hop):
                    move.wait_send()

    out_ref[...] = o_ref[...]


def gather_weights(query, key, value, small, out):
    size = lax.axis_size("wshard")
    rows = query.shape[0]
    width = query.shape[1] + key.shape[1] + value.shape[1]
    sems = pltpu.SemaphoreType.DMA((2, size + 1, 2))
    return pl.pallas_call(
        functools.partial(gather_kernel, size),
        in_specs=[VMEM] * 5,
        out_specs=[VMEM] * 3,
        out_shape=[
            jax.ShapeDtypeStruct((size * rows, width), BF16),
            jax.ShapeDtypeStruct((size * rows, small.shape[1]), BF16),
            jax.ShapeDtypeStruct(out.shape, BF16),
        ],
        scratch_shapes=[sems, sems, sems, sems],
        compiler_params=pltpu.CompilerParams(collective_id=0, has_side_effects=True, vmem_limit_bytes=VMEM_BYTES),
        cost_estimate=cost(1e9, 12 * rows * size * width),
        name="gather_weights",
    )(query, key, value, small, out)


def reduce_kernel(size, columns, *refs):
    count = len(columns)
    ins, outs = refs[:count], refs[count : 2 * count]
    acc, rc, r1, r2, zs, rz, res, send_sem, recv_sem = refs[2 * count :]
    me, z = lax.axis_index("expert"), lax.axis_index("wshard")
    core, xb, yb = lax.rem(me, 2), lax.rem(me // 2, 2), me // 4
    sibling, xp, yp = me + 1 - 2 * core, me + 2 - 4 * xb, me + 4 - 8 * yb
    half = ins[0].shape[1] // 2
    n1, n2 = half // 4, half // 8

    barrier = pltpu.get_barrier_semaphore()
    for peer in (sibling, xp, yp):
        pl.semaphore_signal(barrier, inc=1, device_id=(peer, z), device_id_type=pl.DeviceIdType.MESH)
    for d in range(1, size):
        pl.semaphore_signal(barrier, inc=1, device_id=(me, lax.rem(z + d, size)), device_id_type=pl.DeviceIdType.MESH)
    pl.semaphore_wait(barrier, 2 + size)

    pieces, at = [], 0
    for ref, out, width in zip(ins, outs, columns):
        step = width if width <= 512 else 512
        for lo in range(0, width, step):
            pieces.append((ref, out, lo, step, at))
            at += step

    sent = []

    def move(source, target, piece, kind, device):
        copy = pltpu.make_async_remote_copy(
            src_ref=source, dst_ref=target, send_sem=send_sem.at[kind, piece], recv_sem=recv_sem.at[kind, piece],
            device_id=device, device_id_type=pl.DeviceIdType.MESH,
        )
        copy.start()
        sent.append(copy)
        return copy

    def rows(start, length):
        return pl.ds(pl.multiple_of(start, 16), length)

    def sum_of(*terms):
        total = terms[0].astype(F32)
        for term in terms[1:]:
            total += term.astype(F32)
        return total

    k0, k1 = xb * n1 + yb * n2, half // 2 + yb * n1 + xb * n2
    base = core * half
    first = []
    for p, (ref, _, lo, w, at) in enumerate(pieces):
        first.append(move(ref.at[:, rows((1 - core) * half, half), lo : lo + w], rc.at[:, :, at : at + w], p, 0, (sibling, z)))
    second = []
    for p, (ref, _, lo, w, at) in enumerate(pieces):
        c = slice(at, at + w)
        first[p].wait_recv()
        acc[:, :, c] = sum_of(ref[:, rows(base, half), lo : lo + w], rc[:, :, c]).astype(BF16)
        second.append((
            move(acc.at[:, rows((1 - xb) * n1, n1), c], r1.at[0, :, :, c], p, 1, (xp, z)),
            move(acc.at[:, rows(half // 2 + (1 - yb) * n1, n1), c], r1.at[1, :, :, c], p, 2, (yp, z)),
        ))
    third = []
    for p, (_, _, _, w, at) in enumerate(pieces):
        c = slice(at, at + w)
        keep = (rows(xb * n1, n1), rows(half // 2 + yb * n1, n1))
        for i in range(2):
            second[p][i].wait_recv()
            acc[:, keep[i], c] = sum_of(acc[:, keep[i], c], r1[i, :, :, c]).astype(BF16)
        third.append((
            move(acc.at[:, rows(xb * n1 + (1 - yb) * n2, n2), c], r2.at[0, :, :, c], p, 3, (yp, z)),
            move(acc.at[:, rows(half // 2 + yb * n1 + (1 - xb) * n2, n2), c], r2.at[1, :, :, c], p, 4, (xp, z)),
        ))
    fourth = []
    for p, (_, _, _, w, at) in enumerate(pieces):
        c = slice(at, at + w)
        for i, k in enumerate((k0, k1)):
            third[p][i].wait_recv()
            zs[:, i * n2 : (i + 1) * n2, c] = sum_of(acc[:, rows(k, n2), c], r2[i, :, :, c]).astype(BF16)
        fourth.append([
            move(zs.at[lax.rem(z + d, size), :, c], rz.at[d - 1, :, c], p, 8 + d, (me, lax.rem(z + d, size)))
            for d in range(1, size)
        ])
    fifth = []
    for p, (_, _, _, w, at) in enumerate(pieces):
        c = slice(at, at + w)
        for copy in fourth[p]:
            copy.wait_recv()
        total = sum_of(zs[z, :, c], *[rz[d, :, c] for d in range(size - 1)]).astype(BF16)
        for i, k in enumerate((k0, k1)):
            res[rows(base + k, n2), c] = total[i * n2 : (i + 1) * n2]
        fifth.append((
            move(res.at[rows(base + k0, n2), c], res.at[rows(base + k0, n2), c], p, 5, (yp, z)),
            move(res.at[rows(base + k1, n2), c], res.at[rows(base + k1, n2), c], p, 6, (xp, z)),
        ))
    sixth = []
    for p, (_, _, _, w, at) in enumerate(pieces):
        c = slice(at, at + w)
        for copy in fifth[p]:
            copy.wait_recv()
        mine = rows(base + xb * n1, n1), rows(base + half // 2 + yb * n1, n1)
        sixth.append((
            move(res.at[mine[0], c], res.at[mine[0], c], p, 7, (xp, z)),
            move(res.at[mine[1], c], res.at[mine[1], c], p, 8, (yp, z)),
        ))
    last = []
    for p, (_, _, _, w, at) in enumerate(pieces):
        c = slice(at, at + w)
        for copy in sixth[p]:
            copy.wait_recv()
        last.append(move(res.at[rows(base, half), c], res.at[rows(base, half), c], p, 8 + size, (sibling, z)))
    for p, (_, out, lo, w, at) in enumerate(pieces):
        last[p].wait_recv()
        out[:, lo : lo + w] = res[:, at : at + w].astype(F32)
    for copy in sent:
        copy.wait_send()


def reduce_all(*grads):
    size = lax.axis_size("wshard")
    rows = grads[0].shape[0] // size
    columns = tuple(g.shape[1] for g in grads)
    count = sum(-(-c // 512) for c in columns)
    width, half = sum(columns), rows // 2
    return pl.pallas_call(
        functools.partial(reduce_kernel, size, columns),
        in_specs=[VMEM] * len(grads),
        out_specs=[VMEM] * len(grads),
        out_shape=[jax.ShapeDtypeStruct((rows, c), F32) for c in columns],
        scratch_shapes=[
            pltpu.VMEM((size, half, width), BF16),
            pltpu.VMEM((size, half, width), BF16),
            pltpu.VMEM((2, size, half // 4, width), BF16),
            pltpu.VMEM((2, size, half // 8, width), BF16),
            pltpu.VMEM((size, half // 4, width), BF16),
            pltpu.VMEM((size - 1, half // 4, width), BF16),
            pltpu.VMEM((rows, width), BF16),
            pltpu.SemaphoreType.DMA((9 + size, count)),
            pltpu.SemaphoreType.DMA((9 + size, count)),
        ],
        compiler_params=pltpu.CompilerParams(collective_id=1, has_side_effects=True, vmem_limit_bytes=VMEM_BYTES),
        cost_estimate=cost(1e9, 8 * size * rows * width),
        name="reduce_all",
    )(*[g.reshape(size, rows, g.shape[1]) for g in grads])


def flip(value, axis, bit):
    size = lax.axis_size(axis)
    return lax.ppermute(value, axis, [(i, i ^ bit) for i in range(size)])


def gather_experts(mats, owners):
    slots = {0: tuple([m] for m in mats)}
    if owners == 8:
        slots[2] = tuple([flip(m, "expert", 2)] for m in mats)
        slots[4] = tuple([flip(m, "expert", 4)] for m in mats)
        third = []
        for (a,), (b,) in zip(slots[2], slots[4]):
            cut = a.shape[0] // 2
            third.append([flip(a[:cut], "expert", 4), flip(b[cut:], "expert", 2)])
        slots[6] = tuple(third)
    else:
        bit = 2
        while bit < owners:
            for j in sorted(slots):
                slots[j | bit] = tuple([flip(p, "expert", bit) for p in m] for m in slots[j])
            bit *= 2
    return slots


def across_core(slot):
    return tuple([flip(p, "expert", 1) for p in m] for m in slot)


def add(a, b):
    return (a.astype(F32) + b.astype(F32)).astype(BF16)


def reduce_experts(parts, owners):
    bit = 1
    while bit < owners:
        for j in sorted(parts, reverse=True):
            if j & bit:
                gone = parts.pop(j)
                parts[j ^ bit] = tuple(add(m, flip(s, "expert", bit)) for m, s in zip(parts[j ^ bit], gone))
        bit *= 2
    return parts[0]


def on_device(
    tokens, gain_attn, w_query, key_weight, value_weight, w_out, gain_ffn, w_router, w_gate, w_up, w_down, routes, cotangent
):
    owners = lax.axis_size("expert")
    me = lax.axis_index("expert").astype(jnp.int32)[None]
    rows, width = tokens.shape
    experts = w_router.shape[1]
    slots = gather_experts((w_gate[0], w_up[0], w_down[0]), owners)

    small = jnp.concatenate([gain_attn[:, None], gain_ffn[:, None], w_router], axis=1)
    small = jnp.pad(small, ((0, 0), (0, LANES - small.shape[1])))
    packed, small, out_shard = gather_weights(w_query, key_weight, value_weight, small, w_out)
    out_w = lax.all_gather(out_shard, "wshard", axis=0, tiled=True)
    gain_one, gain_two = small[:, 0][None], small[:, 1][None]
    router_w = jnp.pad(small[:, 2 : 2 + experts], ((0, 0), (0, LANES - experts)))
    cos, sin = (jnp.asarray(a) for a in rope_tables(rows))

    normed, queries, keys, vals = project(tokens, gain_one, packed, cos, sin)
    attended = attend(queries, keys, vals)
    resid, moe_in, moe_in_t, gates = middle(attended, out_w, tokens, gain_two, router_w, routes)
    dy_t = cotangent.T
    for j in sorted(slots):
        here = slots[j] if j == 0 else lax.optimization_barrier((slots[j], attended))[0]
        slots[j | 1] = across_core(here)

    def some(pair, acc, ties=()):
        return moe(pair, me, moe_in, moe_in_t, cotangent, dy_t, gates, acc, [slots[j] for j in pair], ties)

    def turned(acc, ties=()):
        made, dmoe, gate_grads = acc
        return turn(resid, made, dmoe, gates, gate_grads, cotangent, gain_two, router_w, moe_in_t, out_w, ties)

    if owners == 8:
        core = lambda halves: [flip(m, "expert", 1) for m in halves]
        over_x = lambda m: flip(m, "expert", 2)
        over_y = lambda m: flip(m, "expert", 4)
        both = lambda a, b: [plus(m, n) for m, n in zip(a, b)]
        acc, (g2, g3) = some([2, 3], None)
        c3 = core(g3)
        acc, (g6, g7) = some([6, 7], acc)
        s2 = both(g2, c3)
        c7 = core(g7)
        x20 = over_x(s2[0])
        acc, (g4, g5) = some([4, 5], acc, [*s2])
        s6 = both(g6, c7)
        c5 = core(g5)
        x60, y61 = over_x(s6[0]), over_y(s6[1])
        acc, (g0, g1) = some([0, 1], acc, [*s6, x20])
        s4 = both(g4, c5)
        c1 = core(g1)
        left, right = plus(s4[0], x60), plus(s2[1], y61)
        y41, x21 = over_y(s4[1]), over_x(right)
        mixed, dresid, dz, dattended, gain_two_grad, router_grad = turned(acc, [left, right, s4[1]])
        out_grad = dot_tn(attended, dz)
        s0 = both(g0, c1)
        y40 = over_y(left)
        early = attend_back(queries, keys, vals, dattended, cos, sin, 0, 2, [*s0])
        own = [plus(s0[0], x20, y40, ties=early[2:]), plus(s0[1], y41, x21, ties=early[2:])]
        late = attend_back(queries, keys, vals, dattended, cos, sin, 2, 2, own)
        pieces = [early[0], late[0], early[1], late[1], early[2], late[2]]
    else:
        acc, parts = None, {}
        for at in range(0, owners, 2):
            acc, grads = some([at, at + 1], acc)
            parts.update(zip([at, at + 1], grads))
        mixed, dresid, dz, dattended, gain_two_grad, router_grad = turned(acc)
        own = reduce_experts(parts, owners)
        out_grad = dot_tn(attended, dz)
        pieces = attend_back(queries, keys, vals, dattended, cos, sin)
    qkv_grad = dot_tn(normed, jnp.concatenate(pieces, axis=1)).astype(BF16)
    d_tokens, gain_one_grad = finish(pieces, packed, tokens, dresid, gain_one)

    small_grad = jnp.concatenate([gain_one_grad.T, gain_two_grad.T, router_grad[:, :experts]], axis=1)

    small_grad = jnp.pad(small_grad, ((0, 0), (0, LANES - small_grad.shape[1]))).astype(BF16)
    grads = (out_grad.astype(BF16), qkv_grad, small_grad)
    if owners == 8:
        out_grad, qkv_grad, small_grad = reduce_all(*grads)
    else:
        out_grad, qkv_grad, small_grad = (
            lax.psum(lax.psum_scatter(g, "wshard", scatter_dimension=0, tiled=True), "expert").astype(F32) for g in grads
        )
    own = jnp.concatenate(lax.psum(tuple(own), "wshard"), axis=1).astype(F32)
    qw, kw = w_query.shape[1], key_weight.shape[1]
    return (
        mixed,
        d_tokens,
        small_grad[:, 0],
        qkv_grad[:, :qw],
        qkv_grad[:, qw : qw + kw],
        qkv_grad[:, qw + kw :],
        out_grad,
        small_grad[:, 1],
        small_grad[:, 2 : 2 + experts],
        own[0:1],
        own[1:2],
        own[2:3].swapaxes(1, 2),
    )


def solution(mesh):
    whole, shard, matrix, owned = P(("expert", "wshard"), None), P("wshard"), P("wshard", None), P("expert", None, None)
    return jax.shard_map(
        on_device,
        mesh=mesh,
        in_specs=(whole, shard, matrix, matrix, matrix, matrix, shard, matrix, owned, owned, owned, whole, whole),
        out_specs=(whole, whole, shard, matrix, matrix, matrix, matrix, shard, matrix, owned, owned, owned),
        check_vma=False,
    )
```

```python
import functools
import jax
import jax.numpy as jnp
import numpy as np
from jax import lax
from jax.experimental import pallas as pl
from jax.experimental.pallas import tpu as pltpu
from jax.sharding import PartitionSpec as P

QUERY_HEADS = 16
KEY_VALUE_HEADS = 8
HEAD_WIDTH = 64
SEQUENCE_LENGTH = 1024
BLOCK = 256
TILE = 256
LANES = 128
F32 = jnp.float32
BF16 = jnp.bfloat16
ANY = pl.BlockSpec(memory_space=pl.ANY)
VMEM = pl.BlockSpec(memory_space=pltpu.VMEM)
VMEM_BYTES = 60 * 1024 * 1024
LESS_BYTES = 30 * 1024 * 1024
EXPERT_BYTES = 26 * 1024 * 1024


def dot(a, b):
    return jnp.dot(a, b, preferred_element_type=F32)


def dot_nt(a, b):
    return lax.dot_general(a, b, (((1,), (1,)), ((), ())), preferred_element_type=F32)


def dot_tn(a, b):
    return lax.dot_general(a, b, (((0,), (0,)), ((), ())), preferred_element_type=F32)


def params(size=VMEM_BYTES):
    return pltpu.CompilerParams(vmem_limit_bytes=size)


def cost(flops, nbytes, transcendentals=0):
    return pl.CostEstimate(flops=int(flops), bytes_accessed=int(nbytes), transcendentals=int(transcendentals))


def rope_tables(rows):
    half = HEAD_WIDTH // 2
    freq = np.exp(-np.log(10000.0) * np.arange(half, dtype=np.float32) * 2.0 / HEAD_WIDTH).astype(np.float32)
    pos = (np.arange(rows) % SEQUENCE_LENGTH).astype(np.float32)
    angles = (pos[:, None] * freq[None, :]).astype(np.float32)
    cos, sin = np.cos(angles), np.sin(angles)
    return (
        np.concatenate([cos, cos, cos, cos], 1).astype(np.float32),
        np.concatenate([-sin, sin, -sin, sin], 1).astype(np.float32),
    )


def rope(u, cos, sin):
    half = HEAD_WIDTH // 2
    lane = lax.broadcasted_iota(jnp.int32, u.shape, 1)
    swapped = jnp.where(
        lane % HEAD_WIDTH < half, pltpu.roll(u, LANES - half, 1), pltpu.roll(u, half, 1)
    )
    return u * cos + swapped * sin


def row_block(width):
    return pl.BlockSpec((TILE, width), lambda i: (i, 0))


def whole_block(shape):
    return pl.BlockSpec(shape, lambda i: (0,) * len(shape))


def tied(kernel, inputs, ties):
    return lambda *refs: kernel(*refs[:inputs], *refs[inputs + len(ties) :])


def project_kernel(lane, x_ref, gain_ref, w_ref, cos_ref, sin_ref, n_ref, q_ref, k_ref, v_ref):
    x = x_ref[...].astype(F32)
    inverse = lax.rsqrt(jnp.mean(x * x, axis=-1, keepdims=True) + 1e-06)
    normed = (x * inverse * gain_ref[lane : lane + 1].astype(F32)).astype(BF16)
    n_ref[...] = normed.T
    cos, sin = cos_ref[...], sin_ref[...]
    step = 512
    for at in range(0, w_ref.shape[1], step):
        made = dot(normed, w_ref[:, at : at + step])
        for lo in range(0, step, LANES):
            u = made[:, lo : lo + LANES]
            c = at + lo
            if c < q_ref.shape[1]:
                q_ref[:, c : c + LANES] = (rope(u, cos, sin).astype(BF16) * jnp.asarray(HEAD_WIDTH**-0.5, BF16))
            elif c < q_ref.shape[1] + k_ref.shape[1]:
                c -= q_ref.shape[1]
                k_ref[:, c : c + LANES] = rope(u, cos, sin).astype(BF16)
            else:
                c -= q_ref.shape[1] + k_ref.shape[1]
                v_ref[:, c : c + LANES] = u.astype(BF16)


def project(tokens, gain, lane, weights, cos, sin):
    rows, width = tokens.shape
    qw, kw = QUERY_HEADS * HEAD_WIDTH, KEY_VALUE_HEADS * HEAD_WIDTH
    return pl.pallas_call(
        functools.partial(project_kernel, lane),
        grid=(rows // TILE,),
        in_specs=[row_block(width), whole_block(gain.shape), whole_block(weights.shape), row_block(LANES), row_block(LANES)],
        out_specs=[pl.BlockSpec((width, TILE), lambda i: (0, i)), row_block(qw), row_block(kw), row_block(kw)],
        out_shape=[jax.ShapeDtypeStruct(s, BF16) for s in ((width, rows), (rows, qw), (rows, kw), (rows, kw))],
        compiler_params=params(LESS_BYTES),
        cost_estimate=cost(2 * rows * width * (qw + 2 * kw), 12 * rows * width),
        name="project",
    )(tokens, gain, weights, cos, sin)


def attend_kernel(q_ref, k_ref, v_ref, o_ref):
    for c in range(2):
        k = k_ref[:, c * HEAD_WIDTH : (c + 1) * HEAD_WIDTH]
        v = v_ref[:, c * HEAD_WIDTH : (c + 1) * HEAD_WIDTH]
        for h in range(2):
            at = (2 * c + h) * HEAD_WIDTH
            for b in range(SEQUENCE_LENGTH // BLOCK):
                n = (b + 1) * BLOCK
                rows = slice(b * BLOCK, (b + 1) * BLOCK)
                s = dot_nt(q_ref[rows, at : at + HEAD_WIDTH], k[:n])
                p = jnp.exp(s - jnp.max(s, axis=-1, keepdims=True))
                total = jnp.sum(p, axis=-1, keepdims=True)
                o = dot((p * (1.0 / total)).astype(BF16), v[:n])
                o_ref[rows, at : at + HEAD_WIDTH] = o.astype(BF16)


def head_block(width, sequence=SEQUENCE_LENGTH):
    return pl.BlockSpec((sequence, width), lambda s, i: (s, i))


def attend(queries, keys, vals, ties=()):
    rows = queries.shape[0]
    steps = KEY_VALUE_HEADS // 2
    flops = 2 * QUERY_HEADS * rows * SEQUENCE_LENGTH * HEAD_WIDTH * 2
    return pl.pallas_call(
        tied(attend_kernel, 3, ties),
        grid=(rows // SEQUENCE_LENGTH, steps),
        in_specs=[head_block(4 * HEAD_WIDTH), head_block(2 * HEAD_WIDTH), head_block(2 * HEAD_WIDTH)] + [ANY] * len(ties),
        out_specs=head_block(4 * HEAD_WIDTH),
        out_shape=jax.ShapeDtypeStruct(queries.shape, BF16),
        compiler_params=params(),
        cost_estimate=cost(flops * 8, 6 * rows * 1024, QUERY_HEADS * rows * 640),
        name="attend",
    )(queries, keys, vals, *ties)


def attend_back_kernel(q_ref, k_ref, v_ref, g_ref, cos_ref, sin_ref, dq_ref, dk_ref, dv_ref, dk_acc, dv_acc, dq_acc):
    dk_acc[...] = jnp.zeros_like(dk_acc)
    dv_acc[...] = jnp.zeros_like(dv_acc)
    for c in range(2):
        lanes = slice(c * HEAD_WIDTH, (c + 1) * HEAD_WIDTH)
        k, v = k_ref[:, lanes], v_ref[:, lanes]
        for h in range(2):
            at = slice((2 * c + h) * HEAD_WIDTH, (2 * c + h + 1) * HEAD_WIDTH)
            for b in range(SEQUENCE_LENGTH // BLOCK):
                n = (b + 1) * BLOCK
                rows = slice(b * BLOCK, (b + 1) * BLOCK)
                q, g = q_ref[rows, at], g_ref[rows, at]
                s = dot_nt(k[:n], q)
                dp = dot_nt(v[:n], g)
                p = jnp.exp(s - jnp.max(s, axis=0, keepdims=True))
                p = p * (1.0 / jnp.sum(p, axis=0, keepdims=True))
                ds = (p * (dp - jnp.sum(p * dp, axis=0, keepdims=True))).astype(BF16)
                dv_acc[:n, lanes] += dot(p.astype(BF16), g)
                dk_acc[:n, lanes] += dot(ds, q)
                dq_acc[rows, at] = dot_tn(ds, k[:n])
    cos, sin = cos_ref[...], -sin_ref[...]
    scale = HEAD_WIDTH**-0.5
    dq_ref[:, :LANES] = rope(dq_acc[:, :LANES] * scale, cos, sin).astype(BF16)
    dq_ref[:, LANES:] = rope(dq_acc[:, LANES:] * scale, cos, sin).astype(BF16)
    dk_ref[...] = rope(dk_acc[...], cos, sin).astype(BF16)
    dv_ref[...] = dv_acc[...].astype(BF16)


def attend_back(queries, keys, vals, grad, cos, sin, first=0, steps=KEY_VALUE_HEADS // 2, ties=()):
    rows = queries.shape[0]
    flops = 5 * QUERY_HEADS * rows * SEQUENCE_LENGTH * HEAD_WIDTH * 2 * steps // (KEY_VALUE_HEADS // 2)
    table = pl.BlockSpec((SEQUENCE_LENGTH, LANES), lambda s, i: (s, 0))

    def block(width, start):
        return pl.BlockSpec((SEQUENCE_LENGTH, width), lambda s, i: (s, i + start))

    two, four = block(2 * HEAD_WIDTH, first), block(4 * HEAD_WIDTH, first)
    out_two, out_four = block(2 * HEAD_WIDTH, 0), block(4 * HEAD_WIDTH, 0)
    return pl.pallas_call(
        tied(attend_back_kernel, 6, ties),
        grid=(rows // SEQUENCE_LENGTH, steps),
        in_specs=[four, two, two, four, table, table] + [ANY] * len(ties),
        out_specs=[out_four, out_two, out_two],
        out_shape=[jax.ShapeDtypeStruct((rows, steps * w), BF16) for w in (4 * HEAD_WIDTH, 2 * HEAD_WIDTH, 2 * HEAD_WIDTH)],
        scratch_shapes=[
            pltpu.VMEM((SEQUENCE_LENGTH, LANES), F32),
            pltpu.VMEM((SEQUENCE_LENGTH, LANES), F32),
            pltpu.VMEM((SEQUENCE_LENGTH, 2 * LANES), F32),
        ],
        compiler_params=params(),
        cost_estimate=cost(flops * 8, 12 * rows * 1024, QUERY_HEADS * rows * 640),
        name="attend_back",
    )(queries, keys, vals, grad, cos, sin, *ties)


def middle_kernel(lane_of, a_ref, w_ref, x_ref, gain_ref, router_ref, routes_ref, r_ref, m_ref, mt_ref, gates_ref):
    resid = x_ref[...].astype(F32) + dot(a_ref[...], w_ref[...])
    r_ref[...] = resid
    inverse = lax.rsqrt(jnp.mean(resid * resid, axis=-1, keepdims=True) + 1e-06)
    moe_in = (resid * inverse * gain_ref[lane_of : lane_of + 1].astype(F32)).astype(BF16)
    m_ref[...] = moe_in
    mt_ref[...] = moe_in.T
    logits = dot(moe_in, router_ref[...])
    lane = lax.broadcasted_iota(jnp.int32, logits.shape, 1)
    routes = routes_ref[...]
    picked = lane == routes[:, 0:1]
    for k in range(1, routes.shape[1]):
        picked = jnp.logical_or(picked, lane == routes[:, k : k + 1])
    logits = jnp.where(picked, logits, -1e30)
    weights = jnp.where(picked, jnp.exp(logits - jnp.max(logits, axis=-1, keepdims=True)), 0.0)
    gates_ref[...] = weights / jnp.sum(weights, axis=-1, keepdims=True)


def middle(attended, out_w, tokens, gain, lane, router_w, routes, ties=()):
    rows, width = tokens.shape
    return pl.pallas_call(
        tied(functools.partial(middle_kernel, lane), 6, ties),
        grid=(rows // TILE,),
        in_specs=[
            row_block(width),
            whole_block(out_w.shape),
            row_block(width),
            whole_block(gain.shape),
            whole_block(router_w.shape),
            row_block(routes.shape[1]),
        ]
        + [ANY] * len(ties),
        out_specs=[row_block(width), row_block(width), pl.BlockSpec((width, TILE), lambda i: (0, i)), row_block(LANES)],
        out_shape=[
            jax.ShapeDtypeStruct((rows, width), F32),
            jax.ShapeDtypeStruct((rows, width), BF16),
            jax.ShapeDtypeStruct((width, rows), BF16),
            jax.ShapeDtypeStruct((rows, LANES), F32),
        ],
        compiler_params=params(LESS_BYTES),
        cost_estimate=cost(2 * rows * width * (width + LANES), 14 * rows * width),
        name="middle",
    )(attended, out_w, tokens, gain, router_w, routes, *ties)


def moe_kernel(slots, chunks, first, ties, me_ref, *refs):
    refs = list(refs)
    take = lambda count: [refs.pop(0) for _ in range(count)]
    x, xt, dy, dyt, gates_ref = take(5)
    if not first:
        take(3)
    weights = [[take(count) for count in per_slot] for per_slot in chunks]
    take(ties)
    made, dmoe, gg_ref = take(3)
    grads = [take(2) for _ in slots]
    wg, wu, wd, hg, dg, du, stage, sem_w, sem_out = take(9)
    rows, width = x.shape
    step = 512

    def load(source, target, sem):
        copy = pltpu.make_async_copy(source, target, sem)
        copy.start()
        return copy

    def load_weights(index):
        buffer = index % 2
        out = []
        for which, target in enumerate((wg, wu, wd)):
            at, copies = 0, []
            for piece, ref in enumerate(weights[index][which]):
                count = ref.shape[0]
                copies.append(load(ref, target.at[buffer, at : at + count], sem_w.at[buffer, which, piece]))
                at += count
            out.append(copies)
        return out

    pending = {0: load_weights(0)}
    if first:
        gg_ref[...] = jnp.zeros_like(gg_ref)
    stores = []
    lane = lax.broadcasted_iota(jnp.int32, (step, LANES), 1)
    for index, slot in enumerate(slots):
        buffer = index % 2
        arriving = pending.pop(index)
        if index + 1 < len(slots):
            pending[index + 1] = load_weights(index + 1)
        me = me_ref[0] ^ slot
        g_w, u_w, d_w = wg.at[buffer], wu.at[buffer], wd.at[buffer]

        def arrived(which, lo):
            if lo == 0:
                for copy in arriving[which]:
                    copy.wait()

        for lo in range(0, rows, step):
            at = slice(lo, lo + step)
            arrived(0, lo)
            gate = dot(x[at], g_w[...])
            arrived(1, lo)
            upval = dot(x[at], u_w[...])
            arrived(2, lo)
            pre = dot_nt(dy[at], d_w[...])
            column = jnp.sum(jnp.where(lane == me, gates_ref[at], 0.0), axis=1, keepdims=True)
            sigma = 1.0 / (1.0 + jnp.exp(-gate))
            silu = gate * sigma
            hidden = silu * upval
            gained = jnp.sum(hidden * pre, axis=1, keepdims=True)
            gg_ref[at] = gg_ref[at] + jnp.where(lane == me, gained, 0.0)
            weighted = (hidden * column).astype(BF16)
            dhidden = pre * column
            dgate = (dhidden * upval * (sigma + silu * (1.0 - sigma))).astype(BF16)
            dup = (dhidden * silu).astype(BF16)
            hg[at], dg[at], du[at] = weighted, dgate, dup
            fresh = dot(weighted, d_w[...])
            back = dot_nt(dgate, g_w[...]) + dot_nt(dup, u_w[...])
            if first and index == 0:
                made[at], dmoe[at] = fresh, back
            else:
                made[at] += fresh
                dmoe[at] += back
        for copy in stores:
            copy.wait()
        stores = []
        half = width // 2
        for part in range(2):
            at = slice(part * half, (part + 1) * half)
            stage[0, at] = dot(xt[at], dg[...]).astype(BF16)
            stage[1, at] = dot(xt[at], du[...]).astype(BF16)
            stage[2, at] = dot(dyt[at], hg[...]).astype(BF16)
            stores.append(load(stage.at[:, at], grads[index][part], sem_out.at[part]))
    for copy in stores:
        copy.wait()


def moe(slots, me, moe_in, moe_in_t, dy, dy_t, gates, acc, weights, ties=()):
    rows, width = moe_in.shape
    hidden = weights[0][0][0].shape[1]
    first = acc is None
    flat = [piece for per_slot in weights for pieces in per_slot for piece in pieces]
    chunks = tuple(tuple(len(pieces) for pieces in per_slot) for per_slot in weights)
    held = [pltpu.with_memory_space_constraint(a, pltpu.VMEM) for a in (moe_in, moe_in_t, dy, dy_t, gates, *(acc or ()))]
    grad = jax.ShapeDtypeStruct((3, width // 2, hidden), BF16)
    outs = pl.pallas_call(
        functools.partial(moe_kernel, tuple(slots), chunks, first, len(ties)),
        in_specs=[pl.BlockSpec(memory_space=pltpu.SMEM)] + [VMEM] * len(held) + [ANY] * (len(flat) + len(ties)),
        out_specs=[VMEM, VMEM, VMEM] + [ANY] * (2 * len(slots)),
        out_shape=[pltpu.VMEM((rows, width), F32), pltpu.VMEM((rows, width), F32), pltpu.VMEM((rows, LANES), F32)]
        + [grad] * (2 * len(slots)),
        scratch_shapes=[
            pltpu.VMEM((2, width, hidden), BF16),
            pltpu.VMEM((2, width, hidden), BF16),
            pltpu.VMEM((2, hidden, width), BF16),
            pltpu.VMEM((rows, hidden), BF16),
            pltpu.VMEM((rows, hidden), BF16),
            pltpu.VMEM((rows, hidden), BF16),
            pltpu.VMEM((3, width, hidden), BF16),
            pltpu.SemaphoreType.DMA((2, 3, 2)),
            pltpu.SemaphoreType.DMA((2,)),
        ],
        input_output_aliases={} if first else {6: 0, 7: 1, 8: 2},
        compiler_params=pltpu.CompilerParams(vmem_limit_bytes=EXPERT_BYTES),
        cost_estimate=cost(18 * rows * width * hidden * len(slots), 20 * rows * width),
        name="experts",
    )(me, *held, *flat, *ties)
    return outs[:3], [tuple(outs[3 + 2 * i : 5 + 2 * i]) for i in range(len(slots))]


def turn_kernel(
    lane, resid_ref, made_ref, dmoe_ref, gates_ref, gg_ref, dy_ref, gain_ref, router_ref, mt_ref, w_ref,
    mixed_ref, dresid_ref, dz_ref, da_ref, gain_grad_ref, router_grad_ref,
):
    @pl.when(pl.program_id(0) == 0)
    def _():
        gain_grad_ref[...] = jnp.zeros_like(gain_grad_ref)
        router_grad_ref[...] = jnp.zeros_like(router_grad_ref)

    resid = resid_ref[...]
    mixed_ref[...] = (resid + made_ref[...]).astype(BF16)
    gates, gg = gates_ref[...], gg_ref[...]
    dlogits = (gates * (gg - jnp.sum(gates * gg, axis=1, keepdims=True))).astype(BF16)
    router_grad_ref[...] += dot(mt_ref[...], dlogits)
    dmoe = dmoe_ref[...] + dot_nt(dlogits, router_ref[...])
    inverse = lax.rsqrt(jnp.mean(resid * resid, axis=-1, keepdims=True) + 1e-06)
    gain_grad_ref[...] += jnp.sum(dmoe * resid * inverse, axis=0, keepdims=True)
    scaled = dmoe * gain_ref[lane : lane + 1].astype(F32)
    inner = jnp.mean(scaled * resid, axis=-1, keepdims=True)
    dresid = dy_ref[...].astype(F32) + inverse * scaled - resid * (inverse * inverse * inverse * inner)
    dresid_ref[...] = dresid
    dz = dresid.astype(BF16)
    dz_ref[...] = dz
    da_ref[...] = dot_nt(dz, w_ref[...]).astype(BF16)


def turn(resid, made, dmoe, gates, gg, dy, gain, lane, router_w, moe_in_t, out_w, ties=()):
    rows, width = resid.shape
    return pl.pallas_call(
        tied(functools.partial(turn_kernel, lane), 10, ties),
        grid=(rows // TILE,),
        in_specs=[
            row_block(width), row_block(width), row_block(width), row_block(LANES), row_block(LANES), row_block(width),
            whole_block(gain.shape), whole_block(router_w.shape), pl.BlockSpec((width, TILE), lambda i: (0, i)),
            whole_block(out_w.shape),
        ]
        + [ANY] * len(ties),
        out_specs=[row_block(width)] * 4 + [whole_block((1, width)), whole_block((width, LANES))],
        out_shape=[
            jax.ShapeDtypeStruct((rows, width), BF16),
            jax.ShapeDtypeStruct((rows, width), F32),
            jax.ShapeDtypeStruct((rows, width), BF16),
            jax.ShapeDtypeStruct((rows, width), BF16),
            jax.ShapeDtypeStruct((1, width), F32),
            jax.ShapeDtypeStruct((width, LANES), F32),
        ],
        compiler_params=params(LESS_BYTES),
        cost_estimate=cost(2 * rows * width * (width + 2 * LANES), 28 * rows * width),
        name="turn",
    )(resid, made, dmoe, gates, gg, dy, gain, router_w, moe_in_t, out_w, *ties)


def finish_kernel(lane, count, *refs):
    grads = refs[:count]
    w_ref, x_ref, dresid_ref, gain_ref, router_ref, second_ref, out_ref, small_ref, first = refs[count:]

    @pl.when(pl.program_id(0) == 0)
    def _():
        first[...] = jnp.zeros_like(first)

    at, dn = 0, 0.0
    for ref in grads:
        dn += dot_nt(ref[...], w_ref[:, at : at + ref.shape[1]])
        at += ref.shape[1]
    x = x_ref[...].astype(F32)
    inverse = lax.rsqrt(jnp.mean(x * x, axis=-1, keepdims=True) + 1e-06)
    first[...] += jnp.sum(dn * x * inverse, axis=0, keepdims=True)
    scaled = dn * gain_ref[lane : lane + 1].astype(F32)
    inner = jnp.mean(scaled * x, axis=-1, keepdims=True)
    out_ref[...] = dresid_ref[...] + inverse * scaled - x * (inverse * inverse * inverse * inner)

    @pl.when(pl.program_id(0) == pl.num_programs(0) - 1)
    def _():
        row = lax.broadcasted_iota(jnp.int32, (LANES, first.shape[1]), 0)
        gains = jnp.where(row == lane, first[...], 0.0) + jnp.where(row == lane + 1, second_ref[...], 0.0)
        small_ref[...] = (router_ref[...] + gains.T).astype(BF16)


def finish(grads, weights, tokens, dresid, gain, lane, router_grad, second, ties=()):
    rows, width = tokens.shape
    return pl.pallas_call(
        tied(functools.partial(finish_kernel, lane, len(grads)), len(grads) + 6, ties),
        grid=(rows // TILE,),
        in_specs=[row_block(g.shape[1]) for g in grads]
        + [whole_block(weights.shape), row_block(width), row_block(width), whole_block(gain.shape)]
        + [whole_block(router_grad.shape), whole_block(second.shape)]
        + [ANY] * len(ties),
        out_specs=[row_block(width), whole_block((width, LANES))],
        out_shape=[jax.ShapeDtypeStruct((rows, width), F32), jax.ShapeDtypeStruct((width, LANES), BF16)],
        scratch_shapes=[pltpu.VMEM((1, width), F32)],
        compiler_params=params(),
        cost_estimate=cost(1, 1),
        name="finish",
    )(*grads, weights, tokens, dresid, gain, router_grad, second, *ties)


def weights_back_kernel(count, *refs):
    for grad, out in zip(refs[1 : count + 1], refs[count + 1 :]):
        out[...] = dot(refs[0][...], grad[...]).astype(BF16)


def weights_back(turned, grads, ties=()):
    rows = turned.shape[0]
    return pl.pallas_call(
        tied(functools.partial(weights_back_kernel, len(grads)), len(grads) + 1, ties),
        grid=(rows // TILE,),
        in_specs=[row_block(turned.shape[1])] + [whole_block(g.shape) for g in grads] + [ANY] * len(ties),
        out_specs=[row_block(g.shape[1]) for g in grads],
        out_shape=[jax.ShapeDtypeStruct((rows, g.shape[1]), BF16) for g in grads],
        compiler_params=params(),
        cost_estimate=cost(1, 1),
        name="weights_back",
    )(turned, *grads, *ties)


def widen_kernel(top_ref, bottom_ref, gate_ref, up_ref, down_ref):
    step = pl.program_id(0)
    for half, ref in enumerate((top_ref, bottom_ref)):

        @pl.when(step // 2 == half)
        def _():
            gate_ref[...] = ref[0].astype(F32)
            up_ref[...] = ref[1].astype(F32)
            down_ref[...] = ref[2].astype(F32).T


def widen(top, bottom):
    _, rows, columns = top.shape
    step = rows // 2
    block = pl.BlockSpec((step, columns), lambda i: (i, 0))
    return pl.pallas_call(
        widen_kernel,
        grid=(4,),
        in_specs=[
            pl.BlockSpec((3, step, columns), lambda i: (0, jnp.minimum(i, 1), 0)),
            pl.BlockSpec((3, step, columns), lambda i: (0, jnp.maximum(i - 2, 0), 0)),
        ],
        out_specs=[block, block, pl.BlockSpec((columns, step), lambda i: (0, i))],
        out_shape=[
            jax.ShapeDtypeStruct((2 * rows, columns), F32),
            jax.ShapeDtypeStruct((2 * rows, columns), F32),
            jax.ShapeDtypeStruct((columns, 2 * rows), F32),
        ],
        compiler_params=params(),
        cost_estimate=cost(1, 1),
        name="widen",
    )(top, bottom)


def plus_kernel(counts, *refs):
    refs = list(refs)
    refs.pop()[...] = jnp.zeros((8, LANES), F32)
    ins = [[refs.pop(0) for _ in range(count)] for count in counts]
    for terms, out in zip(ins, refs):
        total = terms[0][...].astype(F32)
        for ref in terms[1:]:
            total += ref[...].astype(F32)
        out[...] = total.astype(BF16)


def plus(*groups, ties=()):
    shape = groups[0][0].shape
    block = pl.BlockSpec((1, shape[1] // 2, shape[2]), lambda i, j: (i, j, 0))
    counts = tuple(len(terms) for terms in groups)
    flat = [a for terms in groups for a in terms]
    return pl.pallas_call(
        tied(functools.partial(plus_kernel, counts), len(flat), ties),
        grid=(shape[0], 2),
        in_specs=[block] * len(flat) + [ANY] * len(ties),
        out_specs=[block] * len(groups) + [pl.BlockSpec((8, LANES), lambda i, j: (0, 0))],
        out_shape=[jax.ShapeDtypeStruct(shape, BF16)] * len(groups) + [jax.ShapeDtypeStruct((8, LANES), F32)],
        compiler_params=pltpu.CompilerParams(vmem_limit_bytes=16 * 1024 * 1024),
        cost_estimate=cost(len(flat) * flat[0].size, 2 * (len(flat) + len(groups)) * flat[0].size),
        name="plus",
    )(*flat, *ties)


def gather_kernel(size, count, *refs):
    q_ref, k_ref, v_ref, s_ref, o_ref = refs[:5]
    owned, refs = refs[5 : 5 + count], refs[5 + count :]
    packed_ref, small_ref, out_ref, turned_ref = refs[:4]
    beside, refs = refs[4 : 4 + 2 * count], refs[4 + 2 * count :]
    send_sem, recv_sem, pass_sem, take_sem, away_sem, come_sem = refs
    me, z = lax.axis_index("expert"), lax.axis_index("wshard")
    core = lax.rem(me, 2)
    sibling = me + 1 - 2 * core
    rows = q_ref.shape[0]
    half = rows // 2
    there = lambda step: jnp.logical_and(z + step >= 0, z + step < size)

    barrier = pltpu.get_barrier_semaphore()
    pl.semaphore_signal(barrier, inc=1, device_id=(sibling, z), device_id_type=pl.DeviceIdType.MESH)
    for step in (1, -1):

        @pl.when(there(step))
        def _():
            pl.semaphore_signal(barrier, inc=1, device_id=(me, z + step), device_id_type=pl.DeviceIdType.MESH)

    neighbours = []
    if count:
        xb, yb = lax.rem(me // 2, 2), me // 4
        neighbours = [me + 2 - 4 * xb, me + 4 - 8 * yb]
    for peer in neighbours:
        pl.semaphore_signal(barrier, inc=1, device_id=(peer, z), device_id_type=pl.DeviceIdType.MESH)
    pl.semaphore_wait(barrier, 1 + len(neighbours) + jnp.where(z > 0, 1, 0) + jnp.where(z < size - 1, 1, 0))
    shipped = []
    for i, ref in enumerate(owned):
        for j, peer in enumerate(neighbours):
            shipped.append(
                pltpu.make_async_remote_copy(
                    src_ref=ref, dst_ref=beside[j * count + i], send_sem=away_sem.at[i, j], recv_sem=come_sem.at[i, j],
                    device_id=(peer, z), device_id_type=pl.DeviceIdType.MESH,
                )
            )
    for copy in shipped:
        copy.start()

    own = pl.ds(pl.multiple_of(z * rows, rows), rows)
    at = 0
    for ref in (q_ref, k_ref, v_ref):
        packed_ref[own, at : at + ref.shape[1]] = ref[...]
        at += ref.shape[1]
    small_ref[own] = s_ref[...]

    def moves(way, hop, origin, which, device, send, recv):
        at = pl.ds(pl.multiple_of(origin * rows + which * half, half), half)
        return [
            pltpu.make_async_remote_copy(
                src_ref=ref.at[at], dst_ref=ref.at[at], send_sem=send.at[way, hop, i], recv_sem=recv.at[way, hop, i],
                device_id=device, device_id_type=pl.DeviceIdType.MESH,
            )
            for i, ref in enumerate((packed_ref, small_ref))
        ]

    def onward(way, step, hop):
        return moves(way, hop, z - step * (hop - 1), core, (me, z + step), send_sem, recv_sem)

    def across(way, step, hop, which):
        return moves(way, hop, z - step * hop, which, (sibling, z), pass_sem, take_sem)

    ways = ((0, 1), (1, -1))
    for way, step in ways:

        @pl.when(there(step))
        def _():
            for move in onward(way, step, 1):
                move.start()

    for hop in range(1, size):
        for way, step in ways:

            @pl.when(there(-step * hop))
            def _():
                for move in moves(way, hop, z - step * hop, core, (me, z), send_sem, recv_sem):
                    move.wait_recv()

                @pl.when(there(step))
                def _():
                    for move in onward(way, step, hop + 1):
                        move.start()

                for move in across(way, step, hop, core):
                    move.start()

    for hop in range(1, size):
        for way, step in ways:

            @pl.when(there(-step * hop))
            def _():
                for move in across(way, step, hop, 1 - core):
                    move.wait_recv()
                for move in across(way, step, hop, core):
                    move.wait_send()

            @pl.when(jnp.logical_and(there(step), there(-step * (hop - 1))))
            def _():
                for move in onward(way, step, hop):
                    move.wait_send()

    out_ref[...] = o_ref[...]
    turned_ref[...] = small_ref[...].T
    for copy in shipped:
        copy.wait()


def gather_weights(query, key, value, small, out, owned=()):
    size = lax.axis_size("wshard")
    rows = query.shape[0]
    width = query.shape[1] + key.shape[1] + value.shape[1]
    sems = pltpu.SemaphoreType.DMA((2, size + 1, 2))
    return pl.pallas_call(
        functools.partial(gather_kernel, size, len(owned)),
        in_specs=[VMEM] * 5 + [ANY] * len(owned),
        out_specs=[VMEM] * 4 + [ANY] * (2 * len(owned)),
        out_shape=[
            jax.ShapeDtypeStruct((size * rows, width), BF16),
            jax.ShapeDtypeStruct((size * rows, small.shape[1]), BF16),
            jax.ShapeDtypeStruct(out.shape, BF16),
            jax.ShapeDtypeStruct((small.shape[1], size * rows), BF16),
        ]
        + [jax.ShapeDtypeStruct(a.shape, BF16) for a in owned] * 2,
        scratch_shapes=[sems, sems, sems, sems] + [pltpu.SemaphoreType.DMA((max(len(owned), 1), 2))] * 2,
        compiler_params=pltpu.CompilerParams(collective_id=0, has_side_effects=True, vmem_limit_bytes=VMEM_BYTES),
        cost_estimate=cost(1e9, 12 * rows * size * width),
        name="gather_weights",
    )(query, key, value, small, out, *owned)


def reduce_kernel(size, columns, *refs):
    count = sum(len(widths) for widths in columns)
    ins, outs = list(refs[:count]), refs[count : count + len(columns)]
    acc, rc, r1, r2, zs, rz, res, send_sem, recv_sem = refs[count + len(columns) :]
    me, z = lax.axis_index("expert"), lax.axis_index("wshard")
    core, xb, yb = lax.rem(me, 2), lax.rem(me // 2, 2), me // 4
    sibling, xp, yp = me + 1 - 2 * core, me + 2 - 4 * xb, me + 4 - 8 * yb
    half = ins[0].shape[1] // 2
    n1, n2 = half // 4, half // 8

    barrier = pltpu.get_barrier_semaphore()
    for peer in (sibling, xp, yp):
        pl.semaphore_signal(barrier, inc=1, device_id=(peer, z), device_id_type=pl.DeviceIdType.MESH)
    for d in range(1, size):
        pl.semaphore_signal(barrier, inc=1, device_id=(me, lax.rem(z + d, size)), device_id_type=pl.DeviceIdType.MESH)
    pl.semaphore_wait(barrier, 2 + size)

    pieces, at = [], 0
    for out, widths in zip(outs, columns):
        start = 0
        for width in widths:
            ref, step = ins.pop(0), min(width, 512)
            for lo in range(0, width, step):
                pieces.append((ref, out, lo, step, at, start + lo))
                at += step
            start += width

    sent = []

    def move(source, target, piece, kind, device):
        copy = pltpu.make_async_remote_copy(
            src_ref=source, dst_ref=target, send_sem=send_sem.at[kind, piece], recv_sem=recv_sem.at[kind, piece],
            device_id=device, device_id_type=pl.DeviceIdType.MESH,
        )
        copy.start()
        sent.append(copy)
        return copy

    def rows(start, length):
        return pl.ds(pl.multiple_of(start, 16), length)

    def sum_of(*terms):
        total = terms[0].astype(F32)
        for term in terms[1:]:
            total += term.astype(F32)
        return total

    k0, k1 = xb * n1 + yb * n2, half // 2 + yb * n1 + xb * n2
    base = core * half
    first = []
    for p, (ref, _, lo, w, at, _) in enumerate(pieces):
        first.append(move(ref.at[:, rows((1 - core) * half, half), lo : lo + w], rc.at[:, :, at : at + w], p, 0, (sibling, z)))
    second = []
    for p, (ref, _, lo, w, at, _) in enumerate(pieces):
        c = slice(at, at + w)
        first[p].wait_recv()
        acc[:, :, c] = sum_of(ref[:, rows(base, half), lo : lo + w], rc[:, :, c]).astype(BF16)
        second.append((
            move(acc.at[:, rows((1 - xb) * n1, n1), c], r1.at[0, :, :, c], p, 1, (xp, z)),
            move(acc.at[:, rows(half // 2 + (1 - yb) * n1, n1), c], r1.at[1, :, :, c], p, 2, (yp, z)),
        ))
    third = []
    for p, (_, _, _, w, at, _) in enumerate(pieces):
        c = slice(at, at + w)
        keep = (rows(xb * n1, n1), rows(half // 2 + yb * n1, n1))
        for i in range(2):
            second[p][i].wait_recv()
            acc[:, keep[i], c] = sum_of(acc[:, keep[i], c], r1[i, :, :, c]).astype(BF16)
        third.append((
            move(acc.at[:, rows(xb * n1 + (1 - yb) * n2, n2), c], r2.at[0, :, :, c], p, 3, (yp, z)),
            move(acc.at[:, rows(half // 2 + yb * n1 + (1 - xb) * n2, n2), c], r2.at[1, :, :, c], p, 4, (xp, z)),
        ))
    fourth = []
    for p, (_, _, _, w, at, _) in enumerate(pieces):
        c = slice(at, at + w)
        for i, k in enumerate((k0, k1)):
            third[p][i].wait_recv()
            zs[:, i * n2 : (i + 1) * n2, c] = sum_of(acc[:, rows(k, n2), c], r2[i, :, :, c]).astype(BF16)
        fourth.append([
            move(zs.at[lax.rem(z + d, size), :, c], rz.at[d - 1, :, c], p, 8 + d, (me, lax.rem(z + d, size)))
            for d in range(1, size)
        ])
    fifth = []
    for p, (_, _, _, w, at, _) in enumerate(pieces):
        c = slice(at, at + w)
        for copy in fourth[p]:
            copy.wait_recv()
        total = sum_of(zs[z, :, c], *[rz[d, :, c] for d in range(size - 1)]).astype(BF16)
        for i, k in enumerate((k0, k1)):
            res[rows(base + k, n2), c] = total[i * n2 : (i + 1) * n2]
        fifth.append((
            move(res.at[rows(base + k0, n2), c], res.at[rows(base + k0, n2), c], p, 5, (yp, z)),
            move(res.at[rows(base + k1, n2), c], res.at[rows(base + k1, n2), c], p, 6, (xp, z)),
        ))
    sixth = []
    for p, (_, _, _, w, at, _) in enumerate(pieces):
        c = slice(at, at + w)
        for copy in fifth[p]:
            copy.wait_recv()
        mine = rows(base + xb * n1, n1), rows(base + half // 2 + yb * n1, n1)
        sixth.append((
            move(res.at[mine[0], c], res.at[mine[0], c], p, 7, (xp, z)),
            move(res.at[mine[1], c], res.at[mine[1], c], p, 8, (yp, z)),
        ))
    last = []
    for p, (_, _, _, w, at, _) in enumerate(pieces):
        c = slice(at, at + w)
        for copy in sixth[p]:
            copy.wait_recv()
        last.append(move(res.at[rows(base, half), c], res.at[rows(base, half), c], p, 8 + size, (sibling, z)))
    for p, (_, out, _, w, at, to) in enumerate(pieces):
        last[p].wait_recv()
        out[:, to : to + w] = res[:, at : at + w].astype(F32)
    for copy in sent:
        copy.wait_send()


def reduce_all(*groups):
    size = lax.axis_size("wshard")
    rows = groups[0][0].shape[0] // size
    grads = [g for group in groups for g in group]
    columns = tuple(tuple(g.shape[1] for g in group) for group in groups)
    count = sum(-(-g.shape[1] // 512) for g in grads)
    width, half = sum(g.shape[1] for g in grads), rows // 2
    return pl.pallas_call(
        functools.partial(reduce_kernel, size, columns),
        in_specs=[VMEM] * len(grads),
        out_specs=[VMEM] * len(groups),
        out_shape=[jax.ShapeDtypeStruct((rows, sum(widths)), F32) for widths in columns],
        scratch_shapes=[
            pltpu.VMEM((size, half, width), BF16),
            pltpu.VMEM((size, half, width), BF16),
            pltpu.VMEM((2, size, half // 4, width), BF16),
            pltpu.VMEM((2, size, half // 8, width), BF16),
            pltpu.VMEM((size, half // 4, width), BF16),
            pltpu.VMEM((size - 1, half // 4, width), BF16),
            pltpu.VMEM((rows, width), BF16),
            pltpu.SemaphoreType.DMA((9 + size, count)),
            pltpu.SemaphoreType.DMA((9 + size, count)),
        ],
        compiler_params=pltpu.CompilerParams(collective_id=1, has_side_effects=True, vmem_limit_bytes=VMEM_BYTES),
        cost_estimate=cost(1, 1),
        name="reduce_all",
    )(*[g.reshape(size, rows, g.shape[1]) for g in grads])


def flip(value, axis, bit):
    size = lax.axis_size(axis)
    return lax.ppermute(value, axis, [(i, i ^ bit) for i in range(size)])


def gather_experts(mats, owners):
    slots, bit = {0: tuple([m] for m in mats)}, 2
    while bit < owners:
        for j in sorted(slots):
            slots[j | bit] = tuple([flip(p, "expert", bit) for p in m] for m in slots[j])
        bit *= 2
    return slots


def third_slot(a, b):
    cut = a[2][0].shape[0] // 2
    return (
        [flip(a[0][0], "expert", 4)],
        [flip(b[1][0], "expert", 2)],
        [flip(a[2][0][:cut], "expert", 4), flip(b[2][0][cut:], "expert", 2)],
    )


def across_core(slot):
    return tuple([flip(p, "expert", 1) for p in m] for m in slot)


def add(a, b):
    return (a.astype(F32) + b.astype(F32)).astype(BF16)


def reduce_experts(parts, owners):
    bit = 1
    while bit < owners:
        for j in sorted(parts, reverse=True):
            if j & bit:
                gone = parts.pop(j)
                parts[j ^ bit] = tuple(add(m, flip(s, "expert", bit)) for m, s in zip(parts[j ^ bit], gone))
        bit *= 2
    return parts[0]


def on_device(
    tokens, gain_attn, w_query, key_weight, value_weight, w_out, gain_ffn, w_router, w_gate, w_up, w_down, routes, cotangent
):
    owners = lax.axis_size("expert")
    me = lax.axis_index("expert").astype(jnp.int32)[None]
    rows, width = tokens.shape
    experts = w_router.shape[1]
    mats = (w_gate[0], w_up[0], w_down[0])

    small = jnp.concatenate([w_router, gain_attn[:, None], gain_ffn[:, None]], axis=1)
    small = jnp.pad(small, ((0, 0), (0, LANES - small.shape[1])))
    packed, small, out_shard, gains, *beside = gather_weights(
        w_query, key_weight, value_weight, small, w_out, mats[:2] if owners == 8 else ()
    )
    out_w = lax.all_gather(out_shard, "wshard", axis=0, tiled=True)
    cos, sin = (jnp.asarray(a) for a in rope_tables(rows))

    if owners == 8:
        slots = {0: tuple([m] for m in mats)}
        slots[2] = ([beside[0]], [beside[1]], [flip(mats[2], "expert", 2)])
        slots[4] = ([beside[2]], [beside[3]], [flip(mats[2], "expert", 4)])
        slots[6] = third_slot(slots[2], slots[4])
    else:
        slots = gather_experts(mats, owners)
    normed_t, queries, keys, vals = project(tokens, gains, experts, packed, cos, sin)
    def pieces_of(*which):
        return [p for j in which for m in slots[j] for p in m] if owners == 8 else []

    attended = attend(queries, keys, vals)
    for j in sorted(slots):
        slots[j | 1] = across_core(slots[j])
    resid, moe_in, moe_in_t, gates = middle(
        attended, out_w, tokens, gains, experts + 1, small, routes, pieces_of(2, 4, 3, 5, 1)
    )
    dy_t = cotangent.T

    def one(j, acc, ties=()):
        acc, (halves,) = moe([j], me, moe_in, moe_in_t, cotangent, dy_t, gates, acc, [slots[j]], ties)
        return acc, halves

    def turned(acc, ties=()):
        made, dmoe, gate_grads = acc
        return turn(
            resid, made, dmoe, gates, gate_grads, cotangent, gains, experts + 1, small, moe_in_t, out_w, ties
        )

    if owners == 8:
        core = lambda halves: [flip(m, "expert", 1) for m in halves]
        over_x = lambda m: flip(m, "expert", 2)
        over_y = lambda m: flip(m, "expert", 4)
        acc, g3 = one(3, None, pieces_of(6))
        c3 = core(g3)
        acc, g2 = one(2, acc, pieces_of(7))
        *s2, t2 = plus((g2[0], c3[0]), (g2[1], c3[1]))
        x20 = over_x(s2[0])
        acc, g7 = one(7, acc, [t2])
        c7 = core(g7)
        acc, g6 = one(6, acc)
        *s6, t6 = plus((g6[0], c7[0]), (g6[1], c7[1]))
        x60, y61 = over_x(s6[0]), over_y(s6[1])
        acc, g5 = one(5, acc, [t6])
        c5 = core(g5)
        acc, g4 = one(4, acc, [x20])
        *s4, t4 = plus((g4[0], c5[0]), (g4[1], c5[1]))
        y41 = over_y(s4[1])
        acc, g1 = one(1, acc, [t4])
        c1 = core(g1)
        left, right, sides = plus((s4[0], x60), (s2[1], y61))
        x21, y40 = over_x(right), over_y(left)
        acc, g0 = one(0, acc, [sides])
        *s0, t0 = plus((g0[0], c1[0]), (g0[1], c1[1]))
        mixed, dresid, dz, dattended, gain_two_grad, router_grad = turned(acc, [t0])
        out_grad = dot_tn(attended, dz).astype(BF16)
        early = attend_back(queries, keys, vals, dattended, cos, sin, 0, 2, [out_grad])
        top, bottom, both = plus((s0[0], x20, y40), (s0[1], y41, x21), ties=early[2:])
        late = attend_back(queries, keys, vals, dattended, cos, sin, 2, 2, [both])
        top, bottom = lax.psum((top, bottom), "wshard")
        pieces = [early[0], late[0], early[1], late[1], early[2], late[2]]
        weight_grads = weights_back(normed_t, pieces)
        own, after = [top, bottom], []
    else:
        acc, parts = None, {}
        for j in range(owners):
            acc, parts[j] = one(j, acc)
        mixed, dresid, dz, dattended, gain_two_grad, router_grad = turned(acc)
        own, after = lax.psum(tuple(reduce_experts(parts, owners)), "wshard"), []
        out_grad = dot_tn(attended, dz).astype(BF16)
        pieces = attend_back(queries, keys, vals, dattended, cos, sin)
        weight_grads = weights_back(normed_t, pieces)
    d_tokens, small_grad = finish(pieces, packed, tokens, dresid, gains, experts, router_grad, gain_two_grad, after)
    third = len(weight_grads) // 3
    groups = [[out_grad]] + [weight_grads[i : i + third] for i in range(0, 3 * third, third)] + [[small_grad]]
    if owners == 8:
        sums = reduce_all(*groups)
    else:
        total = lambda g: lax.psum(lax.psum_scatter(g, "wshard", scatter_dimension=0, tiled=True), "expert")
        sums = [total(jnp.concatenate(group, axis=1)).astype(F32) for group in groups]
    out_grad, query_grad, key_grad, value_grad, small_grad = sums
    gate_grad, up_grad, down_grad = widen(*own)
    return (
        mixed,
        d_tokens,
        small_grad[:, experts],
        query_grad,
        key_grad,
        value_grad,
        out_grad,
        small_grad[:, experts + 1],
        small_grad[:, :experts],
        gate_grad[None],
        up_grad[None],
        down_grad[None],
    )


def solution(mesh):
    whole, shard, matrix, owned = P(("expert", "wshard"), None), P("wshard"), P("wshard", None), P("expert", None, None)
    return jax.shard_map(
        on_device,
        mesh=mesh,
        in_specs=(whole, shard, matrix, matrix, matrix, matrix, shard, matrix, owned, owned, owned, whole, whole),
        out_specs=(whole, whole, shard, matrix, matrix, matrix, matrix, shard, matrix, owned, owned, owned),
        check_vma=False,
    )
```

```python
import functools
import jax
import jax.numpy as jnp
import numpy as np
from jax import lax
from jax.experimental import pallas as pl
from jax.experimental.pallas import tpu as pltpu
from jax.sharding import PartitionSpec as P

QUERY_HEADS = 16
KEY_VALUE_HEADS = 8
HEAD_WIDTH = 64
SEQUENCE_LENGTH = 1024
BLOCK = 256
TILE = 256
LANES = 128
F32 = jnp.float32
BF16 = jnp.bfloat16
ANY = pl.BlockSpec(memory_space=pl.ANY)
VMEM = pl.BlockSpec(memory_space=pltpu.VMEM)
VMEM_BYTES = 60 * 1024 * 1024
LESS_BYTES = 30 * 1024 * 1024
EXPERT_BYTES = 26 * 1024 * 1024


def dot(a, b):
    return jnp.dot(a, b, preferred_element_type=F32)


def dot_nt(a, b):
    return lax.dot_general(a, b, (((1,), (1,)), ((), ())), preferred_element_type=F32)


def dot_tn(a, b):
    return lax.dot_general(a, b, (((0,), (0,)), ((), ())), preferred_element_type=F32)


def params(size=VMEM_BYTES):
    return pltpu.CompilerParams(vmem_limit_bytes=size)


def cost(flops, nbytes, transcendentals=0):
    return pl.CostEstimate(flops=int(flops), bytes_accessed=int(nbytes), transcendentals=int(transcendentals))


def rope_tables(rows):
    half = HEAD_WIDTH // 2
    freq = np.exp(-np.log(10000.0) * np.arange(half, dtype=np.float32) * 2.0 / HEAD_WIDTH).astype(np.float32)
    pos = (np.arange(rows) % SEQUENCE_LENGTH).astype(np.float32)
    angles = (pos[:, None] * freq[None, :]).astype(np.float32)
    cos, sin = np.cos(angles), np.sin(angles)
    return (
        np.concatenate([cos, cos, cos, cos], 1).astype(np.float32),
        np.concatenate([-sin, sin, -sin, sin], 1).astype(np.float32),
    )


def rope(u, cos, sin):
    half = HEAD_WIDTH // 2
    lane = lax.broadcasted_iota(jnp.int32, u.shape, 1)
    swapped = jnp.where(
        lane % HEAD_WIDTH < half, pltpu.roll(u, LANES - half, 1), pltpu.roll(u, half, 1)
    )
    return u * cos + swapped * sin


def row_block(width):
    return pl.BlockSpec((TILE, width), lambda i: (i, 0))


def whole_block(shape):
    return pl.BlockSpec(shape, lambda i: (0,) * len(shape))


def tied(kernel, inputs, ties):
    return lambda *refs: kernel(*refs[:inputs], *refs[inputs + len(ties) :])


def project_kernel(lane, x_ref, gain_ref, w_ref, cos_ref, sin_ref, n_ref, q_ref, k_ref, v_ref):
    x = x_ref[...].astype(F32)
    inverse = lax.rsqrt(jnp.mean(x * x, axis=-1, keepdims=True) + 1e-06)
    normed = (x * inverse * gain_ref[lane : lane + 1].astype(F32)).astype(BF16)
    n_ref[...] = normed.T
    cos, sin = cos_ref[...], sin_ref[...]
    step = 512
    for at in range(0, w_ref.shape[1], step):
        made = dot(normed, w_ref[:, at : at + step])
        for lo in range(0, step, LANES):
            u = made[:, lo : lo + LANES]
            c = at + lo
            if c < q_ref.shape[1]:
                q_ref[:, c : c + LANES] = (rope(u, cos, sin).astype(BF16) * jnp.asarray(HEAD_WIDTH**-0.5, BF16))
            elif c < q_ref.shape[1] + k_ref.shape[1]:
                c -= q_ref.shape[1]
                k_ref[:, c : c + LANES] = rope(u, cos, sin).astype(BF16)
            else:
                c -= q_ref.shape[1] + k_ref.shape[1]
                v_ref[:, c : c + LANES] = u.astype(BF16)


def project(tokens, gain, lane, weights, cos, sin):
    rows, width = tokens.shape
    qw, kw = QUERY_HEADS * HEAD_WIDTH, KEY_VALUE_HEADS * HEAD_WIDTH
    return pl.pallas_call(
        functools.partial(project_kernel, lane),
        grid=(rows // TILE,),
        in_specs=[row_block(width), whole_block(gain.shape), whole_block(weights.shape), row_block(LANES), row_block(LANES)],
        out_specs=[pl.BlockSpec((width, TILE), lambda i: (0, i)), row_block(qw), row_block(kw), row_block(kw)],
        out_shape=[jax.ShapeDtypeStruct(s, BF16) for s in ((width, rows), (rows, qw), (rows, kw), (rows, kw))],
        compiler_params=params(),
        cost_estimate=cost(2 * rows * width * (qw + 2 * kw), 12 * rows * width),
        name="project",
    )(tokens, gain, weights, cos, sin)


def attend_kernel(q_ref, k_ref, v_ref, o_ref):
    for c in range(2):
        k = k_ref[:, c * HEAD_WIDTH : (c + 1) * HEAD_WIDTH]
        v = v_ref[:, c * HEAD_WIDTH : (c + 1) * HEAD_WIDTH]
        for h in range(2):
            at = (2 * c + h) * HEAD_WIDTH
            for b in range(SEQUENCE_LENGTH // BLOCK):
                n = (b + 1) * BLOCK
                rows = slice(b * BLOCK, (b + 1) * BLOCK)
                s = dot_nt(q_ref[rows, at : at + HEAD_WIDTH], k[:n])
                p = jnp.exp(s - jnp.max(s, axis=-1, keepdims=True))
                total = jnp.sum(p, axis=-1, keepdims=True)
                o = dot((p * (1.0 / total)).astype(BF16), v[:n])
                o_ref[rows, at : at + HEAD_WIDTH] = o.astype(BF16)


def head_block(width, sequence=SEQUENCE_LENGTH):
    return pl.BlockSpec((sequence, width), lambda s, i: (s, i))


def attend(queries, keys, vals, ties=()):
    rows = queries.shape[0]
    steps = KEY_VALUE_HEADS // 2
    flops = 2 * QUERY_HEADS * rows * SEQUENCE_LENGTH * HEAD_WIDTH * 2
    return pl.pallas_call(
        tied(attend_kernel, 3, ties),
        grid=(rows // SEQUENCE_LENGTH, steps),
        in_specs=[head_block(4 * HEAD_WIDTH), head_block(2 * HEAD_WIDTH), head_block(2 * HEAD_WIDTH)] + [ANY] * len(ties),
        out_specs=head_block(4 * HEAD_WIDTH),
        out_shape=jax.ShapeDtypeStruct(queries.shape, BF16),
        compiler_params=params(),
        cost_estimate=cost(flops * 8, 6 * rows * 1024, QUERY_HEADS * rows * 640),
        name="attend",
    )(queries, keys, vals, *ties)


def attend_back_kernel(q_ref, k_ref, v_ref, g_ref, cos_ref, sin_ref, dq_ref, dk_ref, dv_ref, dk_acc, dv_acc, dq_acc):
    dk_acc[...] = jnp.zeros_like(dk_acc)
    dv_acc[...] = jnp.zeros_like(dv_acc)
    for c in range(2):
        lanes = slice(c * HEAD_WIDTH, (c + 1) * HEAD_WIDTH)
        k, v = k_ref[:, lanes], v_ref[:, lanes]
        for h in range(2):
            at = slice((2 * c + h) * HEAD_WIDTH, (2 * c + h + 1) * HEAD_WIDTH)
            for b in range(SEQUENCE_LENGTH // BLOCK):
                n = (b + 1) * BLOCK
                rows = slice(b * BLOCK, (b + 1) * BLOCK)
                q, g = q_ref[rows, at], g_ref[rows, at]
                s = dot_nt(k[:n], q)
                dp = dot_nt(v[:n], g)
                p = jnp.exp(s - jnp.max(s, axis=0, keepdims=True))
                p = p * (1.0 / jnp.sum(p, axis=0, keepdims=True))
                ds = (p * (dp - jnp.sum(p * dp, axis=0, keepdims=True))).astype(BF16)
                dv_acc[:n, lanes] += dot(p.astype(BF16), g)
                dk_acc[:n, lanes] += dot(ds, q)
                dq_acc[rows, at] = dot_tn(ds, k[:n])
    cos, sin = cos_ref[...], -sin_ref[...]
    scale = HEAD_WIDTH**-0.5
    dq_ref[:, :LANES] = rope(dq_acc[:, :LANES] * scale, cos, sin).astype(BF16)
    dq_ref[:, LANES:] = rope(dq_acc[:, LANES:] * scale, cos, sin).astype(BF16)
    dk_ref[...] = rope(dk_acc[...], cos, sin).astype(BF16)
    dv_ref[...] = dv_acc[...].astype(BF16)


def attend_back(queries, keys, vals, grad, cos, sin, first=0, steps=KEY_VALUE_HEADS // 2, ties=()):
    rows = queries.shape[0]
    flops = 5 * QUERY_HEADS * rows * SEQUENCE_LENGTH * HEAD_WIDTH * 2 * steps // (KEY_VALUE_HEADS // 2)
    table = pl.BlockSpec((SEQUENCE_LENGTH, LANES), lambda s, i: (s, 0))

    def block(width, start):
        return pl.BlockSpec((SEQUENCE_LENGTH, width), lambda s, i: (s, i + start))

    two, four = block(2 * HEAD_WIDTH, first), block(4 * HEAD_WIDTH, first)
    out_two, out_four = block(2 * HEAD_WIDTH, 0), block(4 * HEAD_WIDTH, 0)
    return pl.pallas_call(
        tied(attend_back_kernel, 6, ties),
        grid=(rows // SEQUENCE_LENGTH, steps),
        in_specs=[four, two, two, four, table, table] + [ANY] * len(ties),
        out_specs=[out_four, out_two, out_two],
        out_shape=[jax.ShapeDtypeStruct((rows, steps * w), BF16) for w in (4 * HEAD_WIDTH, 2 * HEAD_WIDTH, 2 * HEAD_WIDTH)],
        scratch_shapes=[
            pltpu.VMEM((SEQUENCE_LENGTH, LANES), F32),
            pltpu.VMEM((SEQUENCE_LENGTH, LANES), F32),
            pltpu.VMEM((SEQUENCE_LENGTH, 2 * LANES), F32),
        ],
        compiler_params=params(),
        cost_estimate=cost(flops * 8, 12 * rows * 1024, QUERY_HEADS * rows * 640),
        name="attend_back",
    )(queries, keys, vals, grad, cos, sin, *ties)


def middle_kernel(lane_of, a_ref, w_ref, x_ref, gain_ref, router_ref, routes_ref, r_ref, m_ref, mt_ref, gates_ref):
    resid = x_ref[...].astype(F32) + dot(a_ref[...], w_ref[...])
    r_ref[...] = resid
    inverse = lax.rsqrt(jnp.mean(resid * resid, axis=-1, keepdims=True) + 1e-06)
    moe_in = (resid * inverse * gain_ref[lane_of : lane_of + 1].astype(F32)).astype(BF16)
    m_ref[...] = moe_in
    mt_ref[...] = moe_in.T
    logits = dot(moe_in, router_ref[...])
    lane = lax.broadcasted_iota(jnp.int32, logits.shape, 1)
    routes = routes_ref[...]
    picked = lane == routes[:, 0:1]
    for k in range(1, routes.shape[1]):
        picked = jnp.logical_or(picked, lane == routes[:, k : k + 1])
    logits = jnp.where(picked, logits, -1e30)
    weights = jnp.where(picked, jnp.exp(logits - jnp.max(logits, axis=-1, keepdims=True)), 0.0)
    gates_ref[...] = weights / jnp.sum(weights, axis=-1, keepdims=True)


def middle(attended, out_w, tokens, gain, lane, router_w, routes, ties=()):
    rows, width = tokens.shape
    return pl.pallas_call(
        tied(functools.partial(middle_kernel, lane), 6, ties),
        grid=(rows // TILE,),
        in_specs=[
            row_block(width),
            whole_block(out_w.shape),
            row_block(width),
            whole_block(gain.shape),
            whole_block(router_w.shape),
            row_block(routes.shape[1]),
        ]
        + [ANY] * len(ties),
        out_specs=[row_block(width), row_block(width), pl.BlockSpec((width, TILE), lambda i: (0, i)), row_block(LANES)],
        out_shape=[
            jax.ShapeDtypeStruct((rows, width), F32),
            jax.ShapeDtypeStruct((rows, width), BF16),
            jax.ShapeDtypeStruct((width, rows), BF16),
            jax.ShapeDtypeStruct((rows, LANES), F32),
        ],
        compiler_params=params(LESS_BYTES),
        cost_estimate=cost(2 * rows * width * (width + LANES), 14 * rows * width),
        name="middle",
    )(attended, out_w, tokens, gain, router_w, routes, *ties)


def moe_kernel(slots, chunks, first, ties, me_ref, *refs):
    refs = list(refs)
    take = lambda count: [refs.pop(0) for _ in range(count)]
    x, xt, dy, dyt, gates_ref = take(5)
    if not first:
        take(3)
    weights = [[take(count) for count in per_slot] for per_slot in chunks]
    take(ties)
    made, dmoe, gg_ref = take(3)
    grads = [take(2) for _ in slots]
    wg, wu, wd, hg, dg, du, stage, sem_w, sem_out = take(9)
    rows, width = x.shape
    step = 512

    def load(source, target, sem):
        copy = pltpu.make_async_copy(source, target, sem)
        copy.start()
        return copy

    def load_weights(index):
        buffer = index % 2
        out = []
        for which, target in enumerate((wg, wu, wd)):
            at, copies = 0, []
            for piece, ref in enumerate(weights[index][which]):
                count = ref.shape[0]
                copies.append(load(ref, target.at[buffer, at : at + count], sem_w.at[buffer, which, piece]))
                at += count
            out.append(copies)
        return out

    pending = {0: load_weights(0)}
    if first:
        gg_ref[...] = jnp.zeros_like(gg_ref)
    stores = []
    lane = lax.broadcasted_iota(jnp.int32, (step, LANES), 1)
    for index, slot in enumerate(slots):
        buffer = index % 2
        arriving = pending.pop(index)
        if index + 1 < len(slots):
            pending[index + 1] = load_weights(index + 1)
        me = me_ref[0] ^ slot
        g_w, u_w, d_w = wg.at[buffer], wu.at[buffer], wd.at[buffer]

        def arrived(which, lo):
            if lo == 0:
                for copy in arriving[which]:
                    copy.wait()

        for lo in range(0, rows, step):
            at = slice(lo, lo + step)
            arrived(0, lo)
            gate = dot(x[at], g_w[...])
            arrived(1, lo)
            upval = dot(x[at], u_w[...])
            arrived(2, lo)
            pre = dot_nt(dy[at], d_w[...])
            column = jnp.sum(jnp.where(lane == me, gates_ref[at], 0.0), axis=1, keepdims=True)
            sigma = 1.0 / (1.0 + jnp.exp(-gate))
            silu = gate * sigma
            hidden = silu * upval
            gained = jnp.sum(hidden * pre, axis=1, keepdims=True)
            gg_ref[at] = gg_ref[at] + jnp.where(lane == me, gained, 0.0)
            weighted = (hidden * column).astype(BF16)
            dhidden = pre * column
            dgate = (dhidden * upval * (sigma + silu * (1.0 - sigma))).astype(BF16)
            dup = (dhidden * silu).astype(BF16)
            hg[at], dg[at], du[at] = weighted, dgate, dup
            fresh = dot(weighted, d_w[...])
            back = dot_nt(dgate, g_w[...]) + dot_nt(dup, u_w[...])
            if first and index == 0:
                made[at], dmoe[at] = fresh, back
            else:
                made[at] += fresh
                dmoe[at] += back
        for copy in stores:
            copy.wait()
        stores = []
        half = width // 2
        for part in range(2):
            at = slice(part * half, (part + 1) * half)
            stage[0, at] = dot(xt[at], dg[...]).astype(BF16)
            stage[1, at] = dot(xt[at], du[...]).astype(BF16)
            stage[2, at] = dot(dyt[at], hg[...]).astype(BF16)
            stores.append(load(stage.at[:, at], grads[index][part], sem_out.at[part]))
    for copy in stores:
        copy.wait()


def moe(slots, me, moe_in, moe_in_t, dy, dy_t, gates, acc, weights, ties=()):
    rows, width = moe_in.shape
    hidden = weights[0][0][0].shape[1]
    first = acc is None
    flat = [piece for per_slot in weights for pieces in per_slot for piece in pieces]
    chunks = tuple(tuple(len(pieces) for pieces in per_slot) for per_slot in weights)
    held = [pltpu.with_memory_space_constraint(a, pltpu.VMEM) for a in (moe_in, moe_in_t, dy, dy_t, gates, *(acc or ()))]
    grad = jax.ShapeDtypeStruct((3, width // 2, hidden), BF16)
    outs = pl.pallas_call(
        functools.partial(moe_kernel, tuple(slots), chunks, first, len(ties)),
        in_specs=[pl.BlockSpec(memory_space=pltpu.SMEM)] + [VMEM] * len(held) + [ANY] * (len(flat) + len(ties)),
        out_specs=[VMEM, VMEM, VMEM] + [ANY] * (2 * len(slots)),
        out_shape=[pltpu.VMEM((rows, width), F32), pltpu.VMEM((rows, width), F32), pltpu.VMEM((rows, LANES), F32)]
        + [grad] * (2 * len(slots)),
        scratch_shapes=[
            pltpu.VMEM((2, width, hidden), BF16),
            pltpu.VMEM((2, width, hidden), BF16),
            pltpu.VMEM((2, hidden, width), BF16),
            pltpu.VMEM((rows, hidden), BF16),
            pltpu.VMEM((rows, hidden), BF16),
            pltpu.VMEM((rows, hidden), BF16),
            pltpu.VMEM((3, width, hidden), BF16),
            pltpu.SemaphoreType.DMA((2, 3, 2)),
            pltpu.SemaphoreType.DMA((2,)),
        ],
        input_output_aliases={} if first else {6: 0, 7: 1, 8: 2},
        compiler_params=pltpu.CompilerParams(vmem_limit_bytes=EXPERT_BYTES),
        cost_estimate=cost(18 * rows * width * hidden * len(slots), 20 * rows * width),
        name="experts",
    )(me, *held, *flat, *ties)
    return outs[:3], [tuple(outs[3 + 2 * i : 5 + 2 * i]) for i in range(len(slots))]


def turn_kernel(
    lane, resid_ref, made_ref, dmoe_ref, gates_ref, gg_ref, dy_ref, gain_ref, router_ref, mt_ref, w_ref,
    mixed_ref, dresid_ref, dz_ref, da_ref, gain_grad_ref, router_grad_ref,
):
    @pl.when(pl.program_id(0) == 0)
    def _():
        gain_grad_ref[...] = jnp.zeros_like(gain_grad_ref)
        router_grad_ref[...] = jnp.zeros_like(router_grad_ref)

    resid = resid_ref[...]
    mixed_ref[...] = (resid + made_ref[...]).astype(BF16)
    gates, gg = gates_ref[...], gg_ref[...]
    dlogits = (gates * (gg - jnp.sum(gates * gg, axis=1, keepdims=True))).astype(BF16)
    router_grad_ref[...] += dot(mt_ref[...], dlogits)
    dmoe = dmoe_ref[...] + dot_nt(dlogits, router_ref[...])
    inverse = lax.rsqrt(jnp.mean(resid * resid, axis=-1, keepdims=True) + 1e-06)
    gain_grad_ref[...] += jnp.sum(dmoe * resid * inverse, axis=0, keepdims=True)
    scaled = dmoe * gain_ref[lane : lane + 1].astype(F32)
    inner = jnp.mean(scaled * resid, axis=-1, keepdims=True)
    dresid = dy_ref[...].astype(F32) + inverse * scaled - resid * (inverse * inverse * inverse * inner)
    dresid_ref[...] = dresid
    dz = dresid.astype(BF16)
    dz_ref[...] = dz
    da_ref[...] = dot_nt(dz, w_ref[...]).astype(BF16)


def turn(resid, made, dmoe, gates, gg, dy, gain, lane, router_w, moe_in_t, out_w, ties=()):
    rows, width = resid.shape
    return pl.pallas_call(
        tied(functools.partial(turn_kernel, lane), 10, ties),
        grid=(rows // TILE,),
        in_specs=[
            row_block(width), row_block(width), row_block(width), row_block(LANES), row_block(LANES), row_block(width),
            whole_block(gain.shape), whole_block(router_w.shape), pl.BlockSpec((width, TILE), lambda i: (0, i)),
            whole_block(out_w.shape),
        ]
        + [ANY] * len(ties),
        out_specs=[row_block(width)] * 4 + [whole_block((1, width)), whole_block((width, LANES))],
        out_shape=[
            jax.ShapeDtypeStruct((rows, width), BF16),
            jax.ShapeDtypeStruct((rows, width), F32),
            jax.ShapeDtypeStruct((rows, width), BF16),
            jax.ShapeDtypeStruct((rows, width), BF16),
            jax.ShapeDtypeStruct((1, width), F32),
            jax.ShapeDtypeStruct((width, LANES), F32),
        ],
        compiler_params=params(LESS_BYTES),
        cost_estimate=cost(2 * rows * width * (width + 2 * LANES), 28 * rows * width),
        name="turn",
    )(resid, made, dmoe, gates, gg, dy, gain, router_w, moe_in_t, out_w, *ties)


def finish_kernel(lane, count, *refs):
    grads = refs[:count]
    w_ref, x_ref, dresid_ref, gain_ref, router_ref, second_ref, out_ref, small_ref, first = refs[count:]

    @pl.when(pl.program_id(0) == 0)
    def _():
        first[...] = jnp.zeros_like(first)

    at, dn = 0, 0.0
    for ref in grads:
        dn += dot_nt(ref[...], w_ref[:, at : at + ref.shape[1]])
        at += ref.shape[1]
    x = x_ref[...].astype(F32)
    inverse = lax.rsqrt(jnp.mean(x * x, axis=-1, keepdims=True) + 1e-06)
    first[...] += jnp.sum(dn * x * inverse, axis=0, keepdims=True)
    scaled = dn * gain_ref[lane : lane + 1].astype(F32)
    inner = jnp.mean(scaled * x, axis=-1, keepdims=True)
    out_ref[...] = dresid_ref[...] + inverse * scaled - x * (inverse * inverse * inverse * inner)

    @pl.when(pl.program_id(0) == pl.num_programs(0) - 1)
    def _():
        row = lax.broadcasted_iota(jnp.int32, (LANES, first.shape[1]), 0)
        gains = jnp.where(row == lane, first[...], 0.0) + jnp.where(row == lane + 1, second_ref[...], 0.0)
        small_ref[...] = (router_ref[...] + gains.T).astype(BF16)


def finish(grads, weights, tokens, dresid, gain, lane, router_grad, second, ties=()):
    rows, width = tokens.shape
    return pl.pallas_call(
        tied(functools.partial(finish_kernel, lane, len(grads)), len(grads) + 6, ties),
        grid=(rows // TILE,),
        in_specs=[row_block(g.shape[1]) for g in grads]
        + [whole_block(weights.shape), row_block(width), row_block(width), whole_block(gain.shape)]
        + [whole_block(router_grad.shape), whole_block(second.shape)]
        + [ANY] * len(ties),
        out_specs=[row_block(width), whole_block((width, LANES))],
        out_shape=[jax.ShapeDtypeStruct((rows, width), F32), jax.ShapeDtypeStruct((width, LANES), BF16)],
        scratch_shapes=[pltpu.VMEM((1, width), F32)],
        compiler_params=params(),
        cost_estimate=cost(1, 1),
        name="finish",
    )(*grads, weights, tokens, dresid, gain, router_grad, second, *ties)


def weights_back_kernel(count, *refs):
    for grad, out in zip(refs[1 : count + 1], refs[count + 1 :]):
        out[...] = dot(refs[0][...], grad[...]).astype(BF16)


def weights_back(turned, grads, ties=()):
    rows = turned.shape[0]
    return pl.pallas_call(
        tied(functools.partial(weights_back_kernel, len(grads)), len(grads) + 1, ties),
        grid=(rows // TILE,),
        in_specs=[row_block(turned.shape[1])] + [whole_block(g.shape) for g in grads] + [ANY] * len(ties),
        out_specs=[row_block(g.shape[1]) for g in grads],
        out_shape=[jax.ShapeDtypeStruct((rows, g.shape[1]), BF16) for g in grads],
        compiler_params=params(),
        cost_estimate=cost(1, 1),
        name="weights_back",
    )(turned, *grads, *ties)


def widen_kernel(top_ref, bottom_ref, gate_ref, up_ref, down_ref):
    step = pl.program_id(0)
    for half, ref in enumerate((top_ref, bottom_ref)):

        @pl.when(step // 2 == half)
        def _():
            gate_ref[...] = ref[0].astype(F32)
            up_ref[...] = ref[1].astype(F32)
            down_ref[...] = ref[2].astype(F32).T


def widen(top, bottom):
    _, rows, columns = top.shape
    step = rows // 2
    block = pl.BlockSpec((step, columns), lambda i: (i, 0))
    return pl.pallas_call(
        widen_kernel,
        grid=(4,),
        in_specs=[
            pl.BlockSpec((3, step, columns), lambda i: (0, jnp.minimum(i, 1), 0)),
            pl.BlockSpec((3, step, columns), lambda i: (0, jnp.maximum(i - 2, 0), 0)),
        ],
        out_specs=[block, block, pl.BlockSpec((columns, step), lambda i: (0, i))],
        out_shape=[
            jax.ShapeDtypeStruct((2 * rows, columns), F32),
            jax.ShapeDtypeStruct((2 * rows, columns), F32),
            jax.ShapeDtypeStruct((columns, 2 * rows), F32),
        ],
        compiler_params=params(),
        cost_estimate=cost(1, 1),
        name="widen",
    )(top, bottom)


def plus_kernel(counts, *refs):
    refs = list(refs)
    refs.pop()[...] = jnp.zeros((8, LANES), F32)
    ins = [[refs.pop(0) for _ in range(count)] for count in counts]
    for terms, out in zip(ins, refs):
        total = terms[0][...].astype(F32)
        for ref in terms[1:]:
            total += ref[...].astype(F32)
        out[...] = total.astype(BF16)


def plus(*groups, ties=()):
    shape = groups[0][0].shape
    block = pl.BlockSpec((1, shape[1] // 2, shape[2]), lambda i, j: (i, j, 0))
    counts = tuple(len(terms) for terms in groups)
    flat = [a for terms in groups for a in terms]
    return pl.pallas_call(
        tied(functools.partial(plus_kernel, counts), len(flat), ties),
        grid=(shape[0], 2),
        in_specs=[block] * len(flat) + [ANY] * len(ties),
        out_specs=[block] * len(groups) + [pl.BlockSpec((8, LANES), lambda i, j: (0, 0))],
        out_shape=[jax.ShapeDtypeStruct(shape, BF16)] * len(groups) + [jax.ShapeDtypeStruct((8, LANES), F32)],
        compiler_params=pltpu.CompilerParams(vmem_limit_bytes=16 * 1024 * 1024),
        cost_estimate=cost(len(flat) * flat[0].size, 2 * (len(flat) + len(groups)) * flat[0].size),
        name="plus",
    )(*flat, *ties)


def gather_kernel(size, count, *refs):
    q_ref, k_ref, v_ref, s_ref, o_ref, d_ref = refs[:6]
    owned, refs = refs[6 : 6 + count], refs[6 + count :]
    packed_ref, small_ref, out_ref, down_ref, turned_ref = refs[:5]
    beside, refs = refs[5 : 5 + 2 * count], refs[5 + 2 * count :]
    beyond, refs = refs[: 2 * count], refs[2 * count :]
    pair, refs = refs[: count + 1 if count else 0], refs[count + 1 if count else 0 :]
    send_sem, recv_sem, pass_sem, take_sem, away_sem, come_sem, over_sem, land_sem = refs
    me, z = lax.axis_index("expert"), lax.axis_index("wshard")
    core = lax.rem(me, 2)
    sibling = me + 1 - 2 * core
    rows = q_ref.shape[0]
    half = rows // 2
    there = lambda step: jnp.logical_and(z + step >= 0, z + step < size)

    barrier = pltpu.get_barrier_semaphore()
    pl.semaphore_signal(barrier, inc=1, device_id=(sibling, z), device_id_type=pl.DeviceIdType.MESH)
    for step in (1, -1):

        @pl.when(there(step))
        def _():
            pl.semaphore_signal(barrier, inc=1, device_id=(me, z + step), device_id_type=pl.DeviceIdType.MESH)

    neighbours = []
    if count:
        xb, yb = lax.rem(me // 2, 2), me // 4
        neighbours = [me + 2 - 4 * xb, me + 4 - 8 * yb]
    for peer in neighbours:
        pl.semaphore_signal(barrier, inc=1, device_id=(peer, z), device_id_type=pl.DeviceIdType.MESH)
    pl.semaphore_wait(barrier, 1 + len(neighbours) + jnp.where(z > 0, 1, 0) + jnp.where(z < size - 1, 1, 0))
    shipped = []
    for i, ref in enumerate(owned):
        for j, peer in enumerate(neighbours):
            shipped.append(
                pltpu.make_async_remote_copy(
                    src_ref=ref, dst_ref=beside[j * count + i], send_sem=away_sem.at[i, j], recv_sem=come_sem.at[i, j],
                    device_id=(peer, z), device_id_type=pl.DeviceIdType.MESH,
                )
            )
    for copy in shipped:
        copy.start()

    def passed(source, target, i, j):
        return pltpu.make_async_remote_copy(
            src_ref=source, dst_ref=target, send_sem=over_sem.at[i, j], recv_sem=land_sem.at[i, j],
            device_id=(sibling, z), device_id_type=pl.DeviceIdType.MESH,
        )

    swapped = [passed(ref, target, i, 2) for i, (ref, target) in enumerate(zip(owned, pair))]

    own = pl.ds(pl.multiple_of(z * rows, rows), rows)
    at = 0
    for ref in (q_ref, k_ref, v_ref):
        packed_ref[own, at : at + ref.shape[1]] = ref[...]
        at += ref.shape[1]
    small_ref[own] = s_ref[...]
    out_ref[...] = o_ref[...]
    down_ref[...] = d_ref[...]
    if count:
        swapped.append(passed(down_ref, pair[count], count, 2))
    for copy in swapped:
        copy.start()

    def moves(way, hop, origin, which, device, send, recv):
        at = pl.ds(pl.multiple_of(origin * rows + which * half, half), half)
        return [
            pltpu.make_async_remote_copy(
                src_ref=ref.at[at], dst_ref=ref.at[at], send_sem=send.at[way, hop, i], recv_sem=recv.at[way, hop, i],
                device_id=device, device_id_type=pl.DeviceIdType.MESH,
            )
            for i, ref in enumerate((packed_ref, small_ref))
        ]

    def onward(way, step, hop):
        return moves(way, hop, z - step * (hop - 1), core, (me, z + step), send_sem, recv_sem)

    def across(way, step, hop, which):
        return moves(way, hop, z - step * hop, which, (sibling, z), pass_sem, take_sem)

    ways = ((0, 1), (1, -1))
    for way, step in ways:

        @pl.when(there(step))
        def _():
            for move in onward(way, step, 1):
                move.start()

    for hop in range(1, size):
        for way, step in ways:

            @pl.when(there(-step * hop))
            def _():
                for move in moves(way, hop, z - step * hop, core, (me, z), send_sem, recv_sem):
                    move.wait_recv()

                @pl.when(there(step))
                def _():
                    for move in onward(way, step, hop + 1):
                        move.start()

                for move in across(way, step, hop, core):
                    move.start()

    for hop in range(1, size):
        for way, step in ways:

            @pl.when(there(-step * hop))
            def _():
                for move in across(way, step, hop, 1 - core):
                    move.wait_recv()
                for move in across(way, step, hop, core):
                    move.wait_send()

            @pl.when(jnp.logical_and(there(step), there(-step * (hop - 1))))
            def _():
                for move in onward(way, step, hop):
                    move.wait_send()

    turned_ref[...] = small_ref[...].T
    onto = []
    for n, copy in enumerate(shipped):
        i, j = n // 2, n % 2
        copy.wait_recv()
        onto.append(passed(beside[j * count + i], beyond[j * count + i], i, j))
        onto[-1].start()
    for copy in shipped:
        copy.wait_send()
    for copy in swapped + onto:
        copy.wait()


def gather_weights(query, key, value, small, out, down, owned=()):
    size = lax.axis_size("wshard")
    rows = query.shape[0]
    width = query.shape[1] + key.shape[1] + value.shape[1]
    sems = pltpu.SemaphoreType.DMA((2, size + 1, 2))
    last = [*owned, down] if len(owned) else []
    return pl.pallas_call(
        functools.partial(gather_kernel, size, len(owned)),
        in_specs=[VMEM] * 6 + [ANY] * len(owned),
        out_specs=[VMEM] * 5 + [ANY] * (4 * len(owned) + len(last)),
        out_shape=[
            jax.ShapeDtypeStruct((size * rows, width), BF16),
            jax.ShapeDtypeStruct((size * rows, small.shape[1]), BF16),
            jax.ShapeDtypeStruct(out.shape, BF16),
            jax.ShapeDtypeStruct(down.shape, BF16),
            jax.ShapeDtypeStruct((small.shape[1], size * rows), BF16),
        ]
        + [jax.ShapeDtypeStruct(a.shape, BF16) for a in owned] * 4
        + [jax.ShapeDtypeStruct(a.shape, BF16) for a in last],
        scratch_shapes=[sems, sems, sems, sems] + [pltpu.SemaphoreType.DMA((len(owned) + 1, 3))] * 4,
        compiler_params=pltpu.CompilerParams(collective_id=0, has_side_effects=True, vmem_limit_bytes=VMEM_BYTES),
        cost_estimate=cost(1e9, 12 * rows * size * width),
        name="gather_weights",
    )(query, key, value, small, out, down, *owned)


def reduce_kernel(size, columns, *refs):
    count = sum(len(widths) for widths in columns)
    ins, outs = list(refs[:count]), refs[count : count + len(columns)]
    acc, rc, r1, r2, zs, rz, res, send_sem, recv_sem = refs[count + len(columns) :]
    me, z = lax.axis_index("expert"), lax.axis_index("wshard")
    core, xb, yb = lax.rem(me, 2), lax.rem(me // 2, 2), me // 4
    sibling, xp, yp = me + 1 - 2 * core, me + 2 - 4 * xb, me + 4 - 8 * yb
    half = ins[0].shape[1] // 2
    n1, n2 = half // 4, half // 8

    barrier = pltpu.get_barrier_semaphore()
    for peer in (sibling, xp, yp):
        pl.semaphore_signal(barrier, inc=1, device_id=(peer, z), device_id_type=pl.DeviceIdType.MESH)
    for d in range(1, size):
        pl.semaphore_signal(barrier, inc=1, device_id=(me, lax.rem(z + d, size)), device_id_type=pl.DeviceIdType.MESH)
    pl.semaphore_wait(barrier, 2 + size)

    pieces, at = [], 0
    for out, widths in zip(outs, columns):
        start = 0
        for width in widths:
            ref, step = ins.pop(0), min(width, 512)
            for lo in range(0, width, step):
                pieces.append((ref, out, lo, step, at, start + lo))
                at += step
            start += width

    sent = []

    def move(source, target, piece, kind, device):
        copy = pltpu.make_async_remote_copy(
            src_ref=source, dst_ref=target, send_sem=send_sem.at[kind, piece], recv_sem=recv_sem.at[kind, piece],
            device_id=device, device_id_type=pl.DeviceIdType.MESH,
        )
        copy.start()
        sent.append(copy)
        return copy

    def rows(start, length):
        return pl.ds(pl.multiple_of(start, 16), length)

    def sum_of(*terms):
        total = terms[0].astype(F32)
        for term in terms[1:]:
            total += term.astype(F32)
        return total

    k0, k1 = xb * n1 + yb * n2, half // 2 + yb * n1 + xb * n2
    base = core * half
    first = []
    for p, (ref, _, lo, w, at, _) in enumerate(pieces):
        first.append(move(ref.at[:, rows((1 - core) * half, half), lo : lo + w], rc.at[:, :, at : at + w], p, 0, (sibling, z)))
    second = []
    for p, (ref, _, lo, w, at, _) in enumerate(pieces):
        c = slice(at, at + w)
        first[p].wait_recv()
        acc[:, :, c] = sum_of(ref[:, rows(base, half), lo : lo + w], rc[:, :, c]).astype(BF16)
        second.append((
            move(acc.at[:, rows((1 - xb) * n1, n1), c], r1.at[0, :, :, c], p, 1, (xp, z)),
            move(acc.at[:, rows(half // 2 + (1 - yb) * n1, n1), c], r1.at[1, :, :, c], p, 2, (yp, z)),
        ))
    third = []
    for p, (_, _, _, w, at, _) in enumerate(pieces):
        c = slice(at, at + w)
        keep = (rows(xb * n1, n1), rows(half // 2 + yb * n1, n1))
        for i in range(2):
            second[p][i].wait_recv()
            acc[:, keep[i], c] = sum_of(acc[:, keep[i], c], r1[i, :, :, c]).astype(BF16)
        third.append((
            move(acc.at[:, rows(xb * n1 + (1 - yb) * n2, n2), c], r2.at[0, :, :, c], p, 3, (yp, z)),
            move(acc.at[:, rows(half // 2 + yb * n1 + (1 - xb) * n2, n2), c], r2.at[1, :, :, c], p, 4, (xp, z)),
        ))
    fourth = []
    for p, (_, _, _, w, at, _) in enumerate(pieces):
        c = slice(at, at + w)
        for i, k in enumerate((k0, k1)):
            third[p][i].wait_recv()
            zs[:, i * n2 : (i + 1) * n2, c] = sum_of(acc[:, rows(k, n2), c], r2[i, :, :, c]).astype(BF16)
        fourth.append([
            move(zs.at[lax.rem(z + d, size), :, c], rz.at[d - 1, :, c], p, 8 + d, (me, lax.rem(z + d, size)))
            for d in range(1, size)
        ])
    fifth = []
    for p, (_, _, _, w, at, _) in enumerate(pieces):
        c = slice(at, at + w)
        for copy in fourth[p]:
            copy.wait_recv()
        total = sum_of(zs[z, :, c], *[rz[d, :, c] for d in range(size - 1)]).astype(BF16)
        for i, k in enumerate((k0, k1)):
            res[rows(base + k, n2), c] = total[i * n2 : (i + 1) * n2]
        fifth.append((
            move(res.at[rows(base + k0, n2), c], res.at[rows(base + k0, n2), c], p, 5, (yp, z)),
            move(res.at[rows(base + k1, n2), c], res.at[rows(base + k1, n2), c], p, 6, (xp, z)),
        ))
    sixth = []
    for p, (_, _, _, w, at, _) in enumerate(pieces):
        c = slice(at, at + w)
        for copy in fifth[p]:
            copy.wait_recv()
        mine = rows(base + xb * n1, n1), rows(base + half // 2 + yb * n1, n1)
        sixth.append((
            move(res.at[mine[0], c], res.at[mine[0], c], p, 7, (xp, z)),
            move(res.at[mine[1], c], res.at[mine[1], c], p, 8, (yp, z)),
        ))
    last = []
    for p, (_, _, _, w, at, _) in enumerate(pieces):
        c = slice(at, at + w)
        for copy in sixth[p]:
            copy.wait_recv()
        last.append(move(res.at[rows(base, half), c], res.at[rows(base, half), c], p, 8 + size, (sibling, z)))
    for p, (_, out, _, w, at, to) in enumerate(pieces):
        last[p].wait_recv()
        out[:, to : to + w] = res[:, at : at + w].astype(F32)
    for copy in sent:
        copy.wait_send()


def reduce_all(*groups):
    size = lax.axis_size("wshard")
    rows = groups[0][0].shape[0] // size
    grads = [g for group in groups for g in group]
    columns = tuple(tuple(g.shape[1] for g in group) for group in groups)
    count = sum(-(-g.shape[1] // 512) for g in grads)
    width, half = sum(g.shape[1] for g in grads), rows // 2
    return pl.pallas_call(
        functools.partial(reduce_kernel, size, columns),
        in_specs=[VMEM] * len(grads),
        out_specs=[VMEM] * len(groups),
        out_shape=[jax.ShapeDtypeStruct((rows, sum(widths)), F32) for widths in columns],
        scratch_shapes=[
            pltpu.VMEM((size, half, width), BF16),
            pltpu.VMEM((size, half, width), BF16),
            pltpu.VMEM((2, size, half // 4, width), BF16),
            pltpu.VMEM((2, size, half // 8, width), BF16),
            pltpu.VMEM((size, half // 4, width), BF16),
            pltpu.VMEM((size - 1, half // 4, width), BF16),
            pltpu.VMEM((rows, width), BF16),
            pltpu.SemaphoreType.DMA((9 + size, count)),
            pltpu.SemaphoreType.DMA((9 + size, count)),
        ],
        compiler_params=pltpu.CompilerParams(collective_id=1, has_side_effects=True, vmem_limit_bytes=VMEM_BYTES),
        cost_estimate=cost(1, 1),
        name="reduce_all",
    )(*[g.reshape(size, rows, g.shape[1]) for g in grads])


def flip(value, axis, bit):
    size = lax.axis_size(axis)
    return lax.ppermute(value, axis, [(i, i ^ bit) for i in range(size)])


def gather_experts(mats, owners):
    slots, bit = {0: tuple([m] for m in mats)}, 2
    while bit < owners:
        for j in sorted(slots):
            slots[j | bit] = tuple([flip(p, "expert", bit) for p in m] for m in slots[j])
        bit *= 2
    return slots


def third_slot(a, b):
    cut = a[2][0].shape[0] // 2
    return (
        [flip(a[0][0], "expert", 4)],
        [flip(b[1][0], "expert", 2)],
        [flip(a[2][0][:cut], "expert", 4), flip(b[2][0][cut:], "expert", 2)],
    )


def across_core(slot):
    return tuple([flip(p, "expert", 1) for p in m] for m in slot)


def add(a, b):
    return (a.astype(F32) + b.astype(F32)).astype(BF16)


def reduce_experts(parts, owners):
    bit = 1
    while bit < owners:
        for j in sorted(parts, reverse=True):
            if j & bit:
                gone = parts.pop(j)
                parts[j ^ bit] = tuple(add(m, flip(s, "expert", bit)) for m, s in zip(parts[j ^ bit], gone))
        bit *= 2
    return parts[0]


def on_device(
    tokens, gain_attn, w_query, key_weight, value_weight, w_out, gain_ffn, w_router, w_gate, w_up, w_down, routes, cotangent
):
    owners = lax.axis_size("expert")
    me = lax.axis_index("expert").astype(jnp.int32)[None]
    rows, width = tokens.shape
    experts = w_router.shape[1]
    mats = (w_gate[0], w_up[0], w_down[0])

    small = jnp.concatenate([w_router, gain_attn[:, None], gain_ffn[:, None]], axis=1)
    small = jnp.pad(small, ((0, 0), (0, LANES - small.shape[1])))
    packed, small, out_shard, down, gains, *beside = gather_weights(
        w_query, key_weight, value_weight, small, w_out, mats[2], mats[:2] if owners == 8 else ()
    )
    out_w = lax.all_gather(out_shard, "wshard", axis=0, tiled=True)
    cos, sin = (jnp.asarray(a) for a in rope_tables(rows))

    if owners == 8:
        slots = {0: tuple([m] for m in mats)}
        slots[2] = ([beside[0]], [beside[1]], [flip(down, "expert", 2)])
        slots[4] = ([beside[2]], [beside[3]], [flip(down, "expert", 4)])
        slots[6] = third_slot(slots[2], slots[4])
    else:
        slots = gather_experts(mats, owners)
    normed_t, queries, keys, vals = project(tokens, gains, experts, packed, cos, sin)
    def pieces_of(*which, first=0, last=3):
        return [p for j in which for m in slots[j][first:last] for p in m] if owners == 8 else []

    attended = attend(queries, keys, vals)
    if owners == 8:
        slots[1] = tuple([m] for m in beside[8:])
        downs = lax.optimization_barrier((slots[2][2][0], slots[4][2][0], attended))
        slots[3] = ([beside[4]], [beside[5]], [flip(downs[0], "expert", 1)])
        slots[5] = ([beside[6]], [beside[7]], [flip(downs[1], "expert", 1)])
        slots[7] = across_core(slots[6])
    else:
        for j in sorted(slots):
            slots[j | 1] = across_core(slots[j])
    resid, moe_in, moe_in_t, gates = middle(
        attended, out_w, tokens, gains, experts + 1, small, routes, pieces_of(2, 4)
    )
    dy_t = cotangent.T

    def one(j, acc, ties=()):
        acc, (halves,) = moe([j], me, moe_in, moe_in_t, cotangent, dy_t, gates, acc, [slots[j]], ties)
        return acc, halves

    def turned(acc, ties=()):
        made, dmoe, gate_grads = acc
        return turn(
            resid, made, dmoe, gates, gate_grads, cotangent, gains, experts + 1, small, moe_in_t, out_w, ties
        )

    if owners == 8:
        core = lambda halves: [flip(m, "expert", 1) for m in halves]
        over_x = lambda m: flip(m, "expert", 2)
        over_y = lambda m: flip(m, "expert", 4)
        acc, g3 = one(3, None, pieces_of(6, last=2))
        c3 = core(g3)
        acc, g2 = one(2, acc, pieces_of(6))
        *s2, t2 = plus((g2[0], c3[0]), (g2[1], c3[1]))
        x20 = over_x(s2[0])
        acc, g7 = one(7, acc, [t2])
        c7 = core(g7)
        acc, g6 = one(6, acc)
        *s6, t6 = plus((g6[0], c7[0]), (g6[1], c7[1]))
        x60, y61 = over_x(s6[0]), over_y(s6[1])
        acc, g5 = one(5, acc, [t6])
        c5 = core(g5)
        acc, g4 = one(4, acc, [x20])
        *s4, t4 = plus((g4[0], c5[0]), (g4[1], c5[1]))
        y41 = over_y(s4[1])
        acc, g1 = one(1, acc, [t4])
        c1 = core(g1)
        left, right, sides = plus((s4[0], x60), (s2[1], y61))
        x21, y40 = over_x(right), over_y(left)
        acc, g0 = one(0, acc, [sides])
        *s0, t0 = plus((g0[0], c1[0]), (g0[1], c1[1]))
        mixed, dresid, dz, dattended, gain_two_grad, router_grad = turned(acc, [t0])
        out_grad = dot_tn(attended, dz).astype(BF16)
        early = attend_back(queries, keys, vals, dattended, cos, sin, 0, 2, [out_grad])
        top, bottom, both = plus((s0[0], x20, y40), (s0[1], y41, x21), ties=early[2:])
        late = attend_back(queries, keys, vals, dattended, cos, sin, 2, 2, [both])
        top, bottom = lax.psum((top, bottom), "wshard")
        pieces = [early[0], late[0], early[1], late[1], early[2], late[2]]
        weight_grads = weights_back(normed_t, pieces)
        own, after = [top, bottom], []
    else:
        acc, parts = None, {}
        for j in range(owners):
            acc, parts[j] = one(j, acc)
        mixed, dresid, dz, dattended, gain_two_grad, router_grad = turned(acc)
        own, after = lax.psum(tuple(reduce_experts(parts, owners)), "wshard"), []
        out_grad = dot_tn(attended, dz).astype(BF16)
        pieces = attend_back(queries, keys, vals, dattended, cos, sin)
        weight_grads = weights_back(normed_t, pieces)
    d_tokens, small_grad = finish(pieces, packed, tokens, dresid, gains, experts, router_grad, gain_two_grad, after)
    third = len(weight_grads) // 3
    groups = [[out_grad]] + [weight_grads[i : i + third] for i in range(0, 3 * third, third)] + [[small_grad]]
    if owners == 8:
        sums = reduce_all(*groups)
    else:
        total = lambda g: lax.psum(lax.psum_scatter(g, "wshard", scatter_dimension=0, tiled=True), "expert")
        sums = [total(jnp.concatenate(group, axis=1)).astype(F32) for group in groups]
    out_grad, query_grad, key_grad, value_grad, small_grad = sums
    gate_grad, up_grad, down_grad = widen(*own)
    return (
        mixed,
        d_tokens,
        small_grad[:, experts],
        query_grad,
        key_grad,
        value_grad,
        out_grad,
        small_grad[:, experts + 1],
        small_grad[:, :experts],
        gate_grad[None],
        up_grad[None],
        down_grad[None],
    )


def solution(mesh):
    whole, shard, matrix, owned = P(("expert", "wshard"), None), P("wshard"), P("wshard", None), P("expert", None, None)
    return jax.shard_map(
        on_device,
        mesh=mesh,
        in_specs=(whole, shard, matrix, matrix, matrix, matrix, shard, matrix, owned, owned, owned, whole, whole),
        out_specs=(whole, whole, shard, matrix, matrix, matrix, matrix, shard, matrix, owned, owned, owned),
        check_vma=False,
    )
```

```python
import functools
import jax
import jax.numpy as jnp
import numpy as np
from jax import lax
from jax.experimental import pallas as pl
from jax.experimental.pallas import tpu as pltpu
from jax.sharding import PartitionSpec as P

QUERY_HEADS = 16
KEY_VALUE_HEADS = 8
HEAD_WIDTH = 64
SEQUENCE_LENGTH = 1024
BLOCK = 256
TILE = 256
LANES = 128
F32 = jnp.float32
BF16 = jnp.bfloat16
ANY = pl.BlockSpec(memory_space=pl.ANY)
VMEM = pl.BlockSpec(memory_space=pltpu.VMEM)
VMEM_BYTES = 60 * 1024 * 1024
LESS_BYTES = 30 * 1024 * 1024
EXPERT_BYTES = 26 * 1024 * 1024


def dot(a, b):
    return jnp.dot(a, b, preferred_element_type=F32)


def dot_nt(a, b):
    return lax.dot_general(a, b, (((1,), (1,)), ((), ())), preferred_element_type=F32)


def dot_tn(a, b):
    return lax.dot_general(a, b, (((0,), (0,)), ((), ())), preferred_element_type=F32)


def params(size=VMEM_BYTES):
    return pltpu.CompilerParams(vmem_limit_bytes=size)


def cost(flops, nbytes, transcendentals=0):
    return pl.CostEstimate(flops=int(flops), bytes_accessed=int(nbytes), transcendentals=int(transcendentals))


def rope_tables(rows):
    half = HEAD_WIDTH // 2
    freq = np.exp(-np.log(10000.0) * np.arange(half, dtype=np.float32) * 2.0 / HEAD_WIDTH).astype(np.float32)
    pos = (np.arange(rows) % SEQUENCE_LENGTH).astype(np.float32)
    angles = (pos[:, None] * freq[None, :]).astype(np.float32)
    cos, sin = np.cos(angles), np.sin(angles)
    return (
        np.concatenate([cos, cos, cos, cos], 1).astype(np.float32),
        np.concatenate([-sin, sin, -sin, sin], 1).astype(np.float32),
    )


def rope(u, cos, sin):
    half = HEAD_WIDTH // 2
    lane = lax.broadcasted_iota(jnp.int32, u.shape, 1)
    swapped = jnp.where(
        lane % HEAD_WIDTH < half, pltpu.roll(u, LANES - half, 1), pltpu.roll(u, half, 1)
    )
    return u * cos + swapped * sin


def row_block(width):
    return pl.BlockSpec((TILE, width), lambda i: (i, 0))


def whole_block(shape):
    return pl.BlockSpec(shape, lambda i: (0,) * len(shape))


def tied(kernel, inputs, ties):
    return lambda *refs: kernel(*refs[:inputs], *refs[inputs + len(ties) :])


def project_kernel(lane, x_ref, gain_ref, w_ref, cos_ref, sin_ref, n_ref, q_ref, k_ref, v_ref):
    x = x_ref[...].astype(F32)
    inverse = lax.rsqrt(jnp.mean(x * x, axis=-1, keepdims=True) + 1e-06)
    normed = (x * inverse * gain_ref[lane : lane + 1].astype(F32)).astype(BF16)
    n_ref[...] = normed.T
    cos, sin = cos_ref[...], sin_ref[...]
    step = 512
    for at in range(0, w_ref.shape[1], step):
        made = dot(normed, w_ref[:, at : at + step])
        for lo in range(0, step, LANES):
            u = made[:, lo : lo + LANES]
            c = at + lo
            if c < q_ref.shape[1]:
                q_ref[:, c : c + LANES] = (rope(u, cos, sin).astype(BF16) * jnp.asarray(HEAD_WIDTH**-0.5, BF16))
            elif c < q_ref.shape[1] + k_ref.shape[1]:
                c -= q_ref.shape[1]
                k_ref[:, c : c + LANES] = rope(u, cos, sin).astype(BF16)
            else:
                c -= q_ref.shape[1] + k_ref.shape[1]
                v_ref[:, c : c + LANES] = u.astype(BF16)


def project(tokens, gain, lane, weights, cos, sin):
    rows, width = tokens.shape
    qw, kw = QUERY_HEADS * HEAD_WIDTH, KEY_VALUE_HEADS * HEAD_WIDTH
    return pl.pallas_call(
        functools.partial(project_kernel, lane),
        grid=(rows // TILE,),
        in_specs=[row_block(width), whole_block(gain.shape), whole_block(weights.shape), row_block(LANES), row_block(LANES)],
        out_specs=[pl.BlockSpec((width, TILE), lambda i: (0, i)), row_block(qw), row_block(kw), row_block(kw)],
        out_shape=[jax.ShapeDtypeStruct(s, BF16) for s in ((width, rows), (rows, qw), (rows, kw), (rows, kw))],
        compiler_params=params(),
        cost_estimate=cost(2 * rows * width * (qw + 2 * kw), 12 * rows * width),
        name="project",
    )(tokens, gain, weights, cos, sin)


def attend_kernel(q_ref, k_ref, v_ref, o_ref):
    for c in range(2):
        k = k_ref[:, c * HEAD_WIDTH : (c + 1) * HEAD_WIDTH]
        v = v_ref[:, c * HEAD_WIDTH : (c + 1) * HEAD_WIDTH]
        for h in range(2):
            at = (2 * c + h) * HEAD_WIDTH
            for b in range(SEQUENCE_LENGTH // BLOCK):
                n = (b + 1) * BLOCK
                rows = slice(b * BLOCK, (b + 1) * BLOCK)
                s = dot_nt(q_ref[rows, at : at + HEAD_WIDTH], k[:n])
                p = jnp.exp(s - jnp.max(s, axis=-1, keepdims=True))
                total = jnp.sum(p, axis=-1, keepdims=True)
                o = dot((p * (1.0 / total)).astype(BF16), v[:n])
                o_ref[rows, at : at + HEAD_WIDTH] = o.astype(BF16)


def head_block(width, sequence=SEQUENCE_LENGTH):
    return pl.BlockSpec((sequence, width), lambda s, i: (s, i))


def attend(queries, keys, vals, ties=()):
    rows = queries.shape[0]
    steps = KEY_VALUE_HEADS // 2
    flops = 2 * QUERY_HEADS * rows * SEQUENCE_LENGTH * HEAD_WIDTH * 2
    return pl.pallas_call(
        tied(attend_kernel, 3, ties),
        grid=(rows // SEQUENCE_LENGTH, steps),
        in_specs=[head_block(4 * HEAD_WIDTH), head_block(2 * HEAD_WIDTH), head_block(2 * HEAD_WIDTH)] + [ANY] * len(ties),
        out_specs=head_block(4 * HEAD_WIDTH),
        out_shape=jax.ShapeDtypeStruct(queries.shape, BF16),
        compiler_params=params(),
        cost_estimate=cost(flops * 8, 6 * rows * 1024, QUERY_HEADS * rows * 640),
        name="attend",
    )(queries, keys, vals, *ties)


def attend_back_kernel(q_ref, k_ref, v_ref, g_ref, cos_ref, sin_ref, dq_ref, dk_ref, dv_ref, dk_acc, dv_acc, dq_acc):
    dk_acc[...] = jnp.zeros_like(dk_acc)
    dv_acc[...] = jnp.zeros_like(dv_acc)
    for c in range(2):
        lanes = slice(c * HEAD_WIDTH, (c + 1) * HEAD_WIDTH)
        k, v = k_ref[:, lanes], v_ref[:, lanes]
        for h in range(2):
            at = slice((2 * c + h) * HEAD_WIDTH, (2 * c + h + 1) * HEAD_WIDTH)
            for b in range(SEQUENCE_LENGTH // BLOCK):
                n = (b + 1) * BLOCK
                rows = slice(b * BLOCK, (b + 1) * BLOCK)
                q, g = q_ref[rows, at], g_ref[rows, at]
                s = dot_nt(k[:n], q)
                dp = dot_nt(v[:n], g)
                p = jnp.exp(s - jnp.max(s, axis=0, keepdims=True))
                p = p * (1.0 / jnp.sum(p, axis=0, keepdims=True))
                ds = (p * (dp - jnp.sum(p * dp, axis=0, keepdims=True))).astype(BF16)
                dv_acc[:n, lanes] += dot(p.astype(BF16), g)
                dk_acc[:n, lanes] += dot(ds, q)
                dq_acc[rows, at] = dot_tn(ds, k[:n])
    cos, sin = cos_ref[...], -sin_ref[...]
    scale = HEAD_WIDTH**-0.5
    dq_ref[:, :LANES] = rope(dq_acc[:, :LANES] * scale, cos, sin).astype(BF16)
    dq_ref[:, LANES:] = rope(dq_acc[:, LANES:] * scale, cos, sin).astype(BF16)
    dk_ref[...] = rope(dk_acc[...], cos, sin).astype(BF16)
    dv_ref[...] = dv_acc[...].astype(BF16)


def attend_back(queries, keys, vals, grad, cos, sin, first=0, steps=KEY_VALUE_HEADS // 2, ties=()):
    rows = queries.shape[0]
    flops = 5 * QUERY_HEADS * rows * SEQUENCE_LENGTH * HEAD_WIDTH * 2 * steps // (KEY_VALUE_HEADS // 2)
    table = pl.BlockSpec((SEQUENCE_LENGTH, LANES), lambda s, i: (s, 0))

    def block(width, start):
        return pl.BlockSpec((SEQUENCE_LENGTH, width), lambda s, i: (s, i + start))

    two, four = block(2 * HEAD_WIDTH, first), block(4 * HEAD_WIDTH, first)
    out_two, out_four = block(2 * HEAD_WIDTH, 0), block(4 * HEAD_WIDTH, 0)
    return pl.pallas_call(
        tied(attend_back_kernel, 6, ties),
        grid=(rows // SEQUENCE_LENGTH, steps),
        in_specs=[four, two, two, four, table, table] + [ANY] * len(ties),
        out_specs=[out_four, out_two, out_two],
        out_shape=[jax.ShapeDtypeStruct((rows, steps * w), BF16) for w in (4 * HEAD_WIDTH, 2 * HEAD_WIDTH, 2 * HEAD_WIDTH)],
        scratch_shapes=[
            pltpu.VMEM((SEQUENCE_LENGTH, LANES), F32),
            pltpu.VMEM((SEQUENCE_LENGTH, LANES), F32),
            pltpu.VMEM((SEQUENCE_LENGTH, 2 * LANES), F32),
        ],
        compiler_params=params(),
        cost_estimate=cost(flops * 8, 12 * rows * 1024, QUERY_HEADS * rows * 640),
        name="attend_back",
    )(queries, keys, vals, grad, cos, sin, *ties)


def middle_kernel(lane_of, a_ref, w_ref, x_ref, gain_ref, router_ref, routes_ref, r_ref, m_ref, mt_ref, gates_ref):
    resid = x_ref[...].astype(F32) + dot(a_ref[...], w_ref[...])
    r_ref[...] = resid
    inverse = lax.rsqrt(jnp.mean(resid * resid, axis=-1, keepdims=True) + 1e-06)
    moe_in = (resid * inverse * gain_ref[lane_of : lane_of + 1].astype(F32)).astype(BF16)
    m_ref[...] = moe_in
    mt_ref[...] = moe_in.T
    logits = dot(moe_in, router_ref[...])
    lane = lax.broadcasted_iota(jnp.int32, logits.shape, 1)
    routes = routes_ref[...]
    picked = lane == routes[:, 0:1]
    for k in range(1, routes.shape[1]):
        picked = jnp.logical_or(picked, lane == routes[:, k : k + 1])
    logits = jnp.where(picked, logits, -1e30)
    weights = jnp.where(picked, jnp.exp(logits - jnp.max(logits, axis=-1, keepdims=True)), 0.0)
    gates_ref[...] = weights / jnp.sum(weights, axis=-1, keepdims=True)


def middle(attended, out_w, tokens, gain, lane, router_w, routes, ties=()):
    rows, width = tokens.shape
    return pl.pallas_call(
        tied(functools.partial(middle_kernel, lane), 6, ties),
        grid=(rows // TILE,),
        in_specs=[
            row_block(width),
            whole_block(out_w.shape),
            row_block(width),
            whole_block(gain.shape),
            whole_block(router_w.shape),
            row_block(routes.shape[1]),
        ]
        + [ANY] * len(ties),
        out_specs=[row_block(width), row_block(width), pl.BlockSpec((width, TILE), lambda i: (0, i)), row_block(LANES)],
        out_shape=[
            jax.ShapeDtypeStruct((rows, width), F32),
            jax.ShapeDtypeStruct((rows, width), BF16),
            jax.ShapeDtypeStruct((width, rows), BF16),
            jax.ShapeDtypeStruct((rows, LANES), F32),
        ],
        compiler_params=params(LESS_BYTES),
        cost_estimate=cost(2 * rows * width * (width + LANES), 14 * rows * width),
        name="middle",
    )(attended, out_w, tokens, gain, router_w, routes, *ties)


def moe_kernel(slots, chunks, first, ties, me_ref, *refs):
    refs = list(refs)
    take = lambda count: [refs.pop(0) for _ in range(count)]
    x, xt, dy, dyt, gates_ref = take(5)
    if not first:
        take(3)
    weights = [[take(count) for count in per_slot] for per_slot in chunks]
    take(ties)
    made, dmoe, gg_ref = take(3)
    grads = [take(2) for _ in slots]
    wg, wu, wd, hg, dg, du, stage, sem_w, sem_out = take(9)
    rows, width = x.shape
    step = 512

    def load(source, target, sem):
        copy = pltpu.make_async_copy(source, target, sem)
        copy.start()
        return copy

    def load_weights(index):
        buffer = index % 2
        out = []
        for which, target in enumerate((wg, wu, wd)):
            at, copies = 0, []
            for piece, ref in enumerate(weights[index][which]):
                count = ref.shape[0]
                copies.append(load(ref, target.at[buffer, at : at + count], sem_w.at[buffer, which, piece]))
                at += count
            out.append(copies)
        return out

    pending = {0: load_weights(0)}
    if first:
        gg_ref[...] = jnp.zeros_like(gg_ref)
    stores = []
    lane = lax.broadcasted_iota(jnp.int32, (step, LANES), 1)
    for index, slot in enumerate(slots):
        buffer = index % 2
        arriving = pending.pop(index)
        if index + 1 < len(slots):
            pending[index + 1] = load_weights(index + 1)
        me = me_ref[0] ^ slot
        g_w, u_w, d_w = wg.at[buffer], wu.at[buffer], wd.at[buffer]

        def arrived(which, lo):
            if lo == 0:
                for copy in arriving[which]:
                    copy.wait()

        for lo in range(0, rows, step):
            at = slice(lo, lo + step)
            arrived(0, lo)
            gate = dot(x[at], g_w[...])
            arrived(1, lo)
            upval = dot(x[at], u_w[...])
            arrived(2, lo)
            pre = dot_nt(dy[at], d_w[...])
            column = jnp.sum(jnp.where(lane == me, gates_ref[at], 0.0), axis=1, keepdims=True)
            sigma = 1.0 / (1.0 + jnp.exp(-gate))
            silu = gate * sigma
            hidden = silu * upval
            gained = jnp.sum(hidden * pre, axis=1, keepdims=True)
            gg_ref[at] = gg_ref[at] + jnp.where(lane == me, gained, 0.0)
            weighted = (hidden * column).astype(BF16)
            dhidden = pre * column
            dgate = (dhidden * upval * (sigma + silu * (1.0 - sigma))).astype(BF16)
            dup = (dhidden * silu).astype(BF16)
            hg[at], dg[at], du[at] = weighted, dgate, dup
            fresh = dot(weighted, d_w[...])
            back = dot_nt(dgate, g_w[...]) + dot_nt(dup, u_w[...])
            if first and index == 0:
                made[at], dmoe[at] = fresh, back
            else:
                made[at] += fresh
                dmoe[at] += back
        for copy in stores:
            copy.wait()
        stores = []
        half = width // 2
        for part in range(2):
            at = slice(part * half, (part + 1) * half)
            stage[0, at] = dot(xt[at], dg[...]).astype(BF16)
            stage[1, at] = dot(xt[at], du[...]).astype(BF16)
            stage[2, at] = dot(dyt[at], hg[...]).astype(BF16)
            stores.append(load(stage.at[:, at], grads[index][part], sem_out.at[part]))
    for copy in stores:
        copy.wait()


def moe(slots, me, moe_in, moe_in_t, dy, dy_t, gates, acc, weights, ties=()):
    rows, width = moe_in.shape
    hidden = weights[0][0][0].shape[1]
    first = acc is None
    flat = [piece for per_slot in weights for pieces in per_slot for piece in pieces]
    chunks = tuple(tuple(len(pieces) for pieces in per_slot) for per_slot in weights)
    held = [pltpu.with_memory_space_constraint(a, pltpu.VMEM) for a in (moe_in, moe_in_t, dy, dy_t, gates, *(acc or ()))]
    grad = jax.ShapeDtypeStruct((3, width // 2, hidden), BF16)
    outs = pl.pallas_call(
        functools.partial(moe_kernel, tuple(slots), chunks, first, len(ties)),
        in_specs=[pl.BlockSpec(memory_space=pltpu.SMEM)] + [VMEM] * len(held) + [ANY] * (len(flat) + len(ties)),
        out_specs=[VMEM, VMEM, VMEM] + [ANY] * (2 * len(slots)),
        out_shape=[pltpu.VMEM((rows, width), F32), pltpu.VMEM((rows, width), F32), pltpu.VMEM((rows, LANES), F32)]
        + [grad] * (2 * len(slots)),
        scratch_shapes=[
            pltpu.VMEM((2, width, hidden), BF16),
            pltpu.VMEM((2, width, hidden), BF16),
            pltpu.VMEM((2, hidden, width), BF16),
            pltpu.VMEM((rows, hidden), BF16),
            pltpu.VMEM((rows, hidden), BF16),
            pltpu.VMEM((rows, hidden), BF16),
            pltpu.VMEM((3, width, hidden), BF16),
            pltpu.SemaphoreType.DMA((2, 3, 2)),
            pltpu.SemaphoreType.DMA((2,)),
        ],
        input_output_aliases={} if first else {6: 0, 7: 1, 8: 2},
        compiler_params=pltpu.CompilerParams(vmem_limit_bytes=EXPERT_BYTES),
        cost_estimate=cost(18 * rows * width * hidden * len(slots), 20 * rows * width),
        name="experts",
    )(me, *held, *flat, *ties)
    return outs[:3], [tuple(outs[3 + 2 * i : 5 + 2 * i]) for i in range(len(slots))]


def turn_kernel(
    lane, resid_ref, made_ref, dmoe_ref, gates_ref, gg_ref, dy_ref, gain_ref, router_ref, mt_ref, w_ref,
    mixed_ref, dresid_ref, dz_ref, da_ref, gain_grad_ref, router_grad_ref,
):
    @pl.when(pl.program_id(0) == 0)
    def _():
        gain_grad_ref[...] = jnp.zeros_like(gain_grad_ref)
        router_grad_ref[...] = jnp.zeros_like(router_grad_ref)

    resid = resid_ref[...]
    mixed_ref[...] = (resid + made_ref[...]).astype(BF16)
    gates, gg = gates_ref[...], gg_ref[...]
    dlogits = (gates * (gg - jnp.sum(gates * gg, axis=1, keepdims=True))).astype(BF16)
    router_grad_ref[...] += dot(mt_ref[...], dlogits)
    dmoe = dmoe_ref[...] + dot_nt(dlogits, router_ref[...])
    inverse = lax.rsqrt(jnp.mean(resid * resid, axis=-1, keepdims=True) + 1e-06)
    gain_grad_ref[...] += jnp.sum(dmoe * resid * inverse, axis=0, keepdims=True)
    scaled = dmoe * gain_ref[lane : lane + 1].astype(F32)
    inner = jnp.mean(scaled * resid, axis=-1, keepdims=True)
    dresid = dy_ref[...].astype(F32) + inverse * scaled - resid * (inverse * inverse * inverse * inner)
    dresid_ref[...] = dresid
    dz = dresid.astype(BF16)
    dz_ref[...] = dz
    da_ref[...] = dot_nt(dz, w_ref[...]).astype(BF16)


def turn(resid, made, dmoe, gates, gg, dy, gain, lane, router_w, moe_in_t, out_w, ties=()):
    rows, width = resid.shape
    return pl.pallas_call(
        tied(functools.partial(turn_kernel, lane), 10, ties),
        grid=(rows // TILE,),
        in_specs=[
            row_block(width), row_block(width), row_block(width), row_block(LANES), row_block(LANES), row_block(width),
            whole_block(gain.shape), whole_block(router_w.shape), pl.BlockSpec((width, TILE), lambda i: (0, i)),
            whole_block(out_w.shape),
        ]
        + [ANY] * len(ties),
        out_specs=[row_block(width)] * 4 + [whole_block((1, width)), whole_block((width, LANES))],
        out_shape=[
            jax.ShapeDtypeStruct((rows, width), BF16),
            jax.ShapeDtypeStruct((rows, width), F32),
            jax.ShapeDtypeStruct((rows, width), BF16),
            jax.ShapeDtypeStruct((rows, width), BF16),
            jax.ShapeDtypeStruct((1, width), F32),
            jax.ShapeDtypeStruct((width, LANES), F32),
        ],
        compiler_params=params(LESS_BYTES),
        cost_estimate=cost(2 * rows * width * (width + 2 * LANES), 28 * rows * width),
        name="turn",
    )(resid, made, dmoe, gates, gg, dy, gain, router_w, moe_in_t, out_w, *ties)


def finish_kernel(lane, count, *refs):
    grads = refs[:count]
    w_ref, x_ref, dresid_ref, gain_ref, router_ref, second_ref, out_ref, small_ref, first = refs[count:]

    @pl.when(pl.program_id(0) == 0)
    def _():
        first[...] = jnp.zeros_like(first)

    at, dn = 0, 0.0
    for ref in grads:
        dn += dot_nt(ref[...], w_ref[:, at : at + ref.shape[1]])
        at += ref.shape[1]
    x = x_ref[...].astype(F32)
    inverse = lax.rsqrt(jnp.mean(x * x, axis=-1, keepdims=True) + 1e-06)
    first[...] += jnp.sum(dn * x * inverse, axis=0, keepdims=True)
    scaled = dn * gain_ref[lane : lane + 1].astype(F32)
    inner = jnp.mean(scaled * x, axis=-1, keepdims=True)
    out_ref[...] = dresid_ref[...] + inverse * scaled - x * (inverse * inverse * inverse * inner)

    @pl.when(pl.program_id(0) == pl.num_programs(0) - 1)
    def _():
        row = lax.broadcasted_iota(jnp.int32, (LANES, first.shape[1]), 0)
        gains = jnp.where(row == lane, first[...], 0.0) + jnp.where(row == lane + 1, second_ref[...], 0.0)
        small_ref[...] = (router_ref[...] + gains.T).astype(BF16)


def finish(grads, weights, tokens, dresid, gain, lane, router_grad, second, ties=()):
    rows, width = tokens.shape
    return pl.pallas_call(
        tied(functools.partial(finish_kernel, lane, len(grads)), len(grads) + 6, ties),
        grid=(rows // TILE,),
        in_specs=[row_block(g.shape[1]) for g in grads]
        + [whole_block(weights.shape), row_block(width), row_block(width), whole_block(gain.shape)]
        + [whole_block(router_grad.shape), whole_block(second.shape)]
        + [ANY] * len(ties),
        out_specs=[row_block(width), whole_block((width, LANES))],
        out_shape=[jax.ShapeDtypeStruct((rows, width), F32), jax.ShapeDtypeStruct((width, LANES), BF16)],
        scratch_shapes=[pltpu.VMEM((1, width), F32)],
        compiler_params=params(),
        cost_estimate=cost(1, 1),
        name="finish",
    )(*grads, weights, tokens, dresid, gain, router_grad, second, *ties)


def weights_back_kernel(count, *refs):
    for grad, out in zip(refs[1 : count + 1], refs[count + 1 :]):
        out[...] = dot(refs[0][...], grad[...]).astype(BF16)


def weights_back(turned, grads, ties=()):
    rows = turned.shape[0]
    return pl.pallas_call(
        tied(functools.partial(weights_back_kernel, len(grads)), len(grads) + 1, ties),
        grid=(rows // TILE,),
        in_specs=[row_block(turned.shape[1])] + [whole_block(g.shape) for g in grads] + [ANY] * len(ties),
        out_specs=[row_block(g.shape[1]) for g in grads],
        out_shape=[jax.ShapeDtypeStruct((rows, g.shape[1]), BF16) for g in grads],
        compiler_params=params(),
        cost_estimate=cost(1, 1),
        name="weights_back",
    )(turned, *grads, *ties)


def widen_kernel(top_ref, bottom_ref, gate_ref, up_ref, down_ref):
    step = pl.program_id(0)
    for half, ref in enumerate((top_ref, bottom_ref)):

        @pl.when(step // 2 == half)
        def _():
            gate_ref[...] = ref[0].astype(F32)
            up_ref[...] = ref[1].astype(F32)
            down_ref[...] = ref[2].astype(F32).T


def widen(top, bottom):
    _, rows, columns = top.shape
    step = rows // 2
    block = pl.BlockSpec((step, columns), lambda i: (i, 0))
    return pl.pallas_call(
        widen_kernel,
        grid=(4,),
        in_specs=[
            pl.BlockSpec((3, step, columns), lambda i: (0, jnp.minimum(i, 1), 0)),
            pl.BlockSpec((3, step, columns), lambda i: (0, jnp.maximum(i - 2, 0), 0)),
        ],
        out_specs=[block, block, pl.BlockSpec((columns, step), lambda i: (0, i))],
        out_shape=[
            jax.ShapeDtypeStruct((2 * rows, columns), F32),
            jax.ShapeDtypeStruct((2 * rows, columns), F32),
            jax.ShapeDtypeStruct((columns, 2 * rows), F32),
        ],
        compiler_params=params(),
        cost_estimate=cost(1, 1),
        name="widen",
    )(top, bottom)


def plus_kernel(counts, *refs):
    refs = list(refs)
    refs.pop()[...] = jnp.zeros((8, LANES), F32)
    ins = [[refs.pop(0) for _ in range(count)] for count in counts]
    for terms, out in zip(ins, refs):
        total = terms[0][...].astype(F32)
        for ref in terms[1:]:
            total += ref[...].astype(F32)
        out[...] = total.astype(BF16)


def plus(*groups, ties=()):
    shape = groups[0][0].shape
    block = pl.BlockSpec((1, shape[1] // 2, shape[2]), lambda i, j: (i, j, 0))
    counts = tuple(len(terms) for terms in groups)
    flat = [a for terms in groups for a in terms]
    return pl.pallas_call(
        tied(functools.partial(plus_kernel, counts), len(flat), ties),
        grid=(shape[0], 2),
        in_specs=[block] * len(flat) + [ANY] * len(ties),
        out_specs=[block] * len(groups) + [pl.BlockSpec((8, LANES), lambda i, j: (0, 0))],
        out_shape=[jax.ShapeDtypeStruct(shape, BF16)] * len(groups) + [jax.ShapeDtypeStruct((8, LANES), F32)],
        compiler_params=pltpu.CompilerParams(vmem_limit_bytes=16 * 1024 * 1024),
        cost_estimate=cost(len(flat) * flat[0].size, 2 * (len(flat) + len(groups)) * flat[0].size),
        name="plus",
    )(*flat, *ties)


def gather_kernel(size, count, *refs):
    q_ref, k_ref, v_ref, s_ref, o_ref, d_ref = refs[:6]
    owned, refs = refs[6 : 6 + count], refs[6 + count :]
    packed_ref, small_ref, out_ref, down_ref, turned_ref = refs[:5]
    beside, refs = refs[5 : 5 + 2 * count], refs[5 + 2 * count :]
    beyond, refs = refs[: 2 * count], refs[2 * count :]
    pair, refs = refs[: count + 1 if count else 0], refs[count + 1 if count else 0 :]
    send_sem, recv_sem, pass_sem, take_sem, away_sem, come_sem, over_sem, land_sem = refs
    me, z = lax.axis_index("expert"), lax.axis_index("wshard")
    core = lax.rem(me, 2)
    sibling = me + 1 - 2 * core
    rows = q_ref.shape[0]
    half = rows // 2
    there = lambda step: jnp.logical_and(z + step >= 0, z + step < size)

    barrier = pltpu.get_barrier_semaphore()
    pl.semaphore_signal(barrier, inc=1, device_id=(sibling, z), device_id_type=pl.DeviceIdType.MESH)
    for step in (1, -1):

        @pl.when(there(step))
        def _():
            pl.semaphore_signal(barrier, inc=1, device_id=(me, z + step), device_id_type=pl.DeviceIdType.MESH)

    neighbours = []
    if count:
        xb, yb = lax.rem(me // 2, 2), me // 4
        neighbours = [me + 2 - 4 * xb, me + 4 - 8 * yb]
    for peer in neighbours:
        pl.semaphore_signal(barrier, inc=1, device_id=(peer, z), device_id_type=pl.DeviceIdType.MESH)
    pl.semaphore_wait(barrier, 1 + len(neighbours) + jnp.where(z > 0, 1, 0) + jnp.where(z < size - 1, 1, 0))
    shipped = []
    for i, ref in enumerate(owned):
        for j, peer in enumerate(neighbours):
            shipped.append(
                pltpu.make_async_remote_copy(
                    src_ref=ref, dst_ref=beside[j * count + i], send_sem=away_sem.at[i, j], recv_sem=come_sem.at[i, j],
                    device_id=(peer, z), device_id_type=pl.DeviceIdType.MESH,
                )
            )
    for copy in shipped:
        copy.start()

    def passed(source, target, i, j):
        return pltpu.make_async_remote_copy(
            src_ref=source, dst_ref=target, send_sem=over_sem.at[i, j], recv_sem=land_sem.at[i, j],
            device_id=(sibling, z), device_id_type=pl.DeviceIdType.MESH,
        )

    swapped = [passed(ref, target, i, 2) for i, (ref, target) in enumerate(zip(owned, pair))]

    own = pl.ds(pl.multiple_of(z * rows, rows), rows)
    at = 0
    for ref in (q_ref, k_ref, v_ref):
        packed_ref[own, at : at + ref.shape[1]] = ref[...]
        at += ref.shape[1]
    small_ref[own] = s_ref[...]
    out_ref[...] = o_ref[...]
    down_ref[...] = d_ref[...]
    if count:
        swapped.append(passed(down_ref, pair[count], count, 2))
    for copy in swapped:
        copy.start()

    def moves(way, hop, origin, which, device, send, recv):
        at = pl.ds(pl.multiple_of(origin * rows + which * half, half), half)
        return [
            pltpu.make_async_remote_copy(
                src_ref=ref.at[at], dst_ref=ref.at[at], send_sem=send.at[way, hop, i], recv_sem=recv.at[way, hop, i],
                device_id=device, device_id_type=pl.DeviceIdType.MESH,
            )
            for i, ref in enumerate((packed_ref, small_ref))
        ]

    def onward(way, step, hop):
        return moves(way, hop, z - step * (hop - 1), core, (me, z + step), send_sem, recv_sem)

    def across(way, step, hop, which):
        return moves(way, hop, z - step * hop, which, (sibling, z), pass_sem, take_sem)

    ways = ((0, 1), (1, -1))
    for way, step in ways:

        @pl.when(there(step))
        def _():
            for move in onward(way, step, 1):
                move.start()

    for hop in range(1, size):
        for way, step in ways:

            @pl.when(there(-step * hop))
            def _():
                for move in moves(way, hop, z - step * hop, core, (me, z), send_sem, recv_sem):
                    move.wait_recv()

                @pl.when(there(step))
                def _():
                    for move in onward(way, step, hop + 1):
                        move.start()

                for move in across(way, step, hop, core):
                    move.start()

    for hop in range(1, size):
        for way, step in ways:

            @pl.when(there(-step * hop))
            def _():
                for move in across(way, step, hop, 1 - core):
                    move.wait_recv()
                for move in across(way, step, hop, core):
                    move.wait_send()

            @pl.when(jnp.logical_and(there(step), there(-step * (hop - 1))))
            def _():
                for move in onward(way, step, hop):
                    move.wait_send()

    turned_ref[...] = small_ref[...].T
    onto = []
    for n, copy in enumerate(shipped):
        i, j = n // 2, n % 2
        copy.wait_recv()
        onto.append(passed(beside[j * count + i], beyond[j * count + i], i, j))
        onto[-1].start()
    for copy in shipped:
        copy.wait_send()
    for copy in swapped + onto:
        copy.wait()


def gather_weights(query, key, value, small, out, down, owned=()):
    size = lax.axis_size("wshard")
    rows = query.shape[0]
    width = query.shape[1] + key.shape[1] + value.shape[1]
    sems = pltpu.SemaphoreType.DMA((2, size + 1, 2))
    last = [*owned, down] if len(owned) else []
    return pl.pallas_call(
        functools.partial(gather_kernel, size, len(owned)),
        in_specs=[VMEM] * 6 + [ANY] * len(owned),
        out_specs=[VMEM] * 5 + [ANY] * (4 * len(owned) + len(last)),
        out_shape=[
            jax.ShapeDtypeStruct((size * rows, width), BF16),
            jax.ShapeDtypeStruct((size * rows, small.shape[1]), BF16),
            jax.ShapeDtypeStruct(out.shape, BF16),
            jax.ShapeDtypeStruct(down.shape, BF16),
            jax.ShapeDtypeStruct((small.shape[1], size * rows), BF16),
        ]
        + [jax.ShapeDtypeStruct(a.shape, BF16) for a in owned] * 4
        + [jax.ShapeDtypeStruct(a.shape, BF16) for a in last],
        scratch_shapes=[sems, sems, sems, sems] + [pltpu.SemaphoreType.DMA((len(owned) + 1, 3))] * 4,
        compiler_params=pltpu.CompilerParams(collective_id=0, has_side_effects=True, vmem_limit_bytes=VMEM_BYTES),
        cost_estimate=cost(1e9, 12 * rows * size * width),
        name="gather_weights",
    )(query, key, value, small, out, down, *owned)


def reduce_kernel(size, columns, *refs):
    count = sum(len(widths) for widths in columns)
    ins, outs = list(refs[:count]), refs[count : count + len(columns)]
    acc, rc, r1, r2, zs, rz, res, send_sem, recv_sem = refs[count + len(columns) :]
    me, z = lax.axis_index("expert"), lax.axis_index("wshard")
    core, xb, yb = lax.rem(me, 2), lax.rem(me // 2, 2), me // 4
    sibling, xp, yp = me + 1 - 2 * core, me + 2 - 4 * xb, me + 4 - 8 * yb
    half = ins[0].shape[1] // 2
    n1, n2 = half // 4, half // 8

    barrier = pltpu.get_barrier_semaphore()
    for peer in (sibling, xp, yp):
        pl.semaphore_signal(barrier, inc=1, device_id=(peer, z), device_id_type=pl.DeviceIdType.MESH)
    for d in range(1, size):
        pl.semaphore_signal(barrier, inc=1, device_id=(me, lax.rem(z + d, size)), device_id_type=pl.DeviceIdType.MESH)
    pl.semaphore_wait(barrier, 2 + size)

    pieces, at = [], 0
    for out, widths in zip(outs, columns):
        start = 0
        for width in widths:
            ref, step = ins.pop(0), min(width, 512)
            for lo in range(0, width, step):
                pieces.append((ref, out, lo, step, at, start + lo))
                at += step
            start += width

    sent = []

    def move(source, target, piece, kind, device):
        copy = pltpu.make_async_remote_copy(
            src_ref=source, dst_ref=target, send_sem=send_sem.at[kind, piece], recv_sem=recv_sem.at[kind, piece],
            device_id=device, device_id_type=pl.DeviceIdType.MESH,
        )
        copy.start()
        sent.append(copy)
        return copy

    def rows(start, length):
        return pl.ds(pl.multiple_of(start, 16), length)

    def sum_of(*terms):
        total = terms[0].astype(F32)
        for term in terms[1:]:
            total += term.astype(F32)
        return total

    k0, k1 = xb * n1 + yb * n2, half // 2 + yb * n1 + xb * n2
    base = core * half
    first = []
    for p, (ref, _, lo, w, at, _) in enumerate(pieces):
        first.append(move(ref.at[:, rows((1 - core) * half, half), lo : lo + w], rc.at[:, :, at : at + w], p, 0, (sibling, z)))
    second = []
    for p, (ref, _, lo, w, at, _) in enumerate(pieces):
        c = slice(at, at + w)
        first[p].wait_recv()
        acc[:, :, c] = sum_of(ref[:, rows(base, half), lo : lo + w], rc[:, :, c]).astype(BF16)
        second.append((
            move(acc.at[:, rows((1 - xb) * n1, n1), c], r1.at[0, :, :, c], p, 1, (xp, z)),
            move(acc.at[:, rows(half // 2 + (1 - yb) * n1, n1), c], r1.at[1, :, :, c], p, 2, (yp, z)),
        ))
    third = []
    for p, (_, _, _, w, at, _) in enumerate(pieces):
        c = slice(at, at + w)
        keep = (rows(xb * n1, n1), rows(half // 2 + yb * n1, n1))
        for i in range(2):
            second[p][i].wait_recv()
            acc[:, keep[i], c] = sum_of(acc[:, keep[i], c], r1[i, :, :, c]).astype(BF16)
        third.append((
            move(acc.at[:, rows(xb * n1 + (1 - yb) * n2, n2), c], r2.at[0, :, :, c], p, 3, (yp, z)),
            move(acc.at[:, rows(half // 2 + yb * n1 + (1 - xb) * n2, n2), c], r2.at[1, :, :, c], p, 4, (xp, z)),
        ))
    fourth = []
    for p, (_, _, _, w, at, _) in enumerate(pieces):
        c = slice(at, at + w)
        for i, k in enumerate((k0, k1)):
            third[p][i].wait_recv()
            zs[:, i * n2 : (i + 1) * n2, c] = sum_of(acc[:, rows(k, n2), c], r2[i, :, :, c]).astype(BF16)
        fourth.append([
            move(zs.at[lax.rem(z + d, size), :, c], rz.at[d - 1, :, c], p, 8 + d, (me, lax.rem(z + d, size)))
            for d in range(1, size)
        ])
    fifth = []
    for p, (_, _, _, w, at, _) in enumerate(pieces):
        c = slice(at, at + w)
        for copy in fourth[p]:
            copy.wait_recv()
        total = sum_of(zs[z, :, c], *[rz[d, :, c] for d in range(size - 1)]).astype(BF16)
        for i, k in enumerate((k0, k1)):
            res[rows(base + k, n2), c] = total[i * n2 : (i + 1) * n2]
        fifth.append((
            move(res.at[rows(base + k0, n2), c], res.at[rows(base + k0, n2), c], p, 5, (yp, z)),
            move(res.at[rows(base + k1, n2), c], res.at[rows(base + k1, n2), c], p, 6, (xp, z)),
        ))
    sixth = []
    for p, (_, _, _, w, at, _) in enumerate(pieces):
        c = slice(at, at + w)
        for copy in fifth[p]:
            copy.wait_recv()
        mine = rows(base + xb * n1, n1), rows(base + half // 2 + yb * n1, n1)
        sixth.append((
            move(res.at[mine[0], c], res.at[mine[0], c], p, 7, (xp, z)),
            move(res.at[mine[1], c], res.at[mine[1], c], p, 8, (yp, z)),
        ))
    last = []
    for p, (_, _, _, w, at, _) in enumerate(pieces):
        c = slice(at, at + w)
        for copy in sixth[p]:
            copy.wait_recv()
        last.append(move(res.at[rows(base, half), c], res.at[rows(base, half), c], p, 8 + size, (sibling, z)))
    for p, (_, out, _, w, at, to) in enumerate(pieces):
        last[p].wait_recv()
        out[:, to : to + w] = res[:, at : at + w].astype(F32)
    for copy in sent:
        copy.wait_send()


def reduce_all(*groups):
    size = lax.axis_size("wshard")
    rows = groups[0][0].shape[0] // size
    grads = [g for group in groups for g in group]
    columns = tuple(tuple(g.shape[1] for g in group) for group in groups)
    count = sum(-(-g.shape[1] // 512) for g in grads)
    width, half = sum(g.shape[1] for g in grads), rows // 2
    return pl.pallas_call(
        functools.partial(reduce_kernel, size, columns),
        in_specs=[VMEM] * len(grads),
        out_specs=[VMEM] * len(groups),
        out_shape=[jax.ShapeDtypeStruct((rows, sum(widths)), F32) for widths in columns],
        scratch_shapes=[
            pltpu.VMEM((size, half, width), BF16),
            pltpu.VMEM((size, half, width), BF16),
            pltpu.VMEM((2, size, half // 4, width), BF16),
            pltpu.VMEM((2, size, half // 8, width), BF16),
            pltpu.VMEM((size, half // 4, width), BF16),
            pltpu.VMEM((size - 1, half // 4, width), BF16),
            pltpu.VMEM((rows, width), BF16),
            pltpu.SemaphoreType.DMA((9 + size, count)),
            pltpu.SemaphoreType.DMA((9 + size, count)),
        ],
        compiler_params=pltpu.CompilerParams(collective_id=1, has_side_effects=True, vmem_limit_bytes=VMEM_BYTES),
        cost_estimate=cost(1, 1),
        name="reduce_all",
    )(*[g.reshape(size, rows, g.shape[1]) for g in grads])


def flip(value, axis, bit):
    size = lax.axis_size(axis)
    return lax.ppermute(value, axis, [(i, i ^ bit) for i in range(size)])


def gather_experts(mats, owners):
    slots, bit = {0: tuple([m] for m in mats)}, 2
    while bit < owners:
        for j in sorted(slots):
            slots[j | bit] = tuple([flip(p, "expert", bit) for p in m] for m in slots[j])
        bit *= 2
    return slots


def third_slot(a, b):
    cut = a[2][0].shape[0] // 2
    return (
        [flip(a[0][0], "expert", 4)],
        [flip(b[1][0], "expert", 2)],
        [flip(a[2][0][:cut], "expert", 4), flip(b[2][0][cut:], "expert", 2)],
    )


def across_core(slot):
    return tuple([flip(p, "expert", 1) for p in m] for m in slot)


def add(a, b):
    return (a.astype(F32) + b.astype(F32)).astype(BF16)


def reduce_experts(parts, owners):
    bit = 1
    while bit < owners:
        for j in sorted(parts, reverse=True):
            if j & bit:
                gone = parts.pop(j)
                parts[j ^ bit] = tuple(add(m, flip(s, "expert", bit)) for m, s in zip(parts[j ^ bit], gone))
        bit *= 2
    return parts[0]


def on_device(
    tokens, gain_attn, w_query, key_weight, value_weight, w_out, gain_ffn, w_router, w_gate, w_up, w_down, routes, cotangent
):
    owners = lax.axis_size("expert")
    me = lax.axis_index("expert").astype(jnp.int32)[None]
    rows, width = tokens.shape
    experts = w_router.shape[1]
    mats = (w_gate[0], w_up[0], w_down[0])

    small = jnp.concatenate([w_router, gain_attn[:, None], gain_ffn[:, None]], axis=1)
    small = jnp.pad(small, ((0, 0), (0, LANES - small.shape[1])))
    packed, small, out_shard, down, gains, *beside = gather_weights(
        w_query, key_weight, value_weight, small, w_out, mats[2], mats[:2] if owners == 8 else ()
    )
    out_w = lax.all_gather(out_shard, "wshard", axis=0, tiled=True)
    cos, sin = (jnp.asarray(a) for a in rope_tables(rows))

    if owners == 8:
        slots = {0: tuple([m] for m in mats)}
        slots[2] = ([beside[0]], [beside[1]], [flip(down, "expert", 2)])
        slots[4] = ([beside[2]], [beside[3]], [flip(down, "expert", 4)])
        slots[6] = third_slot(slots[2], slots[4])
    else:
        slots = gather_experts(mats, owners)
    normed_t, queries, keys, vals = project(tokens, gains, experts, packed, cos, sin)
    def pieces_of(*which, first=0, last=3):
        return [p for j in which for m in slots[j][first:last] for p in m] if owners == 8 else []

    attended = attend(queries, keys, vals)
    if owners == 8:
        slots[1] = tuple([m] for m in beside[8:])
        downs = lax.optimization_barrier((slots[2][2][0], slots[4][2][0], attended))
        slots[3] = ([beside[4]], [beside[5]], [flip(downs[0], "expert", 1)])
        slots[5] = ([beside[6]], [beside[7]], [flip(downs[1], "expert", 1)])
        slots[7] = across_core(slots[6])
    else:
        for j in sorted(slots):
            slots[j | 1] = across_core(slots[j])
    resid, moe_in, moe_in_t, gates = middle(
        attended, out_w, tokens, gains, experts + 1, small, routes, pieces_of(2, 4)
    )
    dy_t = cotangent.T

    def one(j, acc, ties=()):
        acc, (halves,) = moe([j], me, moe_in, moe_in_t, cotangent, dy_t, gates, acc, [slots[j]], ties)
        return acc, halves

    def turned(acc, ties=()):
        made, dmoe, gate_grads = acc
        return turn(
            resid, made, dmoe, gates, gate_grads, cotangent, gains, experts + 1, small, moe_in_t, out_w, ties
        )

    if owners == 8:
        core = lambda halves: [flip(m, "expert", 1) for m in halves]
        over_x = lambda m: flip(m, "expert", 2)
        over_y = lambda m: flip(m, "expert", 4)
        acc, g3 = one(3, None, pieces_of(6))
        c3 = core(g3)
        acc, g2 = one(2, acc)
        *s2, t2 = plus((g2[0], c3[0]), (g2[1], c3[1]))
        x20 = over_x(s2[0])
        acc, g7 = one(7, acc, [t2])
        c7 = core(g7)
        acc, g6 = one(6, acc)
        *s6, t6 = plus((g6[0], c7[0]), (g6[1], c7[1]))
        x60, y61 = over_x(s6[0]), over_y(s6[1])
        acc, g5 = one(5, acc, [t6])
        c5 = core(g5)
        acc, g4 = one(4, acc, [x20])
        *s4, t4 = plus((g4[0], c5[0]), (g4[1], c5[1]))
        y41 = over_y(s4[1])
        acc, g1 = one(1, acc, [t4])
        c1 = core(g1)
        left, right, sides = plus((s4[0], x60), (s2[1], y61))
        x21, y40 = over_x(right), over_y(left)
        acc, g0 = one(0, acc, [sides])
        *s0, t0 = plus((g0[0], c1[0]), (g0[1], c1[1]))
        mixed, dresid, dz, dattended, gain_two_grad, router_grad = turned(acc, [t0])
        out_grad = dot_tn(attended, dz).astype(BF16)
        early = attend_back(queries, keys, vals, dattended, cos, sin, 0, 2, [out_grad])
        top, bottom, both = plus((s0[0], x20, y40), (s0[1], y41, x21), ties=early[2:])
        late = attend_back(queries, keys, vals, dattended, cos, sin, 2, 2, [both])
        top, bottom = lax.psum((top, bottom), "wshard")
        pieces = [early[0], late[0], early[1], late[1], early[2], late[2]]
        weight_grads = weights_back(normed_t, pieces)
        own, after = [top, bottom], []
    else:
        acc, parts = None, {}
        for j in range(owners):
            acc, parts[j] = one(j, acc)
        mixed, dresid, dz, dattended, gain_two_grad, router_grad = turned(acc)
        own, after = lax.psum(tuple(reduce_experts(parts, owners)), "wshard"), []
        out_grad = dot_tn(attended, dz).astype(BF16)
        pieces = attend_back(queries, keys, vals, dattended, cos, sin)
        weight_grads = weights_back(normed_t, pieces)
    d_tokens, small_grad = finish(pieces, packed, tokens, dresid, gains, experts, router_grad, gain_two_grad, after)
    third = len(weight_grads) // 3
    groups = [[out_grad]] + [weight_grads[i : i + third] for i in range(0, 3 * third, third)] + [[small_grad]]
    if owners == 8:
        sums = reduce_all(*groups)
    else:
        total = lambda g: lax.psum(lax.psum_scatter(g, "wshard", scatter_dimension=0, tiled=True), "expert")
        sums = [total(jnp.concatenate(group, axis=1)).astype(F32) for group in groups]
    out_grad, query_grad, key_grad, value_grad, small_grad = sums
    gate_grad, up_grad, down_grad = widen(*own)
    return (
        mixed,
        d_tokens,
        small_grad[:, experts],
        query_grad,
        key_grad,
        value_grad,
        out_grad,
        small_grad[:, experts + 1],
        small_grad[:, :experts],
        gate_grad[None],
        up_grad[None],
        down_grad[None],
    )


def solution(mesh):
    whole, shard, matrix, owned = P(("expert", "wshard"), None), P("wshard"), P("wshard", None), P("expert", None, None)
    return jax.shard_map(
        on_device,
        mesh=mesh,
        in_specs=(whole, shard, matrix, matrix, matrix, matrix, shard, matrix, owned, owned, owned, whole, whole),
        out_specs=(whole, whole, shard, matrix, matrix, matrix, matrix, shard, matrix, owned, owned, owned),
        check_vma=False,
    )
```

```python
import functools
import jax
import jax.numpy as jnp
import numpy as np
from jax import lax
from jax.experimental import pallas as pl
from jax.experimental.pallas import tpu as pltpu
from jax.sharding import PartitionSpec as P

QUERY_HEADS = 16
KEY_VALUE_HEADS = 8
HEAD_WIDTH = 64
SEQUENCE_LENGTH = 1024
BLOCK = 256
TILE = 256
LANES = 128
F32 = jnp.float32
BF16 = jnp.bfloat16
ANY = pl.BlockSpec(memory_space=pl.ANY)
VMEM = pl.BlockSpec(memory_space=pltpu.VMEM)
VMEM_BYTES = 60 * 1024 * 1024
LESS_BYTES = 30 * 1024 * 1024
EXPERT_BYTES = 43 * 1024 * 1024


def dot(a, b):
    return jnp.dot(a, b, preferred_element_type=F32)


def dot_nt(a, b):
    return lax.dot_general(a, b, (((1,), (1,)), ((), ())), preferred_element_type=F32)


def dot_tn(a, b):
    return lax.dot_general(a, b, (((0,), (0,)), ((), ())), preferred_element_type=F32)


def params(size=VMEM_BYTES):
    return pltpu.CompilerParams(vmem_limit_bytes=size)


def cost(flops, nbytes, transcendentals=0):
    return pl.CostEstimate(flops=int(flops), bytes_accessed=int(nbytes), transcendentals=int(transcendentals))


def rope_tables(rows):
    half = HEAD_WIDTH // 2
    freq = np.exp(-np.log(10000.0) * np.arange(half, dtype=np.float32) * 2.0 / HEAD_WIDTH).astype(np.float32)
    pos = (np.arange(rows) % SEQUENCE_LENGTH).astype(np.float32)
    angles = (pos[:, None] * freq[None, :]).astype(np.float32)
    cos, sin = np.cos(angles), np.sin(angles)
    return (
        np.concatenate([cos, cos, cos, cos], 1).astype(np.float32),
        np.concatenate([-sin, sin, -sin, sin], 1).astype(np.float32),
    )


def rope(u, cos, sin):
    half = HEAD_WIDTH // 2
    lane = lax.broadcasted_iota(jnp.int32, u.shape, 1)
    swapped = jnp.where(
        lane % HEAD_WIDTH < half, pltpu.roll(u, LANES - half, 1), pltpu.roll(u, half, 1)
    )
    return u * cos + swapped * sin


def row_block(width):
    return pl.BlockSpec((TILE, width), lambda i: (i, 0))


def whole_block(shape):
    return pl.BlockSpec(shape, lambda i: (0,) * len(shape))


def tied(kernel, inputs, ties):
    return lambda *refs: kernel(*refs[:inputs], *refs[inputs + len(ties) :])


def project_kernel(lane, x_ref, gain_ref, w_ref, cos_ref, sin_ref, n_ref, q_ref, k_ref, v_ref):
    x = x_ref[...].astype(F32)
    inverse = lax.rsqrt(jnp.mean(x * x, axis=-1, keepdims=True) + 1e-06)
    normed = (x * inverse * gain_ref[lane : lane + 1].astype(F32)).astype(BF16)
    n_ref[...] = normed.T
    cos, sin = cos_ref[...], sin_ref[...]
    step = 512
    for at in range(0, w_ref.shape[1], step):
        made = dot(normed, w_ref[:, at : at + step])
        for lo in range(0, step, LANES):
            u = made[:, lo : lo + LANES]
            c = at + lo
            if c < q_ref.shape[1]:
                q_ref[:, c : c + LANES] = (rope(u, cos, sin).astype(BF16) * jnp.asarray(HEAD_WIDTH**-0.5, BF16))
            elif c < q_ref.shape[1] + k_ref.shape[1]:
                c -= q_ref.shape[1]
                k_ref[:, c : c + LANES] = rope(u, cos, sin).astype(BF16)
            else:
                c -= q_ref.shape[1] + k_ref.shape[1]
                v_ref[:, c : c + LANES] = u.astype(BF16)


def project(tokens, gain, lane, weights, cos, sin):
    rows, width = tokens.shape
    qw, kw = QUERY_HEADS * HEAD_WIDTH, KEY_VALUE_HEADS * HEAD_WIDTH
    return pl.pallas_call(
        functools.partial(project_kernel, lane),
        grid=(rows // TILE,),
        in_specs=[row_block(width), whole_block(gain.shape), whole_block(weights.shape), row_block(LANES), row_block(LANES)],
        out_specs=[pl.BlockSpec((width, TILE), lambda i: (0, i)), row_block(qw), row_block(kw), row_block(kw)],
        out_shape=[jax.ShapeDtypeStruct(s, BF16) for s in ((width, rows), (rows, qw), (rows, kw), (rows, kw))],
        compiler_params=params(),
        cost_estimate=cost(2 * rows * width * (qw + 2 * kw), 12 * rows * width),
        name="project",
    )(tokens, gain, weights, cos, sin)


def attend_kernel(q_ref, k_ref, v_ref, o_ref):
    for c in range(2):
        k = k_ref[:, c * HEAD_WIDTH : (c + 1) * HEAD_WIDTH]
        v = v_ref[:, c * HEAD_WIDTH : (c + 1) * HEAD_WIDTH]
        for h in range(2):
            at = (2 * c + h) * HEAD_WIDTH
            for b in range(SEQUENCE_LENGTH // BLOCK):
                n = (b + 1) * BLOCK
                rows = slice(b * BLOCK, (b + 1) * BLOCK)
                s = dot_nt(q_ref[rows, at : at + HEAD_WIDTH], k[:n])
                p = jnp.exp(s - jnp.max(s, axis=-1, keepdims=True))
                total = jnp.sum(p, axis=-1, keepdims=True)
                o = dot((p * (1.0 / total)).astype(BF16), v[:n])
                o_ref[rows, at : at + HEAD_WIDTH] = o.astype(BF16)


def head_block(width, sequence=SEQUENCE_LENGTH):
    return pl.BlockSpec((sequence, width), lambda s, i: (s, i))


def attend(queries, keys, vals, ties=()):
    rows = queries.shape[0]
    steps = KEY_VALUE_HEADS // 2
    flops = 2 * QUERY_HEADS * rows * SEQUENCE_LENGTH * HEAD_WIDTH * 2
    return pl.pallas_call(
        tied(attend_kernel, 3, ties),
        grid=(rows // SEQUENCE_LENGTH, steps),
        in_specs=[head_block(4 * HEAD_WIDTH), head_block(2 * HEAD_WIDTH), head_block(2 * HEAD_WIDTH)] + [ANY] * len(ties),
        out_specs=head_block(4 * HEAD_WIDTH),
        out_shape=jax.ShapeDtypeStruct(queries.shape, BF16),
        compiler_params=params(),
        cost_estimate=cost(flops * 8, 6 * rows * 1024, QUERY_HEADS * rows * 640),
        name="attend",
    )(queries, keys, vals, *ties)


def attend_back_kernel(q_ref, k_ref, v_ref, g_ref, cos_ref, sin_ref, dq_ref, dk_ref, dv_ref, dk_acc, dv_acc, dq_acc):
    dk_acc[...] = jnp.zeros_like(dk_acc)
    dv_acc[...] = jnp.zeros_like(dv_acc)
    for c in range(2):
        lanes = slice(c * HEAD_WIDTH, (c + 1) * HEAD_WIDTH)
        k, v = k_ref[:, lanes], v_ref[:, lanes]
        for h in range(2):
            at = slice((2 * c + h) * HEAD_WIDTH, (2 * c + h + 1) * HEAD_WIDTH)
            for b in range(SEQUENCE_LENGTH // BLOCK):
                n = (b + 1) * BLOCK
                rows = slice(b * BLOCK, (b + 1) * BLOCK)
                q, g = q_ref[rows, at], g_ref[rows, at]
                s = dot_nt(k[:n], q)
                dp = dot_nt(v[:n], g)
                p = jnp.exp(s - jnp.max(s, axis=0, keepdims=True))
                p = p * (1.0 / jnp.sum(p, axis=0, keepdims=True))
                ds = (p * (dp - jnp.sum(p * dp, axis=0, keepdims=True))).astype(BF16)
                dv_acc[:n, lanes] += dot(p.astype(BF16), g)
                dk_acc[:n, lanes] += dot(ds, q)
                dq_acc[rows, at] = dot_tn(ds, k[:n])
    cos, sin = cos_ref[...], -sin_ref[...]
    scale = HEAD_WIDTH**-0.5
    dq_ref[:, :LANES] = rope(dq_acc[:, :LANES] * scale, cos, sin).astype(BF16)
    dq_ref[:, LANES:] = rope(dq_acc[:, LANES:] * scale, cos, sin).astype(BF16)
    dk_ref[...] = rope(dk_acc[...], cos, sin).astype(BF16)
    dv_ref[...] = dv_acc[...].astype(BF16)


def attend_back(queries, keys, vals, grad, cos, sin, first=0, steps=KEY_VALUE_HEADS // 2, ties=()):
    rows = queries.shape[0]
    flops = 5 * QUERY_HEADS * rows * SEQUENCE_LENGTH * HEAD_WIDTH * 2 * steps // (KEY_VALUE_HEADS // 2)
    table = pl.BlockSpec((SEQUENCE_LENGTH, LANES), lambda s, i: (s, 0))

    def block(width, start):
        return pl.BlockSpec((SEQUENCE_LENGTH, width), lambda s, i: (s, i + start))

    two, four = block(2 * HEAD_WIDTH, first), block(4 * HEAD_WIDTH, first)
    out_two, out_four = block(2 * HEAD_WIDTH, 0), block(4 * HEAD_WIDTH, 0)
    return pl.pallas_call(
        tied(attend_back_kernel, 6, ties),
        grid=(rows // SEQUENCE_LENGTH, steps),
        in_specs=[four, two, two, four, table, table] + [ANY] * len(ties),
        out_specs=[out_four, out_two, out_two],
        out_shape=[jax.ShapeDtypeStruct((rows, steps * w), BF16) for w in (4 * HEAD_WIDTH, 2 * HEAD_WIDTH, 2 * HEAD_WIDTH)],
        scratch_shapes=[
            pltpu.VMEM((SEQUENCE_LENGTH, LANES), F32),
            pltpu.VMEM((SEQUENCE_LENGTH, LANES), F32),
            pltpu.VMEM((SEQUENCE_LENGTH, 2 * LANES), F32),
        ],
        compiler_params=params(),
        cost_estimate=cost(flops * 8, 12 * rows * 1024, QUERY_HEADS * rows * 640),
        name="attend_back",
    )(queries, keys, vals, grad, cos, sin, *ties)


def middle_kernel(lane_of, a_ref, w_ref, x_ref, gain_ref, router_ref, routes_ref, r_ref, m_ref, mt_ref, gates_ref):
    resid = x_ref[...].astype(F32) + dot(a_ref[...], w_ref[...])
    r_ref[...] = resid
    inverse = lax.rsqrt(jnp.mean(resid * resid, axis=-1, keepdims=True) + 1e-06)
    moe_in = (resid * inverse * gain_ref[lane_of : lane_of + 1].astype(F32)).astype(BF16)
    m_ref[...] = moe_in
    mt_ref[...] = moe_in.T
    logits = dot(moe_in, router_ref[...])
    lane = lax.broadcasted_iota(jnp.int32, logits.shape, 1)
    routes = routes_ref[...]
    picked = lane == routes[:, 0:1]
    for k in range(1, routes.shape[1]):
        picked = jnp.logical_or(picked, lane == routes[:, k : k + 1])
    logits = jnp.where(picked, logits, -1e30)
    weights = jnp.where(picked, jnp.exp(logits - jnp.max(logits, axis=-1, keepdims=True)), 0.0)
    gates_ref[...] = weights / jnp.sum(weights, axis=-1, keepdims=True)


def middle(attended, out_w, tokens, gain, lane, router_w, routes, ties=()):
    rows, width = tokens.shape
    return pl.pallas_call(
        tied(functools.partial(middle_kernel, lane), 6, ties),
        grid=(rows // TILE,),
        in_specs=[
            row_block(width),
            whole_block(out_w.shape),
            row_block(width),
            whole_block(gain.shape),
            whole_block(router_w.shape),
            row_block(routes.shape[1]),
        ]
        + [ANY] * len(ties),
        out_specs=[row_block(width), row_block(width), pl.BlockSpec((width, TILE), lambda i: (0, i)), row_block(LANES)],
        out_shape=[
            jax.ShapeDtypeStruct((rows, width), F32),
            jax.ShapeDtypeStruct((rows, width), BF16),
            jax.ShapeDtypeStruct((width, rows), BF16),
            jax.ShapeDtypeStruct((rows, LANES), F32),
        ],
        compiler_params=params(LESS_BYTES),
        cost_estimate=cost(2 * rows * width * (width + LANES), 14 * rows * width),
        name="middle",
    )(attended, out_w, tokens, gain, router_w, routes, *ties)


def moe_kernel(slots, chunks, first, ties, me_ref, *refs):
    refs = list(refs)
    take = lambda count: [refs.pop(0) for _ in range(count)]
    x, xt, dy, dyt, gates_ref = take(5)
    if not first:
        take(3)
    weights = [[take(count) for count in per_slot] for per_slot in chunks]
    take(ties)
    made, dmoe, gg_ref = take(3)
    grads = [take(2) for _ in slots]
    wg, wu, wd, hg, dg, du, stage, sem_w, sem_out = take(9)
    rows, width = x.shape
    step = 512

    def load(source, target, sem):
        copy = pltpu.make_async_copy(source, target, sem)
        copy.start()
        return copy

    def load_weights(index):
        buffer = index % 2
        out = []
        for which, target in enumerate((wg, wu, wd)):
            at, copies = 0, []
            for piece, ref in enumerate(weights[index][which]):
                count = ref.shape[0]
                copies.append(load(ref, target.at[buffer, at : at + count], sem_w.at[buffer, which, piece]))
                at += count
            out.append(copies)
        return out

    pending = {0: load_weights(0)}
    if first:
        gg_ref[...] = jnp.zeros_like(gg_ref)
    stores = []
    lane = lax.broadcasted_iota(jnp.int32, (step, LANES), 1)
    for index, slot in enumerate(slots):
        buffer = index % 2
        arriving = pending.pop(index)
        if index + 1 < len(slots):
            pending[index + 1] = load_weights(index + 1)
        me = me_ref[0] ^ slot
        g_w, u_w, d_w = wg.at[buffer], wu.at[buffer], wd.at[buffer]

        def arrived(which, lo):
            if lo == 0:
                for copy in arriving[which]:
                    copy.wait()

        for lo in range(0, rows, step):
            at = slice(lo, lo + step)
            arrived(0, lo)
            gate = dot(x[at], g_w[...])
            arrived(1, lo)
            upval = dot(x[at], u_w[...])
            arrived(2, lo)
            pre = dot_nt(dy[at], d_w[...])
            column = jnp.sum(jnp.where(lane == me, gates_ref[at], 0.0), axis=1, keepdims=True)
            sigma = 1.0 / (1.0 + jnp.exp(-gate))
            silu = gate * sigma
            hidden = silu * upval
            gained = jnp.sum(hidden * pre, axis=1, keepdims=True)
            gg_ref[at] = gg_ref[at] + jnp.where(lane == me, gained, 0.0)
            weighted = (hidden * column).astype(BF16)
            dhidden = pre * column
            dgate = (dhidden * upval * (sigma + silu * (1.0 - sigma))).astype(BF16)
            dup = (dhidden * silu).astype(BF16)
            hg[at], dg[at], du[at] = weighted, dgate, dup
            fresh = dot(weighted, d_w[...])
            back = dot_nt(dgate, g_w[...]) + dot_nt(dup, u_w[...])
            if first and index == 0:
                made[at], dmoe[at] = fresh, back
            else:
                made[at] += fresh
                dmoe[at] += back
        for copy in stores:
            copy.wait()
        stores = []
        half = width // 2
        for part in range(2):
            at = slice(part * half, (part + 1) * half)
            stage[0, at] = dot(xt[at], dg[...]).astype(BF16)
            stage[1, at] = dot(xt[at], du[...]).astype(BF16)
            stage[2, at] = dot(dyt[at], hg[...]).astype(BF16)
            stores.append(load(stage.at[:, at], grads[index][part], sem_out.at[part]))
    for copy in stores:
        copy.wait()


def moe(slots, me, moe_in, moe_in_t, dy, dy_t, gates, acc, weights, ties=()):
    rows, width = moe_in.shape
    hidden = weights[0][0][0].shape[1]
    first = acc is None
    flat = [piece for per_slot in weights for pieces in per_slot for piece in pieces]
    chunks = tuple(tuple(len(pieces) for pieces in per_slot) for per_slot in weights)
    held = [pltpu.with_memory_space_constraint(a, pltpu.VMEM) for a in (moe_in, moe_in_t, dy, dy_t, gates, *(acc or ()))]
    grad = jax.ShapeDtypeStruct((3, width // 2, hidden), BF16)
    outs = pl.pallas_call(
        functools.partial(moe_kernel, tuple(slots), chunks, first, len(ties)),
        in_specs=[pl.BlockSpec(memory_space=pltpu.SMEM)] + [VMEM] * len(held) + [ANY] * (len(flat) + len(ties)),
        out_specs=[VMEM, VMEM, VMEM] + [ANY] * (2 * len(slots)),
        out_shape=[pltpu.VMEM((rows, width), F32), pltpu.VMEM((rows, width), F32), pltpu.VMEM((rows, LANES), F32)]
        + [grad] * (2 * len(slots)),
        scratch_shapes=[
            pltpu.VMEM((2, width, hidden), BF16),
            pltpu.VMEM((2, width, hidden), BF16),
            pltpu.VMEM((2, hidden, width), BF16),
            pltpu.VMEM((rows, hidden), BF16),
            pltpu.VMEM((rows, hidden), BF16),
            pltpu.VMEM((rows, hidden), BF16),
            pltpu.VMEM((3, width, hidden), BF16),
            pltpu.SemaphoreType.DMA((2, 3, 2)),
            pltpu.SemaphoreType.DMA((2,)),
        ],
        input_output_aliases={} if first else {6: 0, 7: 1, 8: 2},
        compiler_params=pltpu.CompilerParams(vmem_limit_bytes=EXPERT_BYTES),
        cost_estimate=cost(18 * rows * width * hidden * len(slots), 20 * rows * width),
        name="experts",
    )(me, *held, *flat, *ties)
    return outs[:3], [tuple(outs[3 + 2 * i : 5 + 2 * i]) for i in range(len(slots))]


def turn_kernel(
    lane, resid_ref, made_ref, dmoe_ref, gates_ref, gg_ref, dy_ref, gain_ref, router_ref, mt_ref, w_ref,
    mixed_ref, dresid_ref, dz_ref, da_ref, gain_grad_ref, router_grad_ref,
):
    @pl.when(pl.program_id(0) == 0)
    def _():
        gain_grad_ref[...] = jnp.zeros_like(gain_grad_ref)
        router_grad_ref[...] = jnp.zeros_like(router_grad_ref)

    resid = resid_ref[...]
    mixed_ref[...] = (resid + made_ref[...]).astype(BF16)
    gates, gg = gates_ref[...], gg_ref[...]
    dlogits = (gates * (gg - jnp.sum(gates * gg, axis=1, keepdims=True))).astype(BF16)
    router_grad_ref[...] += dot(mt_ref[...], dlogits)
    dmoe = dmoe_ref[...] + dot_nt(dlogits, router_ref[...])
    inverse = lax.rsqrt(jnp.mean(resid * resid, axis=-1, keepdims=True) + 1e-06)
    gain_grad_ref[...] += jnp.sum(dmoe * resid * inverse, axis=0, keepdims=True)
    scaled = dmoe * gain_ref[lane : lane + 1].astype(F32)
    inner = jnp.mean(scaled * resid, axis=-1, keepdims=True)
    dresid = dy_ref[...].astype(F32) + inverse * scaled - resid * (inverse * inverse * inverse * inner)
    dresid_ref[...] = dresid
    dz = dresid.astype(BF16)
    dz_ref[...] = dz
    da_ref[...] = dot_nt(dz, w_ref[...]).astype(BF16)


def turn(resid, made, dmoe, gates, gg, dy, gain, lane, router_w, moe_in_t, out_w, ties=()):
    rows, width = resid.shape
    return pl.pallas_call(
        tied(functools.partial(turn_kernel, lane), 10, ties),
        grid=(rows // TILE,),
        in_specs=[
            row_block(width), row_block(width), row_block(width), row_block(LANES), row_block(LANES), row_block(width),
            whole_block(gain.shape), whole_block(router_w.shape), pl.BlockSpec((width, TILE), lambda i: (0, i)),
            whole_block(out_w.shape),
        ]
        + [ANY] * len(ties),
        out_specs=[row_block(width)] * 4 + [whole_block((1, width)), whole_block((width, LANES))],
        out_shape=[
            jax.ShapeDtypeStruct((rows, width), BF16),
            jax.ShapeDtypeStruct((rows, width), F32),
            jax.ShapeDtypeStruct((rows, width), BF16),
            jax.ShapeDtypeStruct((rows, width), BF16),
            jax.ShapeDtypeStruct((1, width), F32),
            jax.ShapeDtypeStruct((width, LANES), F32),
        ],
        compiler_params=params(LESS_BYTES),
        cost_estimate=cost(2 * rows * width * (width + 2 * LANES), 28 * rows * width),
        name="turn",
    )(resid, made, dmoe, gates, gg, dy, gain, router_w, moe_in_t, out_w, *ties)


def finish_kernel(lane, count, *refs):
    grads = refs[:count]
    w_ref, x_ref, dresid_ref, gain_ref, router_ref, second_ref, out_ref, small_ref, first = refs[count:]

    @pl.when(pl.program_id(0) == 0)
    def _():
        first[...] = jnp.zeros_like(first)

    at, dn = 0, 0.0
    for ref in grads:
        dn += dot_nt(ref[...], w_ref[:, at : at + ref.shape[1]])
        at += ref.shape[1]
    x = x_ref[...].astype(F32)
    inverse = lax.rsqrt(jnp.mean(x * x, axis=-1, keepdims=True) + 1e-06)
    first[...] += jnp.sum(dn * x * inverse, axis=0, keepdims=True)
    scaled = dn * gain_ref[lane : lane + 1].astype(F32)
    inner = jnp.mean(scaled * x, axis=-1, keepdims=True)
    out_ref[...] = dresid_ref[...] + inverse * scaled - x * (inverse * inverse * inverse * inner)

    @pl.when(pl.program_id(0) == pl.num_programs(0) - 1)
    def _():
        row = lax.broadcasted_iota(jnp.int32, (LANES, first.shape[1]), 0)
        gains = jnp.where(row == lane, first[...], 0.0) + jnp.where(row == lane + 1, second_ref[...], 0.0)
        small_ref[...] = (router_ref[...] + gains.T).astype(BF16)


def finish(grads, weights, tokens, dresid, gain, lane, router_grad, second, ties=()):
    rows, width = tokens.shape
    return pl.pallas_call(
        tied(functools.partial(finish_kernel, lane, len(grads)), len(grads) + 6, ties),
        grid=(rows // TILE,),
        in_specs=[row_block(g.shape[1]) for g in grads]
        + [whole_block(weights.shape), row_block(width), row_block(width), whole_block(gain.shape)]
        + [whole_block(router_grad.shape), whole_block(second.shape)]
        + [ANY] * len(ties),
        out_specs=[row_block(width), whole_block((width, LANES))],
        out_shape=[jax.ShapeDtypeStruct((rows, width), F32), jax.ShapeDtypeStruct((width, LANES), BF16)],
        scratch_shapes=[pltpu.VMEM((1, width), F32)],
        compiler_params=params(),
        cost_estimate=cost(1, 1),
        name="finish",
    )(*grads, weights, tokens, dresid, gain, router_grad, second, *ties)


def weights_back_kernel(count, *refs):
    for grad, out in zip(refs[1 : count + 1], refs[count + 1 :]):
        out[...] = dot(refs[0][...], grad[...]).astype(BF16)


def weights_back(turned, grads, ties=()):
    rows = turned.shape[0]
    return pl.pallas_call(
        tied(functools.partial(weights_back_kernel, len(grads)), len(grads) + 1, ties),
        grid=(rows // TILE,),
        in_specs=[row_block(turned.shape[1])] + [whole_block(g.shape) for g in grads] + [ANY] * len(ties),
        out_specs=[row_block(g.shape[1]) for g in grads],
        out_shape=[jax.ShapeDtypeStruct((rows, g.shape[1]), BF16) for g in grads],
        compiler_params=params(),
        cost_estimate=cost(1, 1),
        name="weights_back",
    )(turned, *grads, *ties)


def widen_kernel(top_ref, bottom_ref, gate_ref, up_ref, down_ref):
    step = pl.program_id(0)
    for half, ref in enumerate((top_ref, bottom_ref)):

        @pl.when(step // 2 == half)
        def _():
            gate_ref[...] = ref[0].astype(F32)
            up_ref[...] = ref[1].astype(F32)
            down_ref[...] = ref[2].astype(F32).T


def widen(top, bottom):
    _, rows, columns = top.shape
    step = rows // 2
    block = pl.BlockSpec((step, columns), lambda i: (i, 0))
    return pl.pallas_call(
        widen_kernel,
        grid=(4,),
        in_specs=[
            pl.BlockSpec((3, step, columns), lambda i: (0, jnp.minimum(i, 1), 0)),
            pl.BlockSpec((3, step, columns), lambda i: (0, jnp.maximum(i - 2, 0), 0)),
        ],
        out_specs=[block, block, pl.BlockSpec((columns, step), lambda i: (0, i))],
        out_shape=[
            jax.ShapeDtypeStruct((2 * rows, columns), F32),
            jax.ShapeDtypeStruct((2 * rows, columns), F32),
            jax.ShapeDtypeStruct((columns, 2 * rows), F32),
        ],
        compiler_params=params(),
        cost_estimate=cost(1, 1),
        name="widen",
    )(top, bottom)


def plus_kernel(counts, *refs):
    refs = list(refs)
    refs.pop()[...] = jnp.zeros((8, LANES), F32)
    ins = [[refs.pop(0) for _ in range(count)] for count in counts]
    for terms, out in zip(ins, refs):
        total = terms[0][...].astype(F32)
        for ref in terms[1:]:
            total += ref[...].astype(F32)
        out[...] = total.astype(BF16)


def plus(*groups, ties=()):
    shape = groups[0][0].shape
    block = pl.BlockSpec((1, shape[1] // 2, shape[2]), lambda i, j: (i, j, 0))
    counts = tuple(len(terms) for terms in groups)
    flat = [a for terms in groups for a in terms]
    return pl.pallas_call(
        tied(functools.partial(plus_kernel, counts), len(flat), ties),
        grid=(shape[0], 2),
        in_specs=[block] * len(flat) + [ANY] * len(ties),
        out_specs=[block] * len(groups) + [pl.BlockSpec((8, LANES), lambda i, j: (0, 0))],
        out_shape=[jax.ShapeDtypeStruct(shape, BF16)] * len(groups) + [jax.ShapeDtypeStruct((8, LANES), F32)],
        compiler_params=pltpu.CompilerParams(vmem_limit_bytes=16 * 1024 * 1024),
        cost_estimate=cost(len(flat) * flat[0].size, 2 * (len(flat) + len(groups)) * flat[0].size),
        name="plus",
    )(*flat, *ties)


def gather_kernel(size, count, *refs):
    q_ref, k_ref, v_ref, s_ref, o_ref, d_ref = refs[:6]
    owned, refs = refs[6 : 6 + count], refs[6 + count :]
    packed_ref, small_ref, out_ref, down_ref, turned_ref = refs[:5]
    beside, refs = refs[5 : 5 + 2 * count], refs[5 + 2 * count :]
    beyond, refs = refs[: 2 * count], refs[2 * count :]
    pair, refs = refs[: count + 1 if count else 0], refs[count + 1 if count else 0 :]
    send_sem, recv_sem, pass_sem, take_sem, away_sem, come_sem, over_sem, land_sem = refs
    me, z = lax.axis_index("expert"), lax.axis_index("wshard")
    core = lax.rem(me, 2)
    sibling = me + 1 - 2 * core
    rows = q_ref.shape[0]
    half = rows // 2
    there = lambda step: jnp.logical_and(z + step >= 0, z + step < size)

    barrier = pltpu.get_barrier_semaphore()
    pl.semaphore_signal(barrier, inc=1, device_id=(sibling, z), device_id_type=pl.DeviceIdType.MESH)
    for step in (1, -1):

        @pl.when(there(step))
        def _():
            pl.semaphore_signal(barrier, inc=1, device_id=(me, z + step), device_id_type=pl.DeviceIdType.MESH)

    neighbours = []
    if count:
        xb, yb = lax.rem(me // 2, 2), me // 4
        neighbours = [me + 2 - 4 * xb, me + 4 - 8 * yb]
    for peer in neighbours:
        pl.semaphore_signal(barrier, inc=1, device_id=(peer, z), device_id_type=pl.DeviceIdType.MESH)
    pl.semaphore_wait(barrier, 1 + len(neighbours) + jnp.where(z > 0, 1, 0) + jnp.where(z < size - 1, 1, 0))
    shipped = []
    for i, ref in enumerate(owned):
        for j, peer in enumerate(neighbours):
            shipped.append(
                pltpu.make_async_remote_copy(
                    src_ref=ref, dst_ref=beside[j * count + i], send_sem=away_sem.at[i, j], recv_sem=come_sem.at[i, j],
                    device_id=(peer, z), device_id_type=pl.DeviceIdType.MESH,
                )
            )
    for copy in shipped:
        copy.start()

    def passed(source, target, i, j):
        return pltpu.make_async_remote_copy(
            src_ref=source, dst_ref=target, send_sem=over_sem.at[i, j], recv_sem=land_sem.at[i, j],
            device_id=(sibling, z), device_id_type=pl.DeviceIdType.MESH,
        )

    swapped = [passed(ref, target, i, 2) for i, (ref, target) in enumerate(zip(owned, pair))]

    own = pl.ds(pl.multiple_of(z * rows, rows), rows)
    at = 0
    for ref in (q_ref, k_ref, v_ref):
        packed_ref[own, at : at + ref.shape[1]] = ref[...]
        at += ref.shape[1]
    small_ref[own] = s_ref[...]
    out_ref[...] = o_ref[...]
    down_ref[...] = d_ref[...]
    if count:
        swapped.append(passed(down_ref, pair[count], count, 2))
    for copy in swapped:
        copy.start()

    def moves(way, hop, origin, which, device, send, recv):
        at = pl.ds(pl.multiple_of(origin * rows + which * half, half), half)
        return [
            pltpu.make_async_remote_copy(
                src_ref=ref.at[at], dst_ref=ref.at[at], send_sem=send.at[way, hop, i], recv_sem=recv.at[way, hop, i],
                device_id=device, device_id_type=pl.DeviceIdType.MESH,
            )
            for i, ref in enumerate((packed_ref, small_ref))
        ]

    def onward(way, step, hop):
        return moves(way, hop, z - step * (hop - 1), core, (me, z + step), send_sem, recv_sem)

    def across(way, step, hop, which):
        return moves(way, hop, z - step * hop, which, (sibling, z), pass_sem, take_sem)

    ways = ((0, 1), (1, -1))
    for way, step in ways:

        @pl.when(there(step))
        def _():
            for move in onward(way, step, 1):
                move.start()

    for hop in range(1, size):
        for way, step in ways:

            @pl.when(there(-step * hop))
            def _():
                for move in moves(way, hop, z - step * hop, core, (me, z), send_sem, recv_sem):
                    move.wait_recv()

                @pl.when(there(step))
                def _():
                    for move in onward(way, step, hop + 1):
                        move.start()

                for move in across(way, step, hop, core):
                    move.start()

    for hop in range(1, size):
        for way, step in ways:

            @pl.when(there(-step * hop))
            def _():
                for move in across(way, step, hop, 1 - core):
                    move.wait_recv()
                for move in across(way, step, hop, core):
                    move.wait_send()

            @pl.when(jnp.logical_and(there(step), there(-step * (hop - 1))))
            def _():
                for move in onward(way, step, hop):
                    move.wait_send()

    turned_ref[...] = small_ref[...].T
    onto = []
    for n, copy in enumerate(shipped):
        i, j = n // 2, n % 2
        copy.wait_recv()
        onto.append(passed(beside[j * count + i], beyond[j * count + i], i, j))
        onto[-1].start()
    for copy in shipped:
        copy.wait_send()
    for copy in swapped + onto:
        copy.wait()


def gather_weights(query, key, value, small, out, down, owned=()):
    size = lax.axis_size("wshard")
    rows = query.shape[0]
    width = query.shape[1] + key.shape[1] + value.shape[1]
    sems = pltpu.SemaphoreType.DMA((2, size + 1, 2))
    last = [*owned, down] if len(owned) else []
    return pl.pallas_call(
        functools.partial(gather_kernel, size, len(owned)),
        in_specs=[VMEM] * 6 + [ANY] * len(owned),
        out_specs=[VMEM] * 5 + [ANY] * (4 * len(owned) + len(last)),
        out_shape=[
            jax.ShapeDtypeStruct((size * rows, width), BF16),
            jax.ShapeDtypeStruct((size * rows, small.shape[1]), BF16),
            jax.ShapeDtypeStruct(out.shape, BF16),
            jax.ShapeDtypeStruct(down.shape, BF16),
            jax.ShapeDtypeStruct((small.shape[1], size * rows), BF16),
        ]
        + [jax.ShapeDtypeStruct(a.shape, BF16) for a in owned] * 4
        + [jax.ShapeDtypeStruct(a.shape, BF16) for a in last],
        scratch_shapes=[sems, sems, sems, sems] + [pltpu.SemaphoreType.DMA((len(owned) + 1, 3))] * 4,
        compiler_params=pltpu.CompilerParams(collective_id=0, has_side_effects=True, vmem_limit_bytes=VMEM_BYTES),
        cost_estimate=cost(1e9, 12 * rows * size * width),
        name="gather_weights",
    )(query, key, value, small, out, down, *owned)


def reduce_kernel(size, columns, *refs):
    count = sum(len(widths) for widths in columns)
    ins, outs = list(refs[:count]), refs[count : count + len(columns)]
    acc, rc, r1, r2, zs, rz, res, send_sem, recv_sem = refs[count + len(columns) :]
    me, z = lax.axis_index("expert"), lax.axis_index("wshard")
    core, xb, yb = lax.rem(me, 2), lax.rem(me // 2, 2), me // 4
    sibling, xp, yp = me + 1 - 2 * core, me + 2 - 4 * xb, me + 4 - 8 * yb
    half = ins[0].shape[1] // 2
    n1, n2 = half // 4, half // 8

    barrier = pltpu.get_barrier_semaphore()
    for peer in (sibling, xp, yp):
        pl.semaphore_signal(barrier, inc=1, device_id=(peer, z), device_id_type=pl.DeviceIdType.MESH)
    for d in range(1, size):
        pl.semaphore_signal(barrier, inc=1, device_id=(me, lax.rem(z + d, size)), device_id_type=pl.DeviceIdType.MESH)
    pl.semaphore_wait(barrier, 2 + size)

    pieces, at = [], 0
    for out, widths in zip(outs, columns):
        start = 0
        for width in widths:
            ref, step = ins.pop(0), min(width, 512)
            for lo in range(0, width, step):
                pieces.append((ref, out, lo, step, at, start + lo))
                at += step
            start += width

    sent = []

    def move(source, target, piece, kind, device):
        copy = pltpu.make_async_remote_copy(
            src_ref=source, dst_ref=target, send_sem=send_sem.at[kind, piece], recv_sem=recv_sem.at[kind, piece],
            device_id=device, device_id_type=pl.DeviceIdType.MESH,
        )
        copy.start()
        sent.append(copy)
        return copy

    def rows(start, length):
        return pl.ds(pl.multiple_of(start, 16), length)

    def sum_of(*terms):
        total = terms[0].astype(F32)
        for term in terms[1:]:
            total += term.astype(F32)
        return total

    k0, k1 = xb * n1 + yb * n2, half // 2 + yb * n1 + xb * n2
    base = core * half
    first = []
    for p, (ref, _, lo, w, at, _) in enumerate(pieces):
        first.append(move(ref.at[:, rows((1 - core) * half, half), lo : lo + w], rc.at[:, :, at : at + w], p, 0, (sibling, z)))
    second = []
    for p, (ref, _, lo, w, at, _) in enumerate(pieces):
        c = slice(at, at + w)
        first[p].wait_recv()
        acc[:, :, c] = sum_of(ref[:, rows(base, half), lo : lo + w], rc[:, :, c]).astype(BF16)
        second.append((
            move(acc.at[:, rows((1 - xb) * n1, n1), c], r1.at[0, :, :, c], p, 1, (xp, z)),
            move(acc.at[:, rows(half // 2 + (1 - yb) * n1, n1), c], r1.at[1, :, :, c], p, 2, (yp, z)),
        ))
    third = []
    for p, (_, _, _, w, at, _) in enumerate(pieces):
        c = slice(at, at + w)
        keep = (rows(xb * n1, n1), rows(half // 2 + yb * n1, n1))
        for i in range(2):
            second[p][i].wait_recv()
            acc[:, keep[i], c] = sum_of(acc[:, keep[i], c], r1[i, :, :, c]).astype(BF16)
        third.append((
            move(acc.at[:, rows(xb * n1 + (1 - yb) * n2, n2), c], r2.at[0, :, :, c], p, 3, (yp, z)),
            move(acc.at[:, rows(half // 2 + yb * n1 + (1 - xb) * n2, n2), c], r2.at[1, :, :, c], p, 4, (xp, z)),
        ))
    fourth = []
    for p, (_, _, _, w, at, _) in enumerate(pieces):
        c = slice(at, at + w)
        for i, k in enumerate((k0, k1)):
            third[p][i].wait_recv()
            zs[:, i * n2 : (i + 1) * n2, c] = sum_of(acc[:, rows(k, n2), c], r2[i, :, :, c]).astype(BF16)
        fourth.append([
            move(zs.at[lax.rem(z + d, size), :, c], rz.at[d - 1, :, c], p, 8 + d, (me, lax.rem(z + d, size)))
            for d in range(1, size)
        ])
    fifth = []
    for p, (_, _, _, w, at, _) in enumerate(pieces):
        c = slice(at, at + w)
        for copy in fourth[p]:
            copy.wait_recv()
        total = sum_of(zs[z, :, c], *[rz[d, :, c] for d in range(size - 1)]).astype(BF16)
        for i, k in enumerate((k0, k1)):
            res[rows(base + k, n2), c] = total[i * n2 : (i + 1) * n2]
        fifth.append((
            move(res.at[rows(base + k0, n2), c], res.at[rows(base + k0, n2), c], p, 5, (yp, z)),
            move(res.at[rows(base + k1, n2), c], res.at[rows(base + k1, n2), c], p, 6, (xp, z)),
        ))
    sixth = []
    for p, (_, _, _, w, at, _) in enumerate(pieces):
        c = slice(at, at + w)
        for copy in fifth[p]:
            copy.wait_recv()
        mine = rows(base + xb * n1, n1), rows(base + half // 2 + yb * n1, n1)
        sixth.append((
            move(res.at[mine[0], c], res.at[mine[0], c], p, 7, (xp, z)),
            move(res.at[mine[1], c], res.at[mine[1], c], p, 8, (yp, z)),
        ))
    last = []
    for p, (_, _, _, w, at, _) in enumerate(pieces):
        c = slice(at, at + w)
        for copy in sixth[p]:
            copy.wait_recv()
        last.append(move(res.at[rows(base, half), c], res.at[rows(base, half), c], p, 8 + size, (sibling, z)))
    for p, (_, out, _, w, at, to) in enumerate(pieces):
        last[p].wait_recv()
        out[:, to : to + w] = res[:, at : at + w].astype(F32)
    for copy in sent:
        copy.wait_send()


def reduce_all(*groups):
    size = lax.axis_size("wshard")
    rows = groups[0][0].shape[0] // size
    grads = [g for group in groups for g in group]
    columns = tuple(tuple(g.shape[1] for g in group) for group in groups)
    count = sum(-(-g.shape[1] // 512) for g in grads)
    width, half = sum(g.shape[1] for g in grads), rows // 2
    return pl.pallas_call(
        functools.partial(reduce_kernel, size, columns),
        in_specs=[VMEM] * len(grads),
        out_specs=[VMEM] * len(groups),
        out_shape=[jax.ShapeDtypeStruct((rows, sum(widths)), F32) for widths in columns],
        scratch_shapes=[
            pltpu.VMEM((size, half, width), BF16),
            pltpu.VMEM((size, half, width), BF16),
            pltpu.VMEM((2, size, half // 4, width), BF16),
            pltpu.VMEM((2, size, half // 8, width), BF16),
            pltpu.VMEM((size, half // 4, width), BF16),
            pltpu.VMEM((size - 1, half // 4, width), BF16),
            pltpu.VMEM((rows, width), BF16),
            pltpu.SemaphoreType.DMA((9 + size, count)),
            pltpu.SemaphoreType.DMA((9 + size, count)),
        ],
        compiler_params=pltpu.CompilerParams(collective_id=1, has_side_effects=True, vmem_limit_bytes=VMEM_BYTES),
        cost_estimate=cost(1, 1),
        name="reduce_all",
    )(*[g.reshape(size, rows, g.shape[1]) for g in grads])


def flip(value, axis, bit):
    size = lax.axis_size(axis)
    return lax.ppermute(value, axis, [(i, i ^ bit) for i in range(size)])


def gather_experts(mats, owners):
    slots, bit = {0: tuple([m] for m in mats)}, 2
    while bit < owners:
        for j in sorted(slots):
            slots[j | bit] = tuple([flip(p, "expert", bit) for p in m] for m in slots[j])
        bit *= 2
    return slots


def third_slot(a, b):
    cut = a[2][0].shape[0] // 2
    return (
        [flip(a[0][0], "expert", 4)],
        [flip(b[1][0], "expert", 2)],
        [flip(a[2][0][:cut], "expert", 4), flip(b[2][0][cut:], "expert", 2)],
    )


def across_core(slot):
    return tuple([flip(p, "expert", 1) for p in m] for m in slot)


def add(a, b):
    return (a.astype(F32) + b.astype(F32)).astype(BF16)


def reduce_experts(parts, owners):
    bit = 1
    while bit < owners:
        for j in sorted(parts, reverse=True):
            if j & bit:
                gone = parts.pop(j)
                parts[j ^ bit] = tuple(add(m, flip(s, "expert", bit)) for m, s in zip(parts[j ^ bit], gone))
        bit *= 2
    return parts[0]


def on_device(
    tokens, gain_attn, w_query, key_weight, value_weight, w_out, gain_ffn, w_router, w_gate, w_up, w_down, routes, cotangent
):
    owners = lax.axis_size("expert")
    me = lax.axis_index("expert").astype(jnp.int32)[None]
    rows, width = tokens.shape
    experts = w_router.shape[1]
    mats = (w_gate[0], w_up[0], w_down[0])

    small = jnp.concatenate([w_router, gain_attn[:, None], gain_ffn[:, None]], axis=1)
    small = jnp.pad(small, ((0, 0), (0, LANES - small.shape[1])))
    packed, small, out_shard, down, gains, *beside = gather_weights(
        w_query, key_weight, value_weight, small, w_out, mats[2], mats[:2] if owners == 8 else ()
    )
    out_w = lax.all_gather(out_shard, "wshard", axis=0, tiled=True)
    cos, sin = (jnp.asarray(a) for a in rope_tables(rows))

    if owners == 8:
        slots = {0: tuple([m] for m in mats)}
        slots[2] = ([beside[0]], [beside[1]], [flip(down, "expert", 2)])
        slots[4] = ([beside[2]], [beside[3]], [flip(down, "expert", 4)])
        slots[6] = third_slot(slots[2], slots[4])
    else:
        slots = gather_experts(mats, owners)
    normed_t, queries, keys, vals = project(tokens, gains, experts, packed, cos, sin)
    def pieces_of(*which, first=0, last=3):
        return [p for j in which for m in slots[j][first:last] for p in m] if owners == 8 else []

    attended = attend(queries, keys, vals)
    if owners == 8:
        slots[1] = tuple([m] for m in beside[8:])
        downs = lax.optimization_barrier((slots[2][2][0], slots[4][2][0], attended))
        slots[3] = ([beside[4]], [beside[5]], [flip(downs[0], "expert", 1)])
        slots[5] = ([beside[6]], [beside[7]], [flip(downs[1], "expert", 1)])
        slots[7] = across_core(slots[6])
    else:
        for j in sorted(slots):
            slots[j | 1] = across_core(slots[j])
    resid, moe_in, moe_in_t, gates = middle(
        attended, out_w, tokens, gains, experts + 1, small, routes, pieces_of(2, 4)
    )
    dy_t = cotangent.T

    def one(j, acc, ties=()):
        acc, (halves,) = moe([j], me, moe_in, moe_in_t, cotangent, dy_t, gates, acc, [slots[j]], ties)
        return acc, halves

    def turned(acc, ties=()):
        made, dmoe, gate_grads = acc
        return turn(
            resid, made, dmoe, gates, gate_grads, cotangent, gains, experts + 1, small, moe_in_t, out_w, ties
        )

    if owners == 8:
        core = lambda halves: [flip(m, "expert", 1) for m in halves]
        over_x = lambda m: flip(m, "expert", 2)
        over_y = lambda m: flip(m, "expert", 4)
        acc, g3 = one(3, None, pieces_of(6))
        c3 = core(g3)
        acc, g2 = one(2, acc)
        *s2, t2 = plus((g2[0], c3[0]), (g2[1], c3[1]))
        x20 = over_x(s2[0])
        acc, g7 = one(7, acc, [t2])
        c7 = core(g7)
        acc, g6 = one(6, acc)
        *s6, t6 = plus((g6[0], c7[0]), (g6[1], c7[1]))
        x60, y61 = over_x(s6[0]), over_y(s6[1])
        acc, g5 = one(5, acc, [t6])
        c5 = core(g5)
        acc, g4 = one(4, acc, [x20])
        *s4, t4 = plus((g4[0], c5[0]), (g4[1], c5[1]))
        y41 = over_y(s4[1])
        acc, g1 = one(1, acc, [t4])
        c1 = core(g1)
        left, right, sides = plus((s4[0], x60), (s2[1], y61))
        x21, y40 = over_x(right), over_y(left)
        acc, g0 = one(0, acc, [sides])
        *s0, t0 = plus((g0[0], c1[0]), (g0[1], c1[1]))
        mixed, dresid, dz, dattended, gain_two_grad, router_grad = turned(acc, [t0])
        out_grad = dot_tn(attended, dz).astype(BF16)
        early = attend_back(queries, keys, vals, dattended, cos, sin, 0, 2, [out_grad])
        top, bottom, both = plus((s0[0], x20, y40), (s0[1], y41, x21), ties=early[2:])
        late = attend_back(queries, keys, vals, dattended, cos, sin, 2, 2, [both])
        top, bottom = lax.psum((top, bottom), "wshard")
        pieces = [early[0], late[0], early[1], late[1], early[2], late[2]]
        weight_grads = weights_back(normed_t, pieces)
        own, after = [top, bottom], []
    else:
        acc, parts = None, {}
        for j in range(owners):
            acc, parts[j] = one(j, acc)
        mixed, dresid, dz, dattended, gain_two_grad, router_grad = turned(acc)
        own, after = lax.psum(tuple(reduce_experts(parts, owners)), "wshard"), []
        out_grad = dot_tn(attended, dz).astype(BF16)
        pieces = attend_back(queries, keys, vals, dattended, cos, sin)
        weight_grads = weights_back(normed_t, pieces)
    d_tokens, small_grad = finish(pieces, packed, tokens, dresid, gains, experts, router_grad, gain_two_grad, after)
    third = len(weight_grads) // 3
    groups = [[out_grad]] + [weight_grads[i : i + third] for i in range(0, 3 * third, third)] + [[small_grad]]
    if owners == 8:
        sums = reduce_all(*groups)
    else:
        total = lambda g: lax.psum(lax.psum_scatter(g, "wshard", scatter_dimension=0, tiled=True), "expert")
        sums = [total(jnp.concatenate(group, axis=1)).astype(F32) for group in groups]
    out_grad, query_grad, key_grad, value_grad, small_grad = sums
    gate_grad, up_grad, down_grad = widen(*own)
    return (
        mixed,
        d_tokens,
        small_grad[:, experts],
        query_grad,
        key_grad,
        value_grad,
        out_grad,
        small_grad[:, experts + 1],
        small_grad[:, :experts],
        gate_grad[None],
        up_grad[None],
        down_grad[None],
    )


def solution(mesh):
    whole, shard, matrix, owned = P(("expert", "wshard"), None), P("wshard"), P("wshard", None), P("expert", None, None)
    return jax.shard_map(
        on_device,
        mesh=mesh,
        in_specs=(whole, shard, matrix, matrix, matrix, matrix, shard, matrix, owned, owned, owned, whole, whole),
        out_specs=(whole, whole, shard, matrix, matrix, matrix, matrix, shard, matrix, owned, owned, owned),
        check_vma=False,
    )
```

```python
import functools
import jax
import jax.numpy as jnp
import numpy as np
from jax import lax
from jax.experimental import pallas as pl
from jax.experimental.pallas import tpu as pltpu
from jax.sharding import PartitionSpec as P

QUERY_HEADS = 16
KEY_VALUE_HEADS = 8
HEAD_WIDTH = 64
SEQUENCE_LENGTH = 1024
BLOCK = 256
TILE = 256
LANES = 128
F32 = jnp.float32
BF16 = jnp.bfloat16
ANY = pl.BlockSpec(memory_space=pl.ANY)
VMEM = pl.BlockSpec(memory_space=pltpu.VMEM)
VMEM_BYTES = 60 * 1024 * 1024
LESS_BYTES = 30 * 1024 * 1024
EXPERT_BYTES = 22 * 1024 * 1024


def dot(a, b):
    return jnp.dot(a, b, preferred_element_type=F32)


def dot_nt(a, b):
    return lax.dot_general(a, b, (((1,), (1,)), ((), ())), preferred_element_type=F32)


def dot_tn(a, b):
    return lax.dot_general(a, b, (((0,), (0,)), ((), ())), preferred_element_type=F32)


def params(size=VMEM_BYTES):
    return pltpu.CompilerParams(vmem_limit_bytes=size)


def cost(flops, nbytes, transcendentals=0):
    return pl.CostEstimate(flops=int(flops), bytes_accessed=int(nbytes), transcendentals=int(transcendentals))


def rope_tables(rows):
    half = HEAD_WIDTH // 2
    freq = np.exp(-np.log(10000.0) * np.arange(half, dtype=np.float32) * 2.0 / HEAD_WIDTH).astype(np.float32)
    pos = (np.arange(rows) % SEQUENCE_LENGTH).astype(np.float32)
    angles = (pos[:, None] * freq[None, :]).astype(np.float32)
    cos, sin = np.cos(angles), np.sin(angles)
    return (
        np.concatenate([cos, cos, cos, cos], 1).astype(np.float32),
        np.concatenate([-sin, sin, -sin, sin], 1).astype(np.float32),
    )


def rope(u, cos, sin):
    half = HEAD_WIDTH // 2
    lane = lax.broadcasted_iota(jnp.int32, u.shape, 1)
    swapped = jnp.where(
        lane % HEAD_WIDTH < half, pltpu.roll(u, LANES - half, 1), pltpu.roll(u, half, 1)
    )
    return u * cos + swapped * sin


def row_block(width):
    return pl.BlockSpec((TILE, width), lambda i: (i, 0))


def whole_block(shape):
    return pl.BlockSpec(shape, lambda i: (0,) * len(shape))


def tied(kernel, inputs, ties):
    return lambda *refs: kernel(*refs[:inputs], *refs[inputs + len(ties) :])


def project_kernel(lane, x_ref, gain_ref, w_ref, cos_ref, sin_ref, n_ref, q_ref, k_ref, v_ref):
    x = x_ref[...].astype(F32)
    inverse = lax.rsqrt(jnp.mean(x * x, axis=-1, keepdims=True) + 1e-06)
    normed = (x * inverse * gain_ref[lane : lane + 1].astype(F32)).astype(BF16)
    n_ref[...] = normed.T
    cos, sin = cos_ref[...], sin_ref[...]
    step = 512
    for at in range(0, w_ref.shape[1], step):
        made = dot(normed, w_ref[:, at : at + step])
        for lo in range(0, step, LANES):
            u = made[:, lo : lo + LANES]
            c = at + lo
            if c < q_ref.shape[1]:
                q_ref[:, c : c + LANES] = (rope(u, cos, sin).astype(BF16) * jnp.asarray(HEAD_WIDTH**-0.5, BF16))
            elif c < q_ref.shape[1] + k_ref.shape[1]:
                c -= q_ref.shape[1]
                k_ref[:, c : c + LANES] = rope(u, cos, sin).astype(BF16)
            else:
                c -= q_ref.shape[1] + k_ref.shape[1]
                v_ref[:, c : c + LANES] = u.astype(BF16)


def project(tokens, gain, lane, weights, cos, sin):
    rows, width = tokens.shape
    qw, kw = QUERY_HEADS * HEAD_WIDTH, KEY_VALUE_HEADS * HEAD_WIDTH
    return pl.pallas_call(
        functools.partial(project_kernel, lane),
        grid=(rows // TILE,),
        in_specs=[row_block(width), whole_block(gain.shape), whole_block(weights.shape), row_block(LANES), row_block(LANES)],
        out_specs=[pl.BlockSpec((width, TILE), lambda i: (0, i)), row_block(qw), row_block(kw), row_block(kw)],
        out_shape=[jax.ShapeDtypeStruct(s, BF16) for s in ((width, rows), (rows, qw), (rows, kw), (rows, kw))],
        compiler_params=params(),
        cost_estimate=cost(2 * rows * width * (qw + 2 * kw), 12 * rows * width),
        name="project",
    )(tokens, gain, weights, cos, sin)


def attend_kernel(q_ref, k_ref, v_ref, o_ref):
    for c in range(2):
        k = k_ref[:, c * HEAD_WIDTH : (c + 1) * HEAD_WIDTH]
        v = v_ref[:, c * HEAD_WIDTH : (c + 1) * HEAD_WIDTH]
        for h in range(2):
            at = (2 * c + h) * HEAD_WIDTH
            for b in range(SEQUENCE_LENGTH // BLOCK):
                n = (b + 1) * BLOCK
                rows = slice(b * BLOCK, (b + 1) * BLOCK)
                s = dot_nt(q_ref[rows, at : at + HEAD_WIDTH], k[:n])
                p = jnp.exp(s - jnp.max(s, axis=-1, keepdims=True))
                total = jnp.sum(p, axis=-1, keepdims=True)
                o = dot((p * (1.0 / total)).astype(BF16), v[:n])
                o_ref[rows, at : at + HEAD_WIDTH] = o.astype(BF16)


def head_block(width, sequence=SEQUENCE_LENGTH):
    return pl.BlockSpec((sequence, width), lambda s, i: (s, i))


def attend(queries, keys, vals, ties=()):
    rows = queries.shape[0]
    steps = KEY_VALUE_HEADS // 2
    flops = 2 * QUERY_HEADS * rows * SEQUENCE_LENGTH * HEAD_WIDTH * 2
    return pl.pallas_call(
        tied(attend_kernel, 3, ties),
        grid=(rows // SEQUENCE_LENGTH, steps),
        in_specs=[head_block(4 * HEAD_WIDTH), head_block(2 * HEAD_WIDTH), head_block(2 * HEAD_WIDTH)] + [ANY] * len(ties),
        out_specs=head_block(4 * HEAD_WIDTH),
        out_shape=jax.ShapeDtypeStruct(queries.shape, BF16),
        compiler_params=params(),
        cost_estimate=cost(flops * 8, 6 * rows * 1024, QUERY_HEADS * rows * 640),
        name="attend",
    )(queries, keys, vals, *ties)


def attend_back_kernel(q_ref, k_ref, v_ref, g_ref, cos_ref, sin_ref, dq_ref, dk_ref, dv_ref, dk_acc, dv_acc, dq_acc):
    dk_acc[...] = jnp.zeros_like(dk_acc)
    dv_acc[...] = jnp.zeros_like(dv_acc)
    for c in range(2):
        lanes = slice(c * HEAD_WIDTH, (c + 1) * HEAD_WIDTH)
        k, v = k_ref[:, lanes], v_ref[:, lanes]
        for h in range(2):
            at = slice((2 * c + h) * HEAD_WIDTH, (2 * c + h + 1) * HEAD_WIDTH)
            for b in range(SEQUENCE_LENGTH // BLOCK):
                n = (b + 1) * BLOCK
                rows = slice(b * BLOCK, (b + 1) * BLOCK)
                q, g = q_ref[rows, at], g_ref[rows, at]
                s = dot_nt(k[:n], q)
                dp = dot_nt(v[:n], g)
                p = jnp.exp(s - jnp.max(s, axis=0, keepdims=True))
                p = p * (1.0 / jnp.sum(p, axis=0, keepdims=True))
                ds = (p * (dp - jnp.sum(p * dp, axis=0, keepdims=True))).astype(BF16)
                dv_acc[:n, lanes] += dot(p.astype(BF16), g)
                dk_acc[:n, lanes] += dot(ds, q)
                dq_acc[rows, at] = dot_tn(ds, k[:n])
    cos, sin = cos_ref[...], -sin_ref[...]
    scale = HEAD_WIDTH**-0.5
    dq_ref[:, :LANES] = rope(dq_acc[:, :LANES] * scale, cos, sin).astype(BF16)
    dq_ref[:, LANES:] = rope(dq_acc[:, LANES:] * scale, cos, sin).astype(BF16)
    dk_ref[...] = rope(dk_acc[...], cos, sin).astype(BF16)
    dv_ref[...] = dv_acc[...].astype(BF16)


def attend_back(queries, keys, vals, grad, cos, sin, first=0, steps=KEY_VALUE_HEADS // 2, ties=()):
    rows = queries.shape[0]
    flops = 5 * QUERY_HEADS * rows * SEQUENCE_LENGTH * HEAD_WIDTH * 2 * steps // (KEY_VALUE_HEADS // 2)
    table = pl.BlockSpec((SEQUENCE_LENGTH, LANES), lambda s, i: (s, 0))

    def block(width, start):
        return pl.BlockSpec((SEQUENCE_LENGTH, width), lambda s, i: (s, i + start))

    two, four = block(2 * HEAD_WIDTH, first), block(4 * HEAD_WIDTH, first)
    out_two, out_four = block(2 * HEAD_WIDTH, 0), block(4 * HEAD_WIDTH, 0)
    return pl.pallas_call(
        tied(attend_back_kernel, 6, ties),
        grid=(rows // SEQUENCE_LENGTH, steps),
        in_specs=[four, two, two, four, table, table] + [ANY] * len(ties),
        out_specs=[out_four, out_two, out_two],
        out_shape=[jax.ShapeDtypeStruct((rows, steps * w), BF16) for w in (4 * HEAD_WIDTH, 2 * HEAD_WIDTH, 2 * HEAD_WIDTH)],
        scratch_shapes=[
            pltpu.VMEM((SEQUENCE_LENGTH, LANES), F32),
            pltpu.VMEM((SEQUENCE_LENGTH, LANES), F32),
            pltpu.VMEM((SEQUENCE_LENGTH, 2 * LANES), F32),
        ],
        compiler_params=params(),
        cost_estimate=cost(flops * 8, 12 * rows * 1024, QUERY_HEADS * rows * 640),
        name="attend_back",
    )(queries, keys, vals, grad, cos, sin, *ties)


def middle_kernel(lane_of, a_ref, w_ref, x_ref, gain_ref, router_ref, routes_ref, r_ref, m_ref, mt_ref, gates_ref):
    resid = x_ref[...].astype(F32) + dot(a_ref[...], w_ref[...])
    r_ref[...] = resid
    inverse = lax.rsqrt(jnp.mean(resid * resid, axis=-1, keepdims=True) + 1e-06)
    moe_in = (resid * inverse * gain_ref[lane_of : lane_of + 1].astype(F32)).astype(BF16)
    m_ref[...] = moe_in
    mt_ref[...] = moe_in.T
    logits = dot(moe_in, router_ref[...])
    lane = lax.broadcasted_iota(jnp.int32, logits.shape, 1)
    routes = routes_ref[...]
    picked = lane == routes[:, 0:1]
    for k in range(1, routes.shape[1]):
        picked = jnp.logical_or(picked, lane == routes[:, k : k + 1])
    logits = jnp.where(picked, logits, -1e30)
    weights = jnp.where(picked, jnp.exp(logits - jnp.max(logits, axis=-1, keepdims=True)), 0.0)
    gates_ref[...] = weights / jnp.sum(weights, axis=-1, keepdims=True)


def middle(attended, out_w, tokens, gain, lane, router_w, routes, ties=()):
    rows, width = tokens.shape
    return pl.pallas_call(
        tied(functools.partial(middle_kernel, lane), 6, ties),
        grid=(rows // TILE,),
        in_specs=[
            row_block(width),
            whole_block(out_w.shape),
            row_block(width),
            whole_block(gain.shape),
            whole_block(router_w.shape),
            row_block(routes.shape[1]),
        ]
        + [ANY] * len(ties),
        out_specs=[row_block(width), row_block(width), pl.BlockSpec((width, TILE), lambda i: (0, i)), row_block(LANES)],
        out_shape=[
            jax.ShapeDtypeStruct((rows, width), F32),
            jax.ShapeDtypeStruct((rows, width), BF16),
            jax.ShapeDtypeStruct((width, rows), BF16),
            jax.ShapeDtypeStruct((rows, LANES), F32),
        ],
        compiler_params=params(LESS_BYTES),
        cost_estimate=cost(2 * rows * width * (width + LANES), 14 * rows * width),
        name="middle",
    )(attended, out_w, tokens, gain, router_w, routes, *ties)


def moe_kernel(slots, chunks, first, ties, me_ref, *refs):
    refs = list(refs)
    take = lambda count: [refs.pop(0) for _ in range(count)]
    x, xt, dy, dyt, gates_ref = take(5)
    if not first:
        take(3)
    weights = [[take(count) for count in per_slot] for per_slot in chunks]
    take(ties)
    made, dmoe, gg_ref = take(3)
    grads = [take(2) for _ in slots]
    wg, wu, wd, hg, dg, du, stage, sem_w, sem_out = take(9)
    rows, width = x.shape
    step = 512

    def load(source, target, sem):
        copy = pltpu.make_async_copy(source, target, sem)
        copy.start()
        return copy

    def load_weights(index):
        buffer = index % 2
        out = []
        for which, target in enumerate((wg, wu, wd)):
            at, copies = 0, []
            for piece, ref in enumerate(weights[index][which]):
                count = ref.shape[0]
                copies.append(load(ref, target.at[buffer, at : at + count], sem_w.at[buffer, which, piece]))
                at += count
            out.append(copies)
        return out

    pending = {0: load_weights(0)}
    if first:
        gg_ref[...] = jnp.zeros_like(gg_ref)
    stores = []
    lane = lax.broadcasted_iota(jnp.int32, (step, LANES), 1)
    for index, slot in enumerate(slots):
        buffer = index % 2
        arriving = pending.pop(index)
        if index + 1 < len(slots):
            pending[index + 1] = load_weights(index + 1)
        me = me_ref[0] ^ slot
        g_w, u_w, d_w = wg.at[buffer], wu.at[buffer], wd.at[buffer]

        def arrived(which, lo):
            if lo == 0:
                for copy in arriving[which]:
                    copy.wait()

        for lo in range(0, rows, step):
            at = slice(lo, lo + step)
            arrived(0, lo)
            gate = dot(x[at], g_w[...])
            arrived(1, lo)
            upval = dot(x[at], u_w[...])
            arrived(2, lo)
            pre = dot_nt(dy[at], d_w[...])
            column = jnp.sum(jnp.where(lane == me, gates_ref[at], 0.0), axis=1, keepdims=True)
            sigma = 1.0 / (1.0 + jnp.exp(-gate))
            silu = gate * sigma
            hidden = silu * upval
            gained = jnp.sum(hidden * pre, axis=1, keepdims=True)
            gg_ref[at] = gg_ref[at] + jnp.where(lane == me, gained, 0.0)
            weighted = (hidden * column).astype(BF16)
            dhidden = pre * column
            dgate = (dhidden * upval * (sigma + silu * (1.0 - sigma))).astype(BF16)
            dup = (dhidden * silu).astype(BF16)
            hg[at], dg[at], du[at] = weighted, dgate, dup
            fresh = dot(weighted, d_w[...])
            back = dot_nt(dgate, g_w[...]) + dot_nt(dup, u_w[...])
            if first and index == 0:
                made[at], dmoe[at] = fresh, back
            else:
                made[at] += fresh
                dmoe[at] += back
        for copy in stores:
            copy.wait()
        stores = []
        half = width // 2
        for part in range(2):
            at = slice(part * half, (part + 1) * half)
            stage[0, at] = dot(xt[at], dg[...]).astype(BF16)
            stage[1, at] = dot(xt[at], du[...]).astype(BF16)
            stage[2, at] = dot(dyt[at], hg[...]).astype(BF16)
            stores.append(load(stage.at[:, at], grads[index][part], sem_out.at[part]))
    for copy in stores:
        copy.wait()


def moe(slots, me, moe_in, moe_in_t, dy, dy_t, gates, acc, weights, ties=()):
    rows, width = moe_in.shape
    hidden = weights[0][0][0].shape[1]
    first = acc is None
    flat = [piece for per_slot in weights for pieces in per_slot for piece in pieces]
    chunks = tuple(tuple(len(pieces) for pieces in per_slot) for per_slot in weights)
    held = [pltpu.with_memory_space_constraint(a, pltpu.VMEM) for a in (moe_in, moe_in_t, dy, dy_t, gates, *(acc or ()))]
    grad = jax.ShapeDtypeStruct((3, width // 2, hidden), BF16)
    outs = pl.pallas_call(
        functools.partial(moe_kernel, tuple(slots), chunks, first, len(ties)),
        in_specs=[pl.BlockSpec(memory_space=pltpu.SMEM)] + [VMEM] * len(held) + [ANY] * (len(flat) + len(ties)),
        out_specs=[VMEM, VMEM, VMEM] + [ANY] * (2 * len(slots)),
        out_shape=[pltpu.VMEM((rows, width), F32), pltpu.VMEM((rows, width), F32), pltpu.VMEM((rows, LANES), F32)]
        + [grad] * (2 * len(slots)),
        scratch_shapes=[
            pltpu.VMEM((2, width, hidden), BF16),
            pltpu.VMEM((2, width, hidden), BF16),
            pltpu.VMEM((2, hidden, width), BF16),
            pltpu.VMEM((rows, hidden), BF16),
            pltpu.VMEM((rows, hidden), BF16),
            pltpu.VMEM((rows, hidden), BF16),
            pltpu.VMEM((3, width, hidden), BF16),
            pltpu.SemaphoreType.DMA((2, 3, 2)),
            pltpu.SemaphoreType.DMA((2,)),
        ],
        input_output_aliases={} if first else {6: 0, 7: 1, 8: 2},
        compiler_params=pltpu.CompilerParams(vmem_limit_bytes=EXPERT_BYTES),
        cost_estimate=cost(18 * rows * width * hidden * len(slots), 20 * rows * width),
        name="experts",
    )(me, *held, *flat, *ties)
    return outs[:3], [tuple(outs[3 + 2 * i : 5 + 2 * i]) for i in range(len(slots))]


def turn_kernel(
    lane, resid_ref, made_ref, dmoe_ref, gates_ref, gg_ref, dy_ref, gain_ref, router_ref, mt_ref, w_ref,
    mixed_ref, dresid_ref, dz_ref, da_ref, gain_grad_ref, router_grad_ref,
):
    @pl.when(pl.program_id(0) == 0)
    def _():
        gain_grad_ref[...] = jnp.zeros_like(gain_grad_ref)
        router_grad_ref[...] = jnp.zeros_like(router_grad_ref)

    resid = resid_ref[...]
    mixed_ref[...] = (resid + made_ref[...]).astype(BF16)
    gates, gg = gates_ref[...], gg_ref[...]
    dlogits = (gates * (gg - jnp.sum(gates * gg, axis=1, keepdims=True))).astype(BF16)
    router_grad_ref[...] += dot(mt_ref[...], dlogits)
    dmoe = dmoe_ref[...] + dot_nt(dlogits, router_ref[...])
    inverse = lax.rsqrt(jnp.mean(resid * resid, axis=-1, keepdims=True) + 1e-06)
    gain_grad_ref[...] += jnp.sum(dmoe * resid * inverse, axis=0, keepdims=True)
    scaled = dmoe * gain_ref[lane : lane + 1].astype(F32)
    inner = jnp.mean(scaled * resid, axis=-1, keepdims=True)
    dresid = dy_ref[...].astype(F32) + inverse * scaled - resid * (inverse * inverse * inverse * inner)
    dresid_ref[...] = dresid
    dz = dresid.astype(BF16)
    dz_ref[...] = dz
    da_ref[...] = dot_nt(dz, w_ref[...]).astype(BF16)


def turn(resid, made, dmoe, gates, gg, dy, gain, lane, router_w, moe_in_t, out_w, ties=()):
    rows, width = resid.shape
    return pl.pallas_call(
        tied(functools.partial(turn_kernel, lane), 10, ties),
        grid=(rows // TILE,),
        in_specs=[
            row_block(width), row_block(width), row_block(width), row_block(LANES), row_block(LANES), row_block(width),
            whole_block(gain.shape), whole_block(router_w.shape), pl.BlockSpec((width, TILE), lambda i: (0, i)),
            whole_block(out_w.shape),
        ]
        + [ANY] * len(ties),
        out_specs=[row_block(width)] * 4 + [whole_block((1, width)), whole_block((width, LANES))],
        out_shape=[
            jax.ShapeDtypeStruct((rows, width), BF16),
            jax.ShapeDtypeStruct((rows, width), F32),
            jax.ShapeDtypeStruct((rows, width), BF16),
            jax.ShapeDtypeStruct((rows, width), BF16),
            jax.ShapeDtypeStruct((1, width), F32),
            jax.ShapeDtypeStruct((width, LANES), F32),
        ],
        compiler_params=params(LESS_BYTES),
        cost_estimate=cost(2 * rows * width * (width + 2 * LANES), 28 * rows * width),
        name="turn",
    )(resid, made, dmoe, gates, gg, dy, gain, router_w, moe_in_t, out_w, *ties)


def finish_kernel(lane, count, *refs):
    grads = refs[:count]
    w_ref, x_ref, dresid_ref, gain_ref, router_ref, second_ref, out_ref, small_ref, first = refs[count:]

    @pl.when(pl.program_id(0) == 0)
    def _():
        first[...] = jnp.zeros_like(first)

    at, dn = 0, 0.0
    for ref in grads:
        dn += dot_nt(ref[...], w_ref[:, at : at + ref.shape[1]])
        at += ref.shape[1]
    x = x_ref[...].astype(F32)
    inverse = lax.rsqrt(jnp.mean(x * x, axis=-1, keepdims=True) + 1e-06)
    first[...] += jnp.sum(dn * x * inverse, axis=0, keepdims=True)
    scaled = dn * gain_ref[lane : lane + 1].astype(F32)
    inner = jnp.mean(scaled * x, axis=-1, keepdims=True)
    out_ref[...] = dresid_ref[...] + inverse * scaled - x * (inverse * inverse * inverse * inner)

    @pl.when(pl.program_id(0) == pl.num_programs(0) - 1)
    def _():
        row = lax.broadcasted_iota(jnp.int32, (LANES, first.shape[1]), 0)
        gains = jnp.where(row == lane, first[...], 0.0) + jnp.where(row == lane + 1, second_ref[...], 0.0)
        small_ref[...] = (router_ref[...] + gains.T).astype(BF16)


def finish(grads, weights, tokens, dresid, gain, lane, router_grad, second, ties=()):
    rows, width = tokens.shape
    return pl.pallas_call(
        tied(functools.partial(finish_kernel, lane, len(grads)), len(grads) + 6, ties),
        grid=(rows // TILE,),
        in_specs=[row_block(g.shape[1]) for g in grads]
        + [whole_block(weights.shape), row_block(width), row_block(width), whole_block(gain.shape)]
        + [whole_block(router_grad.shape), whole_block(second.shape)]
        + [ANY] * len(ties),
        out_specs=[row_block(width), whole_block((width, LANES))],
        out_shape=[jax.ShapeDtypeStruct((rows, width), F32), jax.ShapeDtypeStruct((width, LANES), BF16)],
        scratch_shapes=[pltpu.VMEM((1, width), F32)],
        compiler_params=params(),
        cost_estimate=cost(1, 1),
        name="finish",
    )(*grads, weights, tokens, dresid, gain, router_grad, second, *ties)


def weights_back_kernel(count, *refs):
    for grad, out in zip(refs[1 : count + 1], refs[count + 1 :]):
        out[...] = dot(refs[0][...], grad[...]).astype(BF16)


def weights_back(turned, grads, ties=()):
    rows = turned.shape[0]
    return pl.pallas_call(
        tied(functools.partial(weights_back_kernel, len(grads)), len(grads) + 1, ties),
        grid=(rows // TILE,),
        in_specs=[row_block(turned.shape[1])] + [whole_block(g.shape) for g in grads] + [ANY] * len(ties),
        out_specs=[row_block(g.shape[1]) for g in grads],
        out_shape=[jax.ShapeDtypeStruct((rows, g.shape[1]), BF16) for g in grads],
        compiler_params=params(),
        cost_estimate=cost(1, 1),
        name="weights_back",
    )(turned, *grads, *ties)


def widen_kernel(top_ref, bottom_ref, gate_ref, up_ref, down_ref):
    step = pl.program_id(0)
    for half, ref in enumerate((top_ref, bottom_ref)):

        @pl.when(step // 2 == half)
        def _():
            gate_ref[...] = ref[0].astype(F32)
            up_ref[...] = ref[1].astype(F32)
            down_ref[...] = ref[2].astype(F32).T


def widen(top, bottom):
    _, rows, columns = top.shape
    step = rows // 2
    block = pl.BlockSpec((step, columns), lambda i: (i, 0))
    return pl.pallas_call(
        widen_kernel,
        grid=(4,),
        in_specs=[
            pl.BlockSpec((3, step, columns), lambda i: (0, jnp.minimum(i, 1), 0)),
            pl.BlockSpec((3, step, columns), lambda i: (0, jnp.maximum(i - 2, 0), 0)),
        ],
        out_specs=[block, block, pl.BlockSpec((columns, step), lambda i: (0, i))],
        out_shape=[
            jax.ShapeDtypeStruct((2 * rows, columns), F32),
            jax.ShapeDtypeStruct((2 * rows, columns), F32),
            jax.ShapeDtypeStruct((columns, 2 * rows), F32),
        ],
        compiler_params=params(),
        cost_estimate=cost(1, 1),
        name="widen",
    )(top, bottom)


def plus_kernel(counts, *refs):
    refs = list(refs)
    refs.pop()[...] = jnp.zeros((8, LANES), F32)
    ins = [[refs.pop(0) for _ in range(count)] for count in counts]
    for terms, out in zip(ins, refs):
        total = terms[0][...].astype(F32)
        for ref in terms[1:]:
            total += ref[...].astype(F32)
        out[...] = total.astype(BF16)


def plus(*groups, ties=()):
    shape = groups[0][0].shape
    block = pl.BlockSpec((1, shape[1] // 2, shape[2]), lambda i, j: (i, j, 0))
    counts = tuple(len(terms) for terms in groups)
    flat = [a for terms in groups for a in terms]
    return pl.pallas_call(
        tied(functools.partial(plus_kernel, counts), len(flat), ties),
        grid=(shape[0], 2),
        in_specs=[block] * len(flat) + [ANY] * len(ties),
        out_specs=[block] * len(groups) + [pl.BlockSpec((8, LANES), lambda i, j: (0, 0))],
        out_shape=[jax.ShapeDtypeStruct(shape, BF16)] * len(groups) + [jax.ShapeDtypeStruct((8, LANES), F32)],
        compiler_params=pltpu.CompilerParams(vmem_limit_bytes=16 * 1024 * 1024),
        cost_estimate=cost(len(flat) * flat[0].size, 2 * (len(flat) + len(groups)) * flat[0].size),
        name="plus",
    )(*flat, *ties)


def gather_kernel(size, count, *refs):
    q_ref, k_ref, v_ref, s_ref, o_ref, d_ref = refs[:6]
    owned, refs = refs[6 : 6 + count], refs[6 + count :]
    packed_ref, small_ref, out_ref, down_ref, turned_ref = refs[:5]
    beside, refs = refs[5 : 5 + 2 * count], refs[5 + 2 * count :]
    beyond, refs = refs[: 2 * count], refs[2 * count :]
    pair, refs = refs[: count + 1 if count else 0], refs[count + 1 if count else 0 :]
    send_sem, recv_sem, pass_sem, take_sem, away_sem, come_sem, over_sem, land_sem = refs
    me, z = lax.axis_index("expert"), lax.axis_index("wshard")
    core = lax.rem(me, 2)
    sibling = me + 1 - 2 * core
    rows = q_ref.shape[0]
    half = rows // 2
    there = lambda step: jnp.logical_and(z + step >= 0, z + step < size)

    barrier = pltpu.get_barrier_semaphore()
    pl.semaphore_signal(barrier, inc=1, device_id=(sibling, z), device_id_type=pl.DeviceIdType.MESH)
    for step in (1, -1):

        @pl.when(there(step))
        def _():
            pl.semaphore_signal(barrier, inc=1, device_id=(me, z + step), device_id_type=pl.DeviceIdType.MESH)

    neighbours = []
    if count:
        xb, yb = lax.rem(me // 2, 2), me // 4
        neighbours = [me + 2 - 4 * xb, me + 4 - 8 * yb]
    for peer in neighbours:
        pl.semaphore_signal(barrier, inc=1, device_id=(peer, z), device_id_type=pl.DeviceIdType.MESH)
    pl.semaphore_wait(barrier, 1 + len(neighbours) + jnp.where(z > 0, 1, 0) + jnp.where(z < size - 1, 1, 0))
    shipped = []
    for i, ref in enumerate(owned):
        for j, peer in enumerate(neighbours):
            shipped.append(
                pltpu.make_async_remote_copy(
                    src_ref=ref, dst_ref=beside[j * count + i], send_sem=away_sem.at[i, j], recv_sem=come_sem.at[i, j],
                    device_id=(peer, z), device_id_type=pl.DeviceIdType.MESH,
                )
            )
    for copy in shipped:
        copy.start()

    def passed(source, target, i, j):
        return pltpu.make_async_remote_copy(
            src_ref=source, dst_ref=target, send_sem=over_sem.at[i, j], recv_sem=land_sem.at[i, j],
            device_id=(sibling, z), device_id_type=pl.DeviceIdType.MESH,
        )

    swapped = [passed(ref, target, i, 2) for i, (ref, target) in enumerate(zip(owned, pair))]

    own = pl.ds(pl.multiple_of(z * rows, rows), rows)
    at = 0
    for ref in (q_ref, k_ref, v_ref):
        packed_ref[own, at : at + ref.shape[1]] = ref[...]
        at += ref.shape[1]
    small_ref[own] = s_ref[...]
    out_ref[...] = o_ref[...]
    down_ref[...] = d_ref[...]
    if count:
        swapped.append(passed(down_ref, pair[count], count, 2))
    for copy in swapped:
        copy.start()

    def moves(way, hop, origin, which, device, send, recv):
        at = pl.ds(pl.multiple_of(origin * rows + which * half, half), half)
        return [
            pltpu.make_async_remote_copy(
                src_ref=ref.at[at], dst_ref=ref.at[at], send_sem=send.at[way, hop, i], recv_sem=recv.at[way, hop, i],
                device_id=device, device_id_type=pl.DeviceIdType.MESH,
            )
            for i, ref in enumerate((packed_ref, small_ref))
        ]

    def onward(way, step, hop):
        return moves(way, hop, z - step * (hop - 1), core, (me, z + step), send_sem, recv_sem)

    def across(way, step, hop, which):
        return moves(way, hop, z - step * hop, which, (sibling, z), pass_sem, take_sem)

    ways = ((0, 1), (1, -1))
    for way, step in ways:

        @pl.when(there(step))
        def _():
            for move in onward(way, step, 1):
                move.start()

    for hop in range(1, size):
        for way, step in ways:

            @pl.when(there(-step * hop))
            def _():
                for move in moves(way, hop, z - step * hop, core, (me, z), send_sem, recv_sem):
                    move.wait_recv()

                @pl.when(there(step))
                def _():
                    for move in onward(way, step, hop + 1):
                        move.start()

                for move in across(way, step, hop, core):
                    move.start()

    for hop in range(1, size):
        for way, step in ways:

            @pl.when(there(-step * hop))
            def _():
                for move in across(way, step, hop, 1 - core):
                    move.wait_recv()
                for move in across(way, step, hop, core):
                    move.wait_send()

            @pl.when(jnp.logical_and(there(step), there(-step * (hop - 1))))
            def _():
                for move in onward(way, step, hop):
                    move.wait_send()

    turned_ref[...] = small_ref[...].T
    onto = []
    for n, copy in enumerate(shipped):
        i, j = n // 2, n % 2
        copy.wait_recv()
        onto.append(passed(beside[j * count + i], beyond[j * count + i], i, j))
        onto[-1].start()
    for copy in shipped:
        copy.wait_send()
    for copy in swapped + onto:
        copy.wait()


def gather_weights(query, key, value, small, out, down, owned=()):
    size = lax.axis_size("wshard")
    rows = query.shape[0]
    width = query.shape[1] + key.shape[1] + value.shape[1]
    sems = pltpu.SemaphoreType.DMA((2, size + 1, 2))
    last = [*owned, down] if len(owned) else []
    return pl.pallas_call(
        functools.partial(gather_kernel, size, len(owned)),
        in_specs=[VMEM] * 6 + [ANY] * len(owned),
        out_specs=[VMEM] * 5 + [ANY] * (4 * len(owned) + len(last)),
        out_shape=[
            jax.ShapeDtypeStruct((size * rows, width), BF16),
            jax.ShapeDtypeStruct((size * rows, small.shape[1]), BF16),
            jax.ShapeDtypeStruct(out.shape, BF16),
            jax.ShapeDtypeStruct(down.shape, BF16),
            jax.ShapeDtypeStruct((small.shape[1], size * rows), BF16),
        ]
        + [jax.ShapeDtypeStruct(a.shape, BF16) for a in owned] * 4
        + [jax.ShapeDtypeStruct(a.shape, BF16) for a in last],
        scratch_shapes=[sems, sems, sems, sems] + [pltpu.SemaphoreType.DMA((len(owned) + 1, 3))] * 4,
        compiler_params=pltpu.CompilerParams(collective_id=0, has_side_effects=True, vmem_limit_bytes=VMEM_BYTES),
        cost_estimate=cost(1e9, 12 * rows * size * width),
        name="gather_weights",
    )(query, key, value, small, out, down, *owned)


def reduce_kernel(size, columns, *refs):
    count = sum(len(widths) for widths in columns)
    ins, outs = list(refs[:count]), refs[count : count + len(columns)]
    acc, rc, r1, r2, zs, rz, res, send_sem, recv_sem = refs[count + len(columns) :]
    me, z = lax.axis_index("expert"), lax.axis_index("wshard")
    core, xb, yb = lax.rem(me, 2), lax.rem(me // 2, 2), me // 4
    sibling, xp, yp = me + 1 - 2 * core, me + 2 - 4 * xb, me + 4 - 8 * yb
    half = ins[0].shape[1] // 2
    n1, n2 = half // 4, half // 8

    barrier = pltpu.get_barrier_semaphore()
    for peer in (sibling, xp, yp):
        pl.semaphore_signal(barrier, inc=1, device_id=(peer, z), device_id_type=pl.DeviceIdType.MESH)
    for d in range(1, size):
        pl.semaphore_signal(barrier, inc=1, device_id=(me, lax.rem(z + d, size)), device_id_type=pl.DeviceIdType.MESH)
    pl.semaphore_wait(barrier, 2 + size)

    pieces, at = [], 0
    for out, widths in zip(outs, columns):
        start = 0
        for width in widths:
            ref, step = ins.pop(0), min(width, 512)
            for lo in range(0, width, step):
                pieces.append((ref, out, lo, step, at, start + lo))
                at += step
            start += width

    sent = []

    def move(source, target, piece, kind, device):
        copy = pltpu.make_async_remote_copy(
            src_ref=source, dst_ref=target, send_sem=send_sem.at[kind, piece], recv_sem=recv_sem.at[kind, piece],
            device_id=device, device_id_type=pl.DeviceIdType.MESH,
        )
        copy.start()
        sent.append(copy)
        return copy

    def rows(start, length):
        return pl.ds(pl.multiple_of(start, 16), length)

    def sum_of(*terms):
        total = terms[0].astype(F32)
        for term in terms[1:]:
            total += term.astype(F32)
        return total

    k0, k1 = xb * n1 + yb * n2, half // 2 + yb * n1 + xb * n2
    base = core * half
    first = []
    for p, (ref, _, lo, w, at, _) in enumerate(pieces):
        first.append(move(ref.at[:, rows((1 - core) * half, half), lo : lo + w], rc.at[:, :, at : at + w], p, 0, (sibling, z)))
    second = []
    for p, (ref, _, lo, w, at, _) in enumerate(pieces):
        c = slice(at, at + w)
        first[p].wait_recv()
        acc[:, :, c] = sum_of(ref[:, rows(base, half), lo : lo + w], rc[:, :, c]).astype(BF16)
        second.append((
            move(acc.at[:, rows((1 - xb) * n1, n1), c], r1.at[0, :, :, c], p, 1, (xp, z)),
            move(acc.at[:, rows(half // 2 + (1 - yb) * n1, n1), c], r1.at[1, :, :, c], p, 2, (yp, z)),
        ))
    third = []
    for p, (_, _, _, w, at, _) in enumerate(pieces):
        c = slice(at, at + w)
        keep = (rows(xb * n1, n1), rows(half // 2 + yb * n1, n1))
        for i in range(2):
            second[p][i].wait_recv()
            acc[:, keep[i], c] = sum_of(acc[:, keep[i], c], r1[i, :, :, c]).astype(BF16)
        third.append((
            move(acc.at[:, rows(xb * n1 + (1 - yb) * n2, n2), c], r2.at[0, :, :, c], p, 3, (yp, z)),
            move(acc.at[:, rows(half // 2 + yb * n1 + (1 - xb) * n2, n2), c], r2.at[1, :, :, c], p, 4, (xp, z)),
        ))
    fourth = []
    for p, (_, _, _, w, at, _) in enumerate(pieces):
        c = slice(at, at + w)
        for i, k in enumerate((k0, k1)):
            third[p][i].wait_recv()
            zs[:, i * n2 : (i + 1) * n2, c] = sum_of(acc[:, rows(k, n2), c], r2[i, :, :, c]).astype(BF16)
        fourth.append([
            move(zs.at[lax.rem(z + d, size), :, c], rz.at[d - 1, :, c], p, 8 + d, (me, lax.rem(z + d, size)))
            for d in range(1, size)
        ])
    fifth = []
    for p, (_, _, _, w, at, _) in enumerate(pieces):
        c = slice(at, at + w)
        for copy in fourth[p]:
            copy.wait_recv()
        total = sum_of(zs[z, :, c], *[rz[d, :, c] for d in range(size - 1)]).astype(BF16)
        for i, k in enumerate((k0, k1)):
            res[rows(base + k, n2), c] = total[i * n2 : (i + 1) * n2]
        fifth.append((
            move(res.at[rows(base + k0, n2), c], res.at[rows(base + k0, n2), c], p, 5, (yp, z)),
            move(res.at[rows(base + k1, n2), c], res.at[rows(base + k1, n2), c], p, 6, (xp, z)),
        ))
    sixth = []
    for p, (_, _, _, w, at, _) in enumerate(pieces):
        c = slice(at, at + w)
        for copy in fifth[p]:
            copy.wait_recv()
        mine = rows(base + xb * n1, n1), rows(base + half // 2 + yb * n1, n1)
        sixth.append((
            move(res.at[mine[0], c], res.at[mine[0], c], p, 7, (xp, z)),
            move(res.at[mine[1], c], res.at[mine[1], c], p, 8, (yp, z)),
        ))
    last = []
    for p, (_, _, _, w, at, _) in enumerate(pieces):
        c = slice(at, at + w)
        for copy in sixth[p]:
            copy.wait_recv()
        last.append(move(res.at[rows(base, half), c], res.at[rows(base, half), c], p, 8 + size, (sibling, z)))
    for p, (_, out, _, w, at, to) in enumerate(pieces):
        last[p].wait_recv()
        out[:, to : to + w] = res[:, at : at + w].astype(F32)
    for copy in sent:
        copy.wait_send()


def reduce_all(*groups):
    size = lax.axis_size("wshard")
    rows = groups[0][0].shape[0] // size
    grads = [g for group in groups for g in group]
    columns = tuple(tuple(g.shape[1] for g in group) for group in groups)
    count = sum(-(-g.shape[1] // 512) for g in grads)
    width, half = sum(g.shape[1] for g in grads), rows // 2
    return pl.pallas_call(
        functools.partial(reduce_kernel, size, columns),
        in_specs=[VMEM] * len(grads),
        out_specs=[VMEM] * len(groups),
        out_shape=[jax.ShapeDtypeStruct((rows, sum(widths)), F32) for widths in columns],
        scratch_shapes=[
            pltpu.VMEM((size, half, width), BF16),
            pltpu.VMEM((size, half, width), BF16),
            pltpu.VMEM((2, size, half // 4, width), BF16),
            pltpu.VMEM((2, size, half // 8, width), BF16),
            pltpu.VMEM((size, half // 4, width), BF16),
            pltpu.VMEM((size - 1, half // 4, width), BF16),
            pltpu.VMEM((rows, width), BF16),
            pltpu.SemaphoreType.DMA((9 + size, count)),
            pltpu.SemaphoreType.DMA((9 + size, count)),
        ],
        compiler_params=pltpu.CompilerParams(collective_id=1, has_side_effects=True, vmem_limit_bytes=VMEM_BYTES),
        cost_estimate=cost(1, 1),
        name="reduce_all",
    )(*[g.reshape(size, rows, g.shape[1]) for g in grads])


def flip(value, axis, bit):
    size = lax.axis_size(axis)
    return lax.ppermute(value, axis, [(i, i ^ bit) for i in range(size)])


def gather_experts(mats, owners):
    slots, bit = {0: tuple([m] for m in mats)}, 2
    while bit < owners:
        for j in sorted(slots):
            slots[j | bit] = tuple([flip(p, "expert", bit) for p in m] for m in slots[j])
        bit *= 2
    return slots


def third_slot(a, b):
    cut = a[2][0].shape[0] // 2
    return (
        [flip(a[0][0], "expert", 4)],
        [flip(b[1][0], "expert", 2)],
        [flip(a[2][0][:cut], "expert", 4), flip(b[2][0][cut:], "expert", 2)],
    )


def across_core(slot):
    return tuple([flip(p, "expert", 1) for p in m] for m in slot)


def add(a, b):
    return (a.astype(F32) + b.astype(F32)).astype(BF16)


def reduce_experts(parts, owners):
    bit = 1
    while bit < owners:
        for j in sorted(parts, reverse=True):
            if j & bit:
                gone = parts.pop(j)
                parts[j ^ bit] = tuple(add(m, flip(s, "expert", bit)) for m, s in zip(parts[j ^ bit], gone))
        bit *= 2
    return parts[0]


def on_device(
    tokens, gain_attn, w_query, key_weight, value_weight, w_out, gain_ffn, w_router, w_gate, w_up, w_down, routes, cotangent
):
    owners = lax.axis_size("expert")
    me = lax.axis_index("expert").astype(jnp.int32)[None]
    rows, width = tokens.shape
    experts = w_router.shape[1]
    mats = (w_gate[0], w_up[0], w_down[0])

    small = jnp.concatenate([w_router, gain_attn[:, None], gain_ffn[:, None]], axis=1)
    small = jnp.pad(small, ((0, 0), (0, LANES - small.shape[1])))
    packed, small, out_shard, down, gains, *beside = gather_weights(
        w_query, key_weight, value_weight, small, w_out, mats[2], mats[:2] if owners == 8 else ()
    )
    out_w = lax.all_gather(out_shard, "wshard", axis=0, tiled=True)
    cos, sin = (jnp.asarray(a) for a in rope_tables(rows))

    if owners == 8:
        slots = {0: tuple([m] for m in mats)}
        slots[2] = ([beside[0]], [beside[1]], [flip(down, "expert", 2)])
        slots[4] = ([beside[2]], [beside[3]], [flip(down, "expert", 4)])
        slots[6] = third_slot(slots[2], slots[4])
    else:
        slots = gather_experts(mats, owners)
    normed_t, queries, keys, vals = project(tokens, gains, experts, packed, cos, sin)
    def pieces_of(*which, first=0, last=3):
        return [p for j in which for m in slots[j][first:last] for p in m] if owners == 8 else []

    attended = attend(queries, keys, vals)
    if owners == 8:
        slots[1] = tuple([m] for m in beside[8:])
        downs = lax.optimization_barrier((slots[2][2][0], slots[4][2][0], attended))
        slots[3] = ([beside[4]], [beside[5]], [flip(downs[0], "expert", 1)])
        slots[5] = ([beside[6]], [beside[7]], [flip(downs[1], "expert", 1)])
        slots[7] = across_core(slots[6])
    else:
        for j in sorted(slots):
            slots[j | 1] = across_core(slots[j])
    resid, moe_in, moe_in_t, gates = middle(
        attended, out_w, tokens, gains, experts + 1, small, routes, pieces_of(2, 4)
    )
    dy_t = cotangent.T

    def one(j, acc, ties=()):
        acc, (halves,) = moe([j], me, moe_in, moe_in_t, cotangent, dy_t, gates, acc, [slots[j]], ties)
        return acc, halves

    def turned(acc, ties=()):
        made, dmoe, gate_grads = acc
        return turn(
            resid, made, dmoe, gates, gate_grads, cotangent, gains, experts + 1, small, moe_in_t, out_w, ties
        )

    if owners == 8:
        core = lambda halves: [flip(m, "expert", 1) for m in halves]
        over_x = lambda m: flip(m, "expert", 2)
        over_y = lambda m: flip(m, "expert", 4)
        acc, g3 = one(3, None, pieces_of(6))
        c3 = core(g3)
        acc, g2 = one(2, acc)
        *s2, t2 = plus((g2[0], c3[0]), (g2[1], c3[1]))
        x20 = over_x(s2[0])
        acc, g7 = one(7, acc, [t2])
        c7 = core(g7)
        acc, g6 = one(6, acc)
        *s6, t6 = plus((g6[0], c7[0]), (g6[1], c7[1]))
        x60, y61 = over_x(s6[0]), over_y(s6[1])
        acc, g5 = one(5, acc, [t6])
        c5 = core(g5)
        acc, g4 = one(4, acc, [x20])
        *s4, t4 = plus((g4[0], c5[0]), (g4[1], c5[1]))
        y41 = over_y(s4[1])
        acc, g1 = one(1, acc, [t4])
        c1 = core(g1)
        left, right, sides = plus((s4[0], x60), (s2[1], y61))
        x21, y40 = over_x(right), over_y(left)
        acc, g0 = one(0, acc, [sides])
        *s0, t0 = plus((g0[0], c1[0]), (g0[1], c1[1]))
        mixed, dresid, dz, dattended, gain_two_grad, router_grad = turned(acc, [t0])
        out_grad = dot_tn(attended, dz).astype(BF16)
        early = attend_back(queries, keys, vals, dattended, cos, sin, 0, 2, [out_grad])
        top, bottom, both = plus((s0[0], x20, y40), (s0[1], y41, x21), ties=early[2:])
        late = attend_back(queries, keys, vals, dattended, cos, sin, 2, 2, [both])
        top, bottom = lax.psum((top, bottom), "wshard")
        pieces = [early[0], late[0], early[1], late[1], early[2], late[2]]
        weight_grads = weights_back(normed_t, pieces)
        own, after = [top, bottom], []
    else:
        acc, parts = None, {}
        for j in range(owners):
            acc, parts[j] = one(j, acc)
        mixed, dresid, dz, dattended, gain_two_grad, router_grad = turned(acc)
        own, after = lax.psum(tuple(reduce_experts(parts, owners)), "wshard"), []
        out_grad = dot_tn(attended, dz).astype(BF16)
        pieces = attend_back(queries, keys, vals, dattended, cos, sin)
        weight_grads = weights_back(normed_t, pieces)
    d_tokens, small_grad = finish(pieces, packed, tokens, dresid, gains, experts, router_grad, gain_two_grad, after)
    third = len(weight_grads) // 3
    groups = [[out_grad]] + [weight_grads[i : i + third] for i in range(0, 3 * third, third)] + [[small_grad]]
    if owners == 8:
        sums = reduce_all(*groups)
    else:
        total = lambda g: lax.psum(lax.psum_scatter(g, "wshard", scatter_dimension=0, tiled=True), "expert")
        sums = [total(jnp.concatenate(group, axis=1)).astype(F32) for group in groups]
    out_grad, query_grad, key_grad, value_grad, small_grad = sums
    gate_grad, up_grad, down_grad = widen(*own)
    return (
        mixed,
        d_tokens,
        small_grad[:, experts],
        query_grad,
        key_grad,
        value_grad,
        out_grad,
        small_grad[:, experts + 1],
        small_grad[:, :experts],
        gate_grad[None],
        up_grad[None],
        down_grad[None],
    )


def solution(mesh):
    whole, shard, matrix, owned = P(("expert", "wshard"), None), P("wshard"), P("wshard", None), P("expert", None, None)
    return jax.shard_map(
        on_device,
        mesh=mesh,
        in_specs=(whole, shard, matrix, matrix, matrix, matrix, shard, matrix, owned, owned, owned, whole, whole),
        out_specs=(whole, whole, shard, matrix, matrix, matrix, matrix, shard, matrix, owned, owned, owned),
        check_vma=False,
    )
```
